256 devices in a mesh: row: 8 (over z_lo, core), col: 16 (over x, y), wf: 2 (over z_hi).
Axes of the slice: x: 4, y: 4, z: 8 (z_hi: 2, z_lo: 4; z = z_hi * 4 + z_lo), core: 2. Of those that a mesh axis runs over, the one named last changes fastest.
Arguments:
- wave_blocks: bfloat16 [2, 32, 128, 128], P(None, None, 'wf'), may hold values from -0.5 to 0.5
- left_operators: bfloat16 [96, 32, 2, 128, 128], P('row', 'col'), may hold values from -0.375 to 0.375
- right_operators: bfloat16 [32, 128, 2, 128, 128], P(None, 'col', None, 'wf'), may hold values from -0.01171875 to 0.01171875
- left_table: int32 [96, 32], P('row'), may hold values from 0 to 31, as said below
- right_table: int32 [128, 32], replicated, may hold values from 0 to 31, as said below
- assignment: int32 [96], replicated, may hold values from 0 to 95, each once
- kramers_map: int32 [96], replicated, may hold values from 0 to 95, each once
Outputs:
- rdm: float32 [2, 2, 96, 128], P(None, None, 'row', ('col', 'wf'))
The draws below stay inside these ranges and needn't reach their ends.
Inputs may be any that keep to these rules, and one draw needn't show every extreme that they name: left_table[s, q] is q, q + 1 or q + 2 modulo 32. right_table[j, q] is q, q + 1 or q + 2 modulo 32. `assignment`: a permutation. `kramers_map`: a permutation.
All inputs are finite; a program needn't handle non-finite values.
Results may differ from the reference program's by a relative error of at most 0.0041.
Values may be sent and summed in bfloat16 or wider, within the bound.
No kernel may reach another device: no remote copies, remote signals or barrier semaphores. Data moves between devices by JAX's collectives and lax.ppermute only.
A program may use at most 128 MiB of HBM per device.

```python
import jax
import jax.numpy as jnp
from jax import lax

BLOCK = 128
BLOCKS = 32
LEFT_OPS = 96
RIGHT_OPS = 128


def draw_left_table(key, part):
    key = jax.random.fold_in(key, 11)
    offsets = jax.random.randint(key, (LEFT_OPS, BLOCKS), 0, 3)
    return ((jnp.arange(BLOCKS, dtype=jnp.int32)[None, :] + offsets) % BLOCKS).astype(jnp.int32)


def draw_right_table(key, part):
    key = jax.random.fold_in(key, 23)
    offsets = jax.random.randint(key, (RIGHT_OPS, BLOCKS), 0, 3)
    return ((jnp.arange(BLOCKS, dtype=jnp.int32)[None, :] + offsets) % BLOCKS).astype(jnp.int32)


def level_of(key, extent, shards, low, high):
    factor_of, own = 1.0, jax.random.fold_in(key, 6)
    for dim, shards_of in shards:
        steps = jnp.exp(jax.random.uniform(jax.random.fold_in(own, dim), (shards_of,), jnp.float32, low / len(shards), high / len(shards)))
        factor_of = factor_of * jnp.repeat(steps, extent[dim] // shards_of).reshape([-1 if axis == dim else 1 for axis in range(len(extent))])
    return factor_of


def normal_values(stream_key, extent, scale, reach, shards=(), kind=jnp.bfloat16):
    array = jax.random.normal(stream_key, extent, jnp.float32) * scale
    if len(shards) > 0:
        array = level_of(stream_key, extent, shards, -0.22, 0.18) * array
    return jnp.clip(array, min=-reach, max=reach).astype(kind)


def setup_inputs(seed: int = 0) -> dict:
    keys = jax.random.split(jax.random.key(seed), 8)
    wave_blocks = normal_values(keys[0], (2, BLOCKS, BLOCK, BLOCK), 0.088, 0.5, ((2, 2),))
    left_operators = normal_values(keys[1], (LEFT_OPS, BLOCKS, 2, BLOCK, BLOCK), (2 * BLOCK) ** -0.5, 0.375, ((0, 8), (1, 16)))
    right_operators = normal_values(keys[2], (BLOCKS, RIGHT_OPS, 2, BLOCK, BLOCK), (BLOCKS * BLOCK * BLOCK // 2) ** -0.5, 0.01171875, ((1, 16), (3, 2)))
    left_table = draw_left_table(jax.random.fold_in(keys[7], 71), 0)
    right_table = draw_right_table(jax.random.fold_in(keys[7], 71), 0)
    assignment = jax.random.permutation(keys[5], LEFT_OPS).astype(jnp.int32)
    kramers_map = jax.random.permutation(keys[6], LEFT_OPS).astype(jnp.int32)
    return {"wave_blocks": wave_blocks, "left_operators": left_operators, "right_operators": right_operators, "left_table": left_table, "right_table": right_table, "assignment": assignment, "kramers_map": kramers_map}


def finish_slot(totals):
    real_part = jnp.stack([totals[0, ..., 0] - totals[1, ..., 1], totals[2, ..., 0] - totals[3, ..., 1]])
    imag_part = jnp.stack([totals[0, ..., 1] + totals[1, ..., 0], totals[2, ..., 1] + totals[3, ..., 0]])
    return jnp.stack([real_part, imag_part])


def reference(wave_blocks, left_operators, right_operators, left_table, right_table, assignment, kramers_map):
    wave_wide = wave_blocks.astype(jnp.float32)
    right_wide = right_operators.astype(jnp.float32)

    def one_slot(inputs):
        operator, table_row = inputs
        sources = wave_wide[:, table_row]
        product = jnp.einsum('qcab,dqbe->qcdae', operator.astype(jnp.float32), sources)
        real_real = product[:, 0, 0]
        real_imag = product[:, 0, 1]
        imag_real = product[:, 1, 0]
        imag_imag = product[:, 1, 1]
        turned = jnp.stack([real_real - imag_imag, real_imag + imag_real, real_real + imag_imag, real_imag - imag_real], axis=1).astype(jnp.bfloat16)
        turned = lax.optimization_barrier(turned).astype(jnp.float32)
        bracket = jnp.einsum('dqar,qkae->qdkre', wave_wide, turned)
        tiles = jnp.stack([bracket[:, 0, 0] + bracket[:, 1, 1], bracket[:, 0, 1] - bracket[:, 1, 0], bracket[:, 0, 2] + bracket[:, 1, 3], bracket[:, 0, 3] - bracket[:, 1, 2]], axis=1).astype(jnp.bfloat16)
        tiles = lax.optimization_barrier(tiles).astype(jnp.float32)
        paired = jnp.einsum('qkab,qjcab->qkjc', tiles, right_wide)
        matching = (table_row[:, None] == right_table.T).astype(jnp.float32)
        totals = jnp.sum(paired * matching[:, None, :, None], axis=0)
        return finish_slot(totals)

    slot_rdm = lax.map(one_slot, (left_operators, left_table))
    inverse = jnp.zeros((LEFT_OPS,), jnp.int32).at[assignment].set(jnp.arange(LEFT_OPS, dtype=jnp.int32))
    direct = slot_rdm[inverse][:, :, 0]
    barred = slot_rdm[inverse[kramers_map]][:, :, 1]
    joined = jnp.stack([direct, barred], axis=2)
    return jnp.transpose(joined, (1, 2, 0, 3))
```

```python
import functools

import jax
import jax.numpy as jnp
from jax import lax
from jax.experimental import pallas as pl
from jax.experimental.pallas import tpu as pltpu
from jax.sharding import PartitionSpec as P

BF = jnp.bfloat16
F32 = jnp.float32
VMEM = 48 * 1024 * 1024


def iota(shape, axis):
    return lax.broadcasted_iota(jnp.int32, shape, axis)


def params():
    return pltpu.CompilerParams(vmem_limit_bytes=VMEM)


def pick_right_kernel(place_ref, right_ref, out_ref):
    to, of = iota((256, 256), 0), iota((256, 256), 1)
    a, c, j = to // 16, (to % 16) // 8, to % 8
    order = (of == (j * 2 + c) * 16 + a).astype(BF)
    for block in range(out_ref.shape[0]):
        rows = right_ref[block].reshape(256, 128)
        turned = jnp.dot(order, rows, preferred_element_type=F32).astype(BF)
        out_ref[block] = turned.reshape(16, 16, 128)


def pick_right(place, right_operators):
    view = right_operators.reshape(16, 2, 8, 2, 4, 16, 128)
    return pl.pallas_call(
        pick_right_kernel,
        grid_spec=pltpu.PrefetchScalarGridSpec(
            num_scalar_prefetch=1,
            grid=(4,),
            in_specs=[
                pl.BlockSpec(
                    (4, None, 8, 2, None, 16, 128),
                    lambda i, place: (i, place[0], 0, 0, place[1], 0, 0),
                )
            ],
            out_specs=pl.BlockSpec((4, 16, 16, 128), lambda i, place: (i, 0, 0, 0)),
        ),
        out_shape=jax.ShapeDtypeStruct((16, 16, 16, 128), BF),
        compiler_params=params(),
        name="pick_right",
    )(place, view)


def tiles_kernel(
    place_ref, own_wave, far_wave, own_left, far_left,
    home, up1, down1, up2, down2, sides, bras, stage,
):
    z = place_ref[2]
    low = z < 4

    def wave(c, o):
        mine, other = own_wave[c, o], far_wave[c, o]
        return jnp.concatenate(
            [jnp.where(low, mine, other), jnp.where(low, other, mine)], axis=0
        )

    for o in range(3):
        re, im = wave(0, o), wave(1, o)
        top = jnp.concatenate([re, im, re, im], axis=1)
        bottom = jnp.concatenate([-im, re, im, -re], axis=1)
        sides[o] = jnp.concatenate([top, bottom], axis=0)
        if o == 0:
            re_t, im_t = re.T, im.T
            bras[0] = jnp.concatenate([re_t, im_t], axis=1)
            bras[1] = jnp.concatenate([-im_t, re_t], axis=1)
    spots = [z, lax.rem(z + 1, 8), lax.rem(z + 7, 8), lax.rem(z + 2, 8), lax.rem(z + 6, 8)]
    bra = jnp.concatenate(
        [bras[c, pl.ds(pl.multiple_of(spot * 16, 16), 16), :] for c in range(2) for spot in spots],
        axis=0,
    )
    to, of = iota((256, 256), 0), iota((256, 256), 1)
    order = ((to // 16 == of % 16) & (to % 16 == of // 16)).astype(BF)
    outs = [home, up1, down1, up2, down2]
    for group in range(6):
        for member in range(4):
            s = group * 4 + member
            source = own_left if s < 12 else far_left
            operator = jnp.concatenate([source[s % 12, 0], source[s % 12, 1]], axis=1)
            side = sides[place_ref[3 + s]]
            turned = jnp.dot(operator, side, preferred_element_type=F32).astype(BF)
            ket = jnp.concatenate(
                [
                    jnp.concatenate([turned[:, 0:128], turned[:, 256:384]], axis=1),
                    jnp.concatenate([turned[:, 128:256], turned[:, 384:512]], axis=1),
                ],
                axis=0,
            )
            stage[member] = jnp.dot(bra, ket, preferred_element_type=F32).astype(BF)
        for spot, out in enumerate(outs):
            if spot == 3 and group >= 3 or spot == 4 and group < 3:
                continue
            rows = jnp.concatenate(
                [
                    stage[member, c * 80 + spot * 16 : c * 80 + spot * 16 + 16, kind * 128 : kind * 128 + 128]
                    for member in range(4)
                    for kind in range(2)
                    for c in range(2)
                ],
                axis=0,
            )
            turned = jnp.dot(order, rows, preferred_element_type=F32).astype(BF)
            out[group - 3 if spot == 4 else group] = turned.reshape(16, 16, 128)


def make_tiles(place, own_wave, far_wave, left_operators, far_left):
    full = lambda shape: pl.BlockSpec(shape, lambda i, place: (0,) * len(shape))
    sizes = [6, 6, 6, 3, 3]
    return pl.pallas_call(
        tiles_kernel,
        grid_spec=pltpu.PrefetchScalarGridSpec(
            num_scalar_prefetch=1,
            grid=(1,),
            in_specs=[
                full((2, 3, 64, 128)),
                full((2, 3, 64, 128)),
                pl.BlockSpec(
                    (12, None, 2, 128, 128), lambda i, place: (0, place[0], 0, 0, 0)
                ),
                full((12, 2, 128, 128)),
            ],
            out_specs=[full((n, 16, 16, 128)) for n in sizes],
            scratch_shapes=[
                pltpu.VMEM((3, 256, 512), BF),
                pltpu.VMEM((2, 128, 256), BF),
                pltpu.VMEM((4, 160, 256), BF),
            ],
        ),
        out_shape=[jax.ShapeDtypeStruct((n, 16, 16, 128), BF) for n in sizes],
        compiler_params=params(),
        name="make_tiles",
    )(place, own_wave, far_wave, left_operators, far_left)


def contract_kernel(
    home, up1, down1, up2, down2, right, slot_label, right_label, slot_key, real_key, imag_key, sign, out
):
    paired = jnp.zeros((256, 384), F32)
    for step in range(8):
        lefts = []
        rights = []
        for a in (2 * step, 2 * step + 1):
            lefts.append(
                jnp.concatenate(
                    [ref[:, a].reshape(-1, 128) for ref in (home, up1, down1, up2, down2)], axis=0
                )
            )
            rights.append(right[:, a].reshape(256, 128))
        paired += lax.dot_general(
            jnp.concatenate(rights, axis=1),
            jnp.concatenate(lefts, axis=1),
            (((1,), (1,)), ((), ())),
            preferred_element_type=F32,
        )
    paired = paired.reshape(16, 2, 8, 384)
    match = right_label[...] == slot_label[...]
    total = jnp.zeros((128, 384), F32)
    for c in range(2):
        part = jnp.where(match, paired[:, c].reshape(128, 384), 0.0)
        if c == 0:
            pick = (slot_key[...] == real_key[...]).astype(F32).astype(BF)
        else:
            pick = jnp.where(slot_key[...] == imag_key[...], sign[...], 0.0).astype(BF)
        for _ in range(3):
            piece = part.astype(BF)
            total += jnp.dot(piece, pick, preferred_element_type=F32)
            part = part - piece.astype(F32)
    out[...] = total.reshape(16, 8, 384)


def contract(tiles, right, labels):
    return pl.pallas_call(
        contract_kernel,
        out_shape=jax.ShapeDtypeStruct((16, 8, 384), F32),
        compiler_params=params(),
        name="contract",
    )(*tiles, right, *labels)


def ring(step):
    pairs = []
    for z in range(8):
        for core in range(2):
            place = lambda z: ((z % 4) * 2 + core) * 2 + z // 4
            pairs.append((place(z), place(step(z))))
    return pairs


def local(
    wave_blocks, left_operators, right_operators, left_table, right_table, assignment, kramers_map
):
    line = ("row", "wf")
    row, col, wf = lax.axis_index("row"), lax.axis_index("col"), lax.axis_index("wf")
    core, z_lo = row % 2, row // 2
    z = wf * 4 + z_lo
    q = 2 * col + core

    own_wave = jnp.concatenate(
        [lax.dynamic_slice_in_dim(wave_blocks, (q + o) % 32, 1, 1) for o in range(3)], axis=1
    )
    far_wave = lax.ppermute(
        own_wave, line, ring(lambda z: (z + 2) % 8 if z in (2, 3, 6, 7) else (z - 2) % 8)
    )
    swap = [(i, i ^ 1) for i in range(8)]
    give = lax.dynamic_index_in_dim(left_operators, 1 - core, 1, keepdims=False)
    far_left = lax.ppermute(give, "row", swap)
    columns = lax.dynamic_slice_in_dim(left_table, 2 * col, 2, 1)
    own_label = lax.dynamic_index_in_dim(columns, core, 1, keepdims=False)
    far_label = lax.ppermute(
        lax.dynamic_index_in_dim(columns, 1 - core, 1, keepdims=False), "row", swap
    )
    shift = jnp.mod(jnp.concatenate([own_label, far_label]) - q, 32)
    place = jnp.stack([core, z_lo, z]).astype(jnp.int32)
    right = pick_right(place, right_operators)
    home, up1, down1, up2, down2 = make_tiles(
        jnp.concatenate([place, shift]), own_wave, far_wave, left_operators, far_left
    )
    right, home = lax.optimization_barrier((right, home))
    tiles = [
        home,
        lax.ppermute(up1, line, ring(lambda z: (z + 1) % 8)),
        lax.ppermute(down1, line, ring(lambda z: (z + 7) % 8)),
        lax.ppermute(up2, line, ring(lambda z: (z + 2) % 8)),
        lax.ppermute(down2, line, ring(lambda z: (z + 6) % 8)),
    ]
    right = lax.all_to_all(right, "col", 0, 0, tiled=True)

    all_table = lax.all_gather(left_table, "row", axis=0, tiled=True)
    q_label = lax.dynamic_index_in_dim(all_table, q, 1, keepdims=False)
    both = jnp.stack([q_label, assignment], axis=0).reshape(2, 4, 2, 12)
    both = jnp.where(core == 0, both, both[:, :, ::-1])
    both = jnp.concatenate([both, both], axis=1)
    both = lax.dynamic_slice_in_dim(both, z_lo, 4, 1)
    both = both[:, jnp.array([0, 3, 1, 2])].reshape(2, 96)
    kind_c = jnp.arange(4, dtype=jnp.int32)
    slot_label = jnp.repeat(both[0], 4)[None, :]
    slot_key = (both[1][:, None] * 4 + kind_c[None, :]).reshape(384, 1)
    right_label = lax.dynamic_index_in_dim(right_table, q, 1, keepdims=True)
    target = jnp.stack([jnp.arange(96, dtype=jnp.int32), kramers_map]).reshape(1, 2, 8, 12)
    target = target.transpose(2, 0, 1, 3)
    kind = jnp.arange(2, dtype=jnp.int32)[None, None, :, None]
    part = jnp.arange(2, dtype=jnp.int32)[None, :, None, None]
    real_key = (target * 4 + kind * 2 + part).reshape(1, 384)
    imag_key = (target * 4 + kind * 2 + 1 - part).reshape(1, 384)
    sign = jnp.broadcast_to((2 * part - 1).astype(F32), (8, 2, 2, 12)).reshape(1, 384)

    shares = contract(
        tiles, right, [slot_label, right_label, slot_key, real_key, imag_key, sign]
    )
    shares = jnp.sum(lax.all_to_all(shares, "col", 0, 0, tiled=True), axis=0)
    shares = shares.reshape(2, 4, 8, 48).transpose(2, 0, 1, 3).reshape(16, 192)
    total = jnp.sum(lax.all_to_all(shares, line, 0, 0, tiled=True), axis=0)
    return total.reshape(4, 2, 2, 12).transpose(1, 2, 3, 0)


def solution(mesh):
    return jax.shard_map(
        local,
        mesh=mesh,
        in_specs=(
            P(None, None, "wf", None),
            P("row", "col", None, None, None),
            P(None, "col", None, "wf", None),
            P("row", None),
            P(),
            P(),
            P(),
        ),
        out_specs=P(None, None, "row", ("col", "wf")),
        check_vma=False,
    )
```

```python
import functools

import jax
import jax.numpy as jnp
from jax import lax
from jax.experimental import pallas as pl
from jax.experimental.pallas import tpu as pltpu
from jax.sharding import PartitionSpec as P

BF = jnp.bfloat16
F32 = jnp.float32
VMEM = 48 * 1024 * 1024


def iota(shape, axis):
    return lax.broadcasted_iota(jnp.int32, shape, axis)


def params():
    return pltpu.CompilerParams(vmem_limit_bytes=VMEM)


def pick_right_kernel(place_ref, right_ref, out_ref):
    for block in range(out_ref.shape[0]):
        rows = jnp.concatenate(
            [right_ref[block, j, c][None] for c in range(2) for j in range(8)], axis=0
        )
        out_ref[block] = jnp.swapaxes(rows, 0, 1)


def pick_right(place, right_operators):
    view = right_operators.reshape(16, 2, 8, 2, 4, 16, 128)
    return pl.pallas_call(
        pick_right_kernel,
        grid_spec=pltpu.PrefetchScalarGridSpec(
            num_scalar_prefetch=1,
            grid=(4,),
            in_specs=[
                pl.BlockSpec(
                    (4, None, 8, 2, None, 16, 128),
                    lambda i, place: (i, place[0], 0, 0, place[1], 0, 0),
                )
            ],
            out_specs=pl.BlockSpec((4, 16, 16, 128), lambda i, place: (i, 0, 0, 0)),
        ),
        out_shape=jax.ShapeDtypeStruct((16, 16, 16, 128), BF),
        compiler_params=params(),
        name="pick_right",
    )(place, view)


GROUPS = (6, 6, 6, 3, 3)
STARTS = (0, 96, 192, 288, 336)


def tiles_kernel(
    place_ref, own_table, far_table, own_wave, far_wave, own_left, far_left,
    home, up1, down1, up2, down2, sides, bras, kets,
):
    z, q = place_ref[2], place_ref[3]
    outs = (home, up1, down1, up2, down2)
    low = z < 4

    def wave(c, o):
        mine, other = own_wave[c, o], far_wave[c, o]
        return jnp.concatenate(
            [jnp.where(low, mine, other), jnp.where(low, other, mine)], axis=0
        )

    for o in range(3):
        re, im = wave(0, o), wave(1, o)
        top = jnp.concatenate([re, im, re, im], axis=1)
        bottom = jnp.concatenate([-im, re, im, -re], axis=1)
        sides[o] = jnp.concatenate([top, bottom], axis=0)
        if o == 0:
            re_t, im_t = re.T, im.T
            bras[0] = jnp.concatenate([re_t, im_t], axis=1)
            bras[1] = jnp.concatenate([-im_t, re_t], axis=1)
    spots = [z, lax.rem(z + 1, 8), lax.rem(z + 7, 8), lax.rem(z + 2, 8), lax.rem(z + 6, 8)]

    def bra(picked):
        return jnp.concatenate(
            [
                bras[c, pl.ds(pl.multiple_of(spots[i] * 16, 16), 16), :]
                for c in range(2)
                for i in picked
            ],
            axis=0,
        )

    labels = [own_table[s, q] for s in range(12)] + [far_table[s, q] for s in range(12)]
    shifts = [lax.rem(label - q + 32, 32) for label in labels]
    for half in range(2):
        picked = (0, 1, 2, 3 + half)
        left = bra(picked)
        source = far_left if half else own_left
        for s in range(12):
            operator = jnp.concatenate([source[s, 0], source[s, 1]], axis=1)
            turned = jnp.dot(
                operator, sides[shifts[half * 12 + s]], preferred_element_type=F32
            ).astype(BF)
            kets[s] = jnp.concatenate(
                [
                    jnp.concatenate([turned[:, 0:128], turned[:, 256:384]], axis=1),
                    jnp.concatenate([turned[:, 128:256], turned[:, 384:512]], axis=1),
                ],
                axis=0,
            )
        for group in range(3):
            brackets = [
                jnp.dot(left, kets[group * 4 + s], preferred_element_type=F32).astype(BF)
                for s in range(4)
            ]
            for i, spot in enumerate(picked):
                rows = jnp.concatenate(
                    [
                        brackets[s][
                            c * 64 + i * 16 : c * 64 + i * 16 + 16,
                            kind * 128 : kind * 128 + 128,
                        ][None]
                        for s in range(4)
                        for kind in range(2)
                        for c in range(2)
                    ],
                    axis=0,
                )
                first = (group if spot > 2 else half * 3 + group) * 16
                outs[spot][first : first + 16] = jnp.swapaxes(rows, 0, 1)
    for spot, out in enumerate(outs):
        count = GROUPS[spot] * 4
        offset = 12 if spot == 4 else 0
        for tile in range(3):
            place = (iota((16, 128), 1) + tile * 128 - STARTS[spot]) // 4
            row = jnp.zeros((16, 128), F32)
            low_s, high_s = (tile * 128 - STARTS[spot]) // 4, (tile * 128 + 128 - STARTS[spot]) // 4
            for s in range(max(0, low_s), min(count, high_s)):
                row = jnp.where(place == s, labels[offset + s].astype(F32), row)
            out[GROUPS[spot] * 16 + tile] = row.astype(BF)


def make_tiles(place, own_table, far_table, own_wave, far_wave, left_operators, far_left):
    full = lambda shape: pl.BlockSpec(shape, lambda i, place: (0,) * len(shape))
    table = pl.BlockSpec(memory_space=pltpu.SMEM)
    operators = pl.BlockSpec(
        (12, None, 2, 128, 128), lambda i, place: (0, place[0], 0, 0, 0)
    )
    return pl.pallas_call(
        tiles_kernel,
        grid_spec=pltpu.PrefetchScalarGridSpec(
            num_scalar_prefetch=1,
            grid=(1,),
            in_specs=[
                table, table, full((2, 3, 64, 128)), full((2, 3, 64, 128)), operators, operators
            ],
            out_specs=[full((n * 16 + 3, 16, 128)) for n in GROUPS],
            scratch_shapes=[
                pltpu.VMEM((3, 256, 512), BF),
                pltpu.VMEM((2, 128, 256), BF),
                pltpu.VMEM((12, 256, 256), BF),
            ],
        ),
        out_shape=[jax.ShapeDtypeStruct((n * 16 + 3, 16, 128), BF) for n in GROUPS],
        compiler_params=params(),
        name="make_tiles",
    )(place, own_table, far_table, own_wave, far_wave, left_operators, far_left)


def contract_kernel(
    place_ref, home, up1, down1, up2, down2, right, right_table, slot_key, real_key, imag_key, sign, out
):
    arrays = (home, up1, down1, up2, down2)
    paired = jnp.zeros((256, 384), F32)
    for step in range(8):
        lefts = []
        rights = []
        for a in (2 * step, 2 * step + 1):
            lefts.append(
                jnp.concatenate(
                    [ref[g * 16 + a] for ref, n in zip(arrays, GROUPS) for g in range(n)], axis=0
                )
            )
            rights.append(right[:, a].reshape(256, 128))
        paired += lax.dot_general(
            jnp.concatenate(rights, axis=1),
            jnp.concatenate(lefts, axis=1),
            (((1,), (1,)), ((), ())),
            preferred_element_type=F32,
        )
    paired = paired.reshape(16, 2, 8, 384)
    slot_label = jnp.concatenate(
        [
            sum(ref[n * 16 + tile].astype(F32)[0:1] for ref, n in zip(arrays, GROUPS))
            for tile in range(3)
        ],
        axis=1,
    )
    here = iota((128, 32), 1) == place_ref[3]
    right_label = jnp.sum(
        jnp.where(here, right_table[...].astype(F32), 0.0), axis=1, keepdims=True
    )
    match = right_label == slot_label
    total = jnp.zeros((128, 384), F32)
    for c in range(2):
        part = jnp.where(match, paired[:, c].reshape(128, 384), 0.0)
        if c == 0:
            pick = (slot_key[...] == real_key[...]).astype(F32).astype(BF)
        else:
            pick = jnp.where(slot_key[...] == imag_key[...], sign[...], 0.0).astype(BF)
        for _ in range(3):
            piece = part.astype(BF)
            total += jnp.dot(piece, pick, preferred_element_type=F32)
            part = part - piece.astype(F32)
    out[...] = total.reshape(16, 8, 384)


def contract(place, tiles, right, right_table, keys):
    whole = pl.BlockSpec(memory_space=pltpu.VMEM)
    return pl.pallas_call(
        contract_kernel,
        in_specs=[pl.BlockSpec(memory_space=pltpu.SMEM)] + [whole] * 11,
        out_shape=jax.ShapeDtypeStruct((16, 8, 384), F32),
        compiler_params=params(),
        name="contract",
    )(place, *tiles, right, right_table, *keys)


def ring(step):
    pairs = []
    for z in range(8):
        for core in range(2):
            place = lambda z: ((z % 4) * 2 + core) * 2 + z // 4
            pairs.append((place(z), place(step(z))))
    return pairs


def local(
    wave_blocks, left_operators, right_operators, left_table, right_table, assignment, kramers_map
):
    line = ("row", "wf")
    row, col, wf = lax.axis_index("row"), lax.axis_index("col"), lax.axis_index("wf")
    core, z_lo = row % 2, row // 2
    z = wf * 4 + z_lo
    q = 2 * col + core

    own_wave = jnp.concatenate(
        [lax.dynamic_slice_in_dim(wave_blocks, (q + o) % 32, 1, 1) for o in range(3)], axis=1
    )
    far_wave = lax.ppermute(
        own_wave, line, ring(lambda z: (z + 2) % 8 if z in (2, 3, 6, 7) else (z - 2) % 8)
    )
    swap = [(i, i ^ 1) for i in range(8)]
    far_left = lax.ppermute(left_operators, "row", swap)
    far_table = lax.ppermute(left_table, "row", swap)
    place = jnp.stack([core, z_lo, z, q]).astype(jnp.int32)
    right = pick_right(place, right_operators)
    right = lax.all_to_all(right, "col", 0, 0, tiled=True)
    home, up1, down1, up2, down2 = make_tiles(
        place, left_table, far_table, own_wave, far_wave, left_operators, far_left
    )
    tiles = [
        home,
        lax.ppermute(up1, line, ring(lambda z: (z + 1) % 8)),
        lax.ppermute(down1, line, ring(lambda z: (z + 7) % 8)),
        lax.ppermute(up2, line, ring(lambda z: (z + 2) % 8)),
        lax.ppermute(down2, line, ring(lambda z: (z + 6) % 8)),
    ]

    held = assignment.reshape(4, 2, 12)
    held = jnp.where(core == 0, held, held[:, ::-1])
    held = lax.dynamic_slice_in_dim(jnp.concatenate([held, held], axis=0), z_lo, 4, 0)
    held = jnp.concatenate([held[0:1], held[3:4], held[1:3]], axis=0).reshape(96, 1)
    slot_key = (held * 4 + jnp.arange(4, dtype=jnp.int32)[None, :]).reshape(384, 1)
    target = jnp.stack([jnp.arange(96, dtype=jnp.int32), kramers_map]).reshape(1, 2, 8, 12)
    target = target.transpose(2, 0, 1, 3)
    kind = jnp.arange(2, dtype=jnp.int32)[None, None, :, None]
    part = jnp.arange(2, dtype=jnp.int32)[None, :, None, None]
    real_key = (target * 4 + kind * 2 + part).reshape(1, 384)
    imag_key = (target * 4 + kind * 2 + 1 - part).reshape(1, 384)
    sign = jnp.broadcast_to((2 * part - 1).astype(F32), (8, 2, 2, 12)).reshape(1, 384)

    shares = contract(place, tiles, right, right_table, [slot_key, real_key, imag_key, sign])
    shares = jnp.sum(lax.all_to_all(shares, "col", 0, 0, tiled=True), axis=0)
    shares = shares.reshape(2, 4, 8, 4, 12).transpose(2, 0, 3, 1, 4).reshape(16, 192)
    total = jnp.sum(lax.all_to_all(shares, line, 0, 0, tiled=True), axis=0)
    return total.reshape(2, 2, 4, 12).transpose(0, 1, 3, 2)


def solution(mesh):
    return jax.shard_map(
        local,
        mesh=mesh,
        in_specs=(
            P(None, None, "wf", None),
            P("row", "col", None, None, None),
            P(None, "col", None, "wf", None),
            P("row", None),
            P(),
            P(),
            P(),
        ),
        out_specs=P(None, None, "row", ("col", "wf")),
        check_vma=False,
    )
```

```python
import functools

import jax
import jax.numpy as jnp
from jax import lax
from jax.experimental import pallas as pl
from jax.experimental.pallas import tpu as pltpu
from jax.sharding import PartitionSpec as P

BF = jnp.bfloat16
F32 = jnp.float32
VMEM = 48 * 1024 * 1024


def iota(shape, axis):
    return lax.broadcasted_iota(jnp.int32, shape, axis)


def params():
    return pltpu.CompilerParams(vmem_limit_bytes=VMEM)


def pick_right_kernel(place_ref, near_ref, cross_ref, out_ref):
    for block in range(out_ref.shape[0]):
        for ref, first in ((near_ref, 0), (cross_ref, 8)):
            rows = jnp.concatenate(
                [ref[block, j, c][None] for c in range(2) for j in range(8)], axis=0
            )
            rows = jnp.swapaxes(rows, 0, 1)
            if first:
                out_ref[block, 16:24] = rows[8:16]
            else:
                out_ref[block, 0:16] = rows


def pick_right(place, right_operators):
    view = right_operators.reshape(16, 2, 8, 2, 4, 16, 128)
    rows = lambda flip: pl.BlockSpec(
        (8, None, 8, 2, None, 16, 128),
        lambda i, place: (i, place[0], 0, 0, place[1] ^ flip, 0, 0),
    )
    return pl.pallas_call(
        pick_right_kernel,
        grid_spec=pltpu.PrefetchScalarGridSpec(
            num_scalar_prefetch=1,
            grid=(2,),
            in_specs=[rows(0), rows(2)],
            out_specs=pl.BlockSpec((8, 24, 16, 128), lambda i, place: (i, 0, 0, 0)),
        ),
        out_shape=jax.ShapeDtypeStruct((16, 24, 16, 128), BF),
        compiler_params=params(),
        name="pick_right",
    )(place, view, view)


GROUPS = (6, 6, 6, 3, 3)
ROWS = (24, 16, 16, 8, 8)
STARTS = (0, 96, 192, 288, 336)
TILES = tuple(n * rows for n, rows in zip(GROUPS, ROWS))


def tiles_kernel(
    place_ref, own_table, far_table, own_wave, far_wave, own_left, far_left,
    home, up1, down1, up2, down2, sides, bras, kets,
):
    z, q = place_ref[2], place_ref[3]
    outs = (home, up1, down1, up2, down2)
    low = z < 4

    def wave(c, o):
        mine, other = own_wave[c, o], far_wave[c, o]
        return jnp.concatenate(
            [jnp.where(low, mine, other), jnp.where(low, other, mine)], axis=0
        )

    for o in range(3):
        re, im = wave(0, o), wave(1, o)
        top = jnp.concatenate([re, im, re, im], axis=1)
        bottom = jnp.concatenate([-im, re, im, -re], axis=1)
        sides[o] = jnp.concatenate([top, bottom], axis=0)
        if o == 0:
            re_t, im_t = re.T, im.T
            bras[0] = jnp.concatenate([re_t, im_t], axis=1)
            bras[1] = jnp.concatenate([-im_t, re_t], axis=1)
    spots = [z, lax.rem(z + 1, 8), lax.rem(z + 7, 8), lax.rem(z + 2, 8), lax.rem(z + 6, 8)]

    upper = iota((16, 256), 0) < 8

    def bra(far):
        def block(c, spot):
            return bras[c, pl.ds(pl.multiple_of(spot * 16, 16), 16), :]

        parts = []
        for c in range(2):
            parts += [block(c, spot) for spot in spots[0:3]]
            parts.append(jnp.where(upper, block(c, spots[far]), block(c, z ^ 2)))
        return jnp.concatenate(parts, axis=0)

    labels = [own_table[s, q] for s in range(12)] + [far_table[s, q] for s in range(12)]
    shifts = [lax.rem(label - q + 32, 32) for label in labels]
    for half in range(2):
        left = bra(3 + half)
        source = far_left if half else own_left
        for s in range(12):
            operator = jnp.concatenate([source[s, 0], source[s, 1]], axis=1)
            turned = jnp.dot(
                operator, sides[shifts[half * 12 + s]], preferred_element_type=F32
            ).astype(BF)
            kets[s] = jnp.concatenate(
                [
                    jnp.concatenate([turned[:, 0:128], turned[:, 256:384]], axis=1),
                    jnp.concatenate([turned[:, 128:256], turned[:, 384:512]], axis=1),
                ],
                axis=0,
            )
        for group in range(3):
            brackets = [
                jnp.dot(left, kets[group * 4 + s], preferred_element_type=F32).astype(BF)
                for s in range(4)
            ]
            for i in range(4):
                rows = jnp.concatenate(
                    [
                        brackets[s][
                            c * 64 + i * 16 : c * 64 + i * 16 + 16,
                            kind * 128 : kind * 128 + 128,
                        ][None]
                        for s in range(4)
                        for kind in range(2)
                        for c in range(2)
                    ],
                    axis=0,
                )
                rows = jnp.swapaxes(rows, 0, 1)
                whole = half * 3 + group
                if i < 3:
                    outs[i][whole * 16 : whole * 16 + 16] = rows
                else:
                    outs[3 + half][group * 8 : group * 8 + 8] = rows[0:8]
                    home[96 + whole * 8 : 96 + whole * 8 + 8] = rows[8:16]
    for spot, out in enumerate(outs):
        count = GROUPS[spot] * 4
        offset = 12 if spot == 4 else 0
        for tile in range(3):
            place = (iota((16, 128), 1) + tile * 128 - STARTS[spot]) // 4
            row = jnp.zeros((16, 128), F32)
            low_s, high_s = (tile * 128 - STARTS[spot]) // 4, (tile * 128 + 128 - STARTS[spot]) // 4
            for s in range(max(0, low_s), min(count, high_s)):
                row = jnp.where(place == s, labels[offset + s].astype(F32), row)
            out[TILES[spot] + tile] = row.astype(BF)


def make_tiles(place, own_table, far_table, own_wave, far_wave, left_operators, far_left):
    full = lambda shape: pl.BlockSpec(shape, lambda i, place: (0,) * len(shape))
    table = pl.BlockSpec(memory_space=pltpu.SMEM)
    operators = pl.BlockSpec(
        (12, None, 2, 128, 128), lambda i, place: (0, place[0], 0, 0, 0)
    )
    return pl.pallas_call(
        tiles_kernel,
        grid_spec=pltpu.PrefetchScalarGridSpec(
            num_scalar_prefetch=1,
            grid=(1,),
            in_specs=[
                table, table, full((2, 3, 64, 128)), full((2, 3, 64, 128)), operators, operators
            ],
            out_specs=[full((n + 3, 16, 128)) for n in TILES],
            scratch_shapes=[
                pltpu.VMEM((3, 256, 512), BF),
                pltpu.VMEM((2, 128, 256), BF),
                pltpu.VMEM((12, 256, 256), BF),
            ],
        ),
        out_shape=[jax.ShapeDtypeStruct((n + 3, 16, 128), BF) for n in TILES],
        compiler_params=params(),
        name="make_tiles",
    )(place, own_table, far_table, own_wave, far_wave, left_operators, far_left)


def contract_kernel(
    place_ref, home, up1, down1, up2, down2, right, right_table, slot_key, real_key, imag_key, sign, out
):
    arrays = (home, up1, down1, up2, down2)
    zero = jnp.zeros((96, 128), BF)

    def lefts(a):
        if a >= 16:
            return [home[96 + g * 8 + a - 16] for g in range(6)] + [zero[0:32]]
        tiles = [ref[g * 16 + a] for ref in arrays[0:3] for g in range(6)]
        if a >= 8:
            return tiles + [zero]
        return tiles + [ref[g * 8 + a] for ref in arrays[3:5] for g in range(3)]

    def product(start):
        total = 0.0
        for a in range(start, start + 8, 2):
            total += lax.dot_general(
                jnp.concatenate([right[:, a + i].reshape(256, 128) for i in range(2)], axis=1),
                jnp.concatenate(
                    [jnp.concatenate(lefts(a + i), axis=0) for i in range(2)], axis=1
                ),
                (((1,), (1,)), ((), ())),
                preferred_element_type=F32,
            )
        return total

    paired = product(0) + product(8)
    paired = jnp.concatenate([paired[:, 0:128] + product(16), paired[:, 128:384]], axis=1)
    paired = paired.reshape(16, 2, 8, 384)
    slot_label = jnp.concatenate(
        [
            sum(ref[n + tile].astype(F32)[0:1] for ref, n in zip(arrays, TILES))
            for tile in range(3)
        ],
        axis=1,
    )
    here = iota((128, 32), 1) == place_ref[3]
    right_label = jnp.sum(
        jnp.where(here, right_table[...].astype(F32), 0.0), axis=1, keepdims=True
    )
    match = right_label == slot_label
    total = jnp.zeros((128, 384), F32)
    for c in range(2):
        part = jnp.where(match, paired[:, c].reshape(128, 384), 0.0)
        if c == 0:
            pick = (slot_key[...] == real_key[...]).astype(F32).astype(BF)
        else:
            pick = jnp.where(slot_key[...] == imag_key[...], sign[...], 0.0).astype(BF)
        for _ in range(3):
            piece = part.astype(BF)
            total += jnp.dot(piece, pick, preferred_element_type=F32)
            part = part - piece.astype(F32)
    out[...] = total.reshape(16, 8, 384)


def contract(place, tiles, right, right_table, keys):
    whole = pl.BlockSpec(memory_space=pltpu.VMEM)
    return pl.pallas_call(
        contract_kernel,
        in_specs=[pl.BlockSpec(memory_space=pltpu.SMEM)] + [whole] * 11,
        out_shape=jax.ShapeDtypeStruct((16, 8, 384), F32),
        compiler_params=params(),
        name="contract",
    )(place, *tiles, right, right_table, *keys)


def ring(step):
    pairs = []
    for z in range(8):
        for core in range(2):
            place = lambda z: ((z % 4) * 2 + core) * 2 + z // 4
            pairs.append((place(z), place(step(z))))
    return pairs


def local(
    wave_blocks, left_operators, right_operators, left_table, right_table, assignment, kramers_map
):
    line = ("row", "wf")
    row, col, wf = lax.axis_index("row"), lax.axis_index("col"), lax.axis_index("wf")
    core, z_lo = row % 2, row // 2
    z = wf * 4 + z_lo
    q = 2 * col + core

    own_wave = jnp.concatenate(
        [lax.dynamic_slice_in_dim(wave_blocks, (q + o) % 32, 1, 1) for o in range(3)], axis=1
    )
    far_wave = lax.ppermute(
        own_wave, line, ring(lambda z: (z + 2) % 8 if z in (2, 3, 6, 7) else (z - 2) % 8)
    )
    swap = [(i, i ^ 1) for i in range(8)]
    far_left = lax.ppermute(left_operators, "row", swap)
    far_table = lax.ppermute(left_table, "row", swap)
    place = jnp.stack([core, z_lo, z, q]).astype(jnp.int32)
    right = pick_right(place, right_operators)
    right = lax.all_to_all(right, "col", 0, 0, tiled=True)
    home, up1, down1, up2, down2 = make_tiles(
        place, left_table, far_table, own_wave, far_wave, left_operators, far_left
    )
    tiles = [
        home,
        lax.ppermute(up1, line, ring(lambda z: (z + 1) % 8)),
        lax.ppermute(down1, line, ring(lambda z: (z + 7) % 8)),
        lax.ppermute(up2, line, ring(lambda z: (z + 2) % 8)),
        lax.ppermute(down2, line, ring(lambda z: (z + 6) % 8)),
    ]

    held = assignment.reshape(4, 2, 12)
    held = jnp.where(core == 0, held, held[:, ::-1])
    held = lax.dynamic_slice_in_dim(jnp.concatenate([held, held], axis=0), z_lo, 4, 0)
    held = jnp.concatenate([held[0:1], held[3:4], held[1:3]], axis=0).reshape(96, 1)
    slot_key = (held * 4 + jnp.arange(4, dtype=jnp.int32)[None, :]).reshape(384, 1)
    target = jnp.stack([jnp.arange(96, dtype=jnp.int32), kramers_map]).reshape(1, 2, 8, 12)
    target = target.transpose(2, 0, 1, 3)
    kind = jnp.arange(2, dtype=jnp.int32)[None, None, :, None]
    part = jnp.arange(2, dtype=jnp.int32)[None, :, None, None]
    real_key = (target * 4 + kind * 2 + part).reshape(1, 384)
    imag_key = (target * 4 + kind * 2 + 1 - part).reshape(1, 384)
    sign = jnp.broadcast_to((2 * part - 1).astype(F32), (8, 2, 2, 12)).reshape(1, 384)

    shares = contract(place, tiles, right, right_table, [slot_key, real_key, imag_key, sign])
    shares = jnp.sum(lax.all_to_all(shares, "col", 0, 0, tiled=True), axis=0)
    shares = shares.reshape(2, 4, 8, 4, 12).transpose(2, 0, 3, 1, 4).reshape(16, 192)
    total = jnp.sum(lax.all_to_all(shares, line, 0, 0, tiled=True), axis=0)
    return total.reshape(2, 2, 4, 12).transpose(0, 1, 3, 2)


def solution(mesh):
    return jax.shard_map(
        local,
        mesh=mesh,
        in_specs=(
            P(None, None, "wf", None),
            P("row", "col", None, None, None),
            P(None, "col", None, "wf", None),
            P("row", None),
            P(),
            P(),
            P(),
        ),
        out_specs=P(None, None, "row", ("col", "wf")),
        check_vma=False,
    )
```

```python
import functools

import jax
import jax.numpy as jnp
from jax import lax
from jax.experimental import pallas as pl
from jax.experimental.pallas import tpu as pltpu
from jax.sharding import PartitionSpec as P

BF = jnp.bfloat16
F32 = jnp.float32


def iota(shape, axis):
    return lax.broadcasted_iota(jnp.int32, shape, axis)


def params(mebibytes):
    return pltpu.CompilerParams(vmem_limit_bytes=mebibytes * 1024 * 1024)


def pick_right_kernel(place_ref, near_ref, cross_ref, out_ref):
    for block in range(out_ref.shape[0]):
        for ref, first in ((near_ref, 0), (cross_ref, 8)):
            rows = jnp.concatenate(
                [ref[block, j, c][None] for c in range(2) for j in range(8)], axis=0
            )
            rows = jnp.swapaxes(rows, 0, 1)
            if first:
                out_ref[block, 16:24] = rows[8:16]
            else:
                out_ref[block, 0:16] = rows


def pick_right(place, right_operators):
    view = right_operators.reshape(16, 2, 8, 2, 4, 16, 128)
    rows = lambda flip: pl.BlockSpec(
        (8, None, 8, 2, None, 16, 128),
        lambda i, place: (i, place[0], 0, 0, place[1] ^ flip, 0, 0),
    )
    return pl.pallas_call(
        pick_right_kernel,
        grid_spec=pltpu.PrefetchScalarGridSpec(
            num_scalar_prefetch=1,
            grid=(2,),
            in_specs=[rows(0), rows(2)],
            out_specs=pl.BlockSpec((8, 24, 16, 128), lambda i, place: (i, 0, 0, 0)),
        ),
        out_shape=jax.ShapeDtypeStruct((16, 24, 16, 128), BF),
        compiler_params=params(12),
        name="pick_right",
    )(place, view, view)


GROUPS = (6, 6, 6, 3, 3)
ROWS = (24, 16, 16, 8, 8)
STARTS = (0, 96, 192, 288, 336)
TILES = tuple(n * rows for n, rows in zip(GROUPS, ROWS))


def tiles_kernel(
    place_ref, own_table, far_table, own_wave, far_wave, own_left, far_left,
    home, up1, down1, up2, down2, sides, bras, kets,
):
    z, q = place_ref[2], place_ref[3]
    outs = (home, up1, down1, up2, down2)
    low = z < 4

    def wave(c, o):
        mine, other = own_wave[c, o], far_wave[c, o]
        return jnp.concatenate(
            [jnp.where(low, mine, other), jnp.where(low, other, mine)], axis=0
        )

    for o in range(3):
        re, im = wave(0, o), wave(1, o)
        top = jnp.concatenate([re, im, re, im], axis=1)
        bottom = jnp.concatenate([-im, re, im, -re], axis=1)
        sides[o] = jnp.concatenate([top, bottom], axis=0)
        if o == 0:
            re_t, im_t = re.T, im.T
            bras[0] = jnp.concatenate([re_t, im_t], axis=1)
            bras[1] = jnp.concatenate([-im_t, re_t], axis=1)
    spots = [z, lax.rem(z + 1, 8), lax.rem(z + 7, 8), lax.rem(z + 2, 8), lax.rem(z + 6, 8)]

    upper = iota((16, 256), 0) < 8

    def bra(far):
        def block(c, spot):
            return bras[c, pl.ds(pl.multiple_of(spot * 16, 16), 16), :]

        parts = []
        for c in range(2):
            parts += [block(c, spot) for spot in spots[0:3]]
            parts.append(jnp.where(upper, block(c, spots[far]), block(c, z ^ 2)))
        return jnp.concatenate(parts, axis=0)

    labels = [own_table[s, q] for s in range(12)] + [far_table[s, q] for s in range(12)]
    shifts = [lax.rem(label - q + 32, 32) for label in labels]
    for half in range(2):
        left = bra(3 + half)
        source = far_left if half else own_left
        for s in range(12):
            operator = jnp.concatenate([source[s, 0], source[s, 1]], axis=1)
            turned = jnp.dot(
                operator, sides[shifts[half * 12 + s]], preferred_element_type=F32
            ).astype(BF)
            kets[s] = jnp.concatenate(
                [
                    jnp.concatenate([turned[:, 0:128], turned[:, 256:384]], axis=1),
                    jnp.concatenate([turned[:, 128:256], turned[:, 384:512]], axis=1),
                ],
                axis=0,
            )
        for group in range(3):
            brackets = [
                jnp.dot(left, kets[group * 4 + s], preferred_element_type=F32).astype(BF)
                for s in range(4)
            ]
            for i in range(4):
                rows = jnp.concatenate(
                    [
                        brackets[s][
                            c * 64 + i * 16 : c * 64 + i * 16 + 16,
                            kind * 128 : kind * 128 + 128,
                        ][None]
                        for s in range(4)
                        for kind in range(2)
                        for c in range(2)
                    ],
                    axis=0,
                )
                rows = jnp.swapaxes(rows, 0, 1)
                whole = half * 3 + group
                if i < 3:
                    outs[i][whole * 16 : whole * 16 + 16] = rows
                else:
                    outs[3 + half][group * 8 : group * 8 + 8] = rows[0:8]
                    home[96 + whole * 8 : 96 + whole * 8 + 8] = rows[8:16]
    for spot, out in enumerate(outs):
        count = GROUPS[spot] * 4
        offset = 12 if spot == 4 else 0
        for tile in range(3):
            place = (iota((16, 128), 1) + tile * 128 - STARTS[spot]) // 4
            row = jnp.zeros((16, 128), F32)
            low_s, high_s = (tile * 128 - STARTS[spot]) // 4, (tile * 128 + 128 - STARTS[spot]) // 4
            for s in range(max(0, low_s), min(count, high_s)):
                row = jnp.where(place == s, labels[offset + s].astype(F32), row)
            out[TILES[spot] + tile] = row.astype(BF)


def make_tiles(place, own_table, far_table, own_wave, far_wave, left_operators, far_left):
    full = lambda shape: pl.BlockSpec(shape, lambda i, place: (0,) * len(shape))
    table = pl.BlockSpec(memory_space=pltpu.SMEM)
    operators = pl.BlockSpec(
        (12, None, 2, 128, 128), lambda i, place: (0, place[0], 0, 0, 0)
    )
    return pl.pallas_call(
        tiles_kernel,
        grid_spec=pltpu.PrefetchScalarGridSpec(
            num_scalar_prefetch=1,
            grid=(1,),
            in_specs=[
                table, table, full((2, 3, 64, 128)), full((2, 3, 64, 128)), operators, operators
            ],
            out_specs=[full((n + 3, 16, 128)) for n in TILES],
            scratch_shapes=[
                pltpu.VMEM((3, 256, 512), BF),
                pltpu.VMEM((2, 128, 256), BF),
                pltpu.VMEM((12, 256, 256), BF),
            ],
        ),
        out_shape=[jax.ShapeDtypeStruct((n + 3, 16, 128), BF) for n in TILES],
        compiler_params=params(20),
        name="make_tiles",
    )(place, own_table, far_table, own_wave, far_wave, left_operators, far_left)


def picks_kernel(slot_key, real_key, imag_key, sign, out):
    out[0:384] = (slot_key[...] == real_key[...]).astype(F32).astype(BF)
    out[384:768] = jnp.where(slot_key[...] == imag_key[...], sign[...], 0.0).astype(BF)


def make_picks(keys):
    return pl.pallas_call(
        picks_kernel,
        out_shape=jax.ShapeDtypeStruct((768, 384), BF),
        compiler_params=params(8),
        name="make_picks",
    )(*keys)


def contract_kernel(
    place_ref, home, up1, down1, up2, down2, right, right_table, picks, out, paired_ref
):
    arrays = (home, up1, down1, up2, down2)
    zero = jnp.zeros((96, 128), BF)

    def lefts(a):
        if a >= 16:
            return [home[96 + g * 8 + a - 16] for g in range(6)] + [zero[0:32]]
        tiles = [ref[g * 16 + a] for ref in arrays[0:3] for g in range(6)]
        if a >= 8:
            return tiles + [zero]
        return tiles + [ref[g * 8 + a] for ref in arrays[3:5] for g in range(3)]

    def product(start):
        total = 0.0
        for a in range(start, start + 8, 2):
            total += lax.dot_general(
                jnp.concatenate([right[:, a + i].reshape(256, 128) for i in range(2)], axis=1),
                jnp.concatenate(
                    [jnp.concatenate(lefts(a + i), axis=0) for i in range(2)], axis=1
                ),
                (((1,), (1,)), ((), ())),
                preferred_element_type=F32,
            )
        return total

    paired = product(0) + product(8)
    cross = product(16)
    for third in range(3):
        lanes = slice(third * 128, third * 128 + 128)
        paired_ref[third] = paired[:, lanes] + cross if third == 0 else paired[:, lanes]

    slot_label = jnp.concatenate(
        [
            sum(ref[n + tile].astype(F32)[0:1] for ref, n in zip(arrays, TILES))
            for tile in range(3)
        ],
        axis=1,
    )
    row = iota((128, 128), 0)
    j = (row % 16) * 8 + (row // 16 % 2) * 4 + row // 32
    labels = right_table[pl.ds(place_ref[3], 1), :].astype(F32)
    right_label = jnp.sum(jnp.where(iota((128, 128), 1) == j, labels, 0.0), axis=1, keepdims=True)
    match = right_label == slot_label

    def part(c):
        rows = [
            jnp.concatenate(
                [paired_ref[third, pl.ds(c * 8 + w * 4 + j, 16, 16), :] for third in range(3)],
                axis=1,
            )
            for j in range(4)
            for w in range(2)
        ]
        return jnp.where(match, jnp.concatenate(rows, axis=0), 0.0)

    rest = jnp.concatenate([part(0), part(1)], axis=1)
    total = jnp.zeros((128, 384), F32)
    for _ in range(3):
        piece = rest.astype(BF)
        total += jnp.dot(piece, picks[...], preferred_element_type=F32)
        rest = rest - piece.astype(F32)
    for j in range(4):
        for row in range(8):
            out[row, :, j * 48 : j * 48 + 48] = total[j * 32 : j * 32 + 32, row * 48 : row * 48 + 48]


def contract(place, tiles, right, right_table, picks):
    whole = pl.BlockSpec(memory_space=pltpu.VMEM)
    return pl.pallas_call(
        contract_kernel,
        in_specs=[pl.BlockSpec(memory_space=pltpu.SMEM)] + [whole] * 8,
        out_specs=whole,
        out_shape=jax.ShapeDtypeStruct((8, 32, 192), F32),
        scratch_shapes=[pltpu.VMEM((3, 256, 128), F32)],
        compiler_params=params(16),
        name="contract",
    )(place, *tiles, right, right_table, picks)


def ring(step):
    pairs = []
    for z in range(8):
        for core in range(2):
            place = lambda z: ((z % 4) * 2 + core) * 2 + z // 4
            pairs.append((place(z), place(step(z))))
    return pairs


def local(
    wave_blocks, left_operators, right_operators, left_table, right_table, assignment, kramers_map
):
    line = ("row", "wf")
    row, col, wf = lax.axis_index("row"), lax.axis_index("col"), lax.axis_index("wf")
    core, z_lo = row % 2, row // 2
    z = wf * 4 + z_lo
    q = 2 * col + core

    own_wave = jnp.concatenate(
        [lax.dynamic_slice_in_dim(wave_blocks, (q + o) % 32, 1, 1) for o in range(3)], axis=1
    )
    far_wave = lax.ppermute(
        own_wave, line, ring(lambda z: (z + 2) % 8 if z in (2, 3, 6, 7) else (z - 2) % 8)
    )
    swap = [(i, i ^ 1) for i in range(8)]
    far_left = lax.ppermute(left_operators, "row", swap)
    far_table = lax.ppermute(left_table, "row", swap)
    place = jnp.stack([core, z_lo, z, q]).astype(jnp.int32)
    right = pick_right(place, right_operators)
    right = lax.all_to_all(right, "col", 0, 0, tiled=True)
    home, up1, down1, up2, down2 = make_tiles(
        place, left_table, far_table, own_wave, far_wave, left_operators, far_left
    )
    assignment, kramers_map, home = lax.optimization_barrier((assignment, kramers_map, home))
    tiles = [
        home,
        lax.ppermute(up1, line, ring(lambda z: (z + 1) % 8)),
        lax.ppermute(down1, line, ring(lambda z: (z + 7) % 8)),
        lax.ppermute(up2, line, ring(lambda z: (z + 2) % 8)),
        lax.ppermute(down2, line, ring(lambda z: (z + 6) % 8)),
    ]

    held = assignment.reshape(4, 2, 12)
    held = jnp.where(core == 0, held, held[:, ::-1])
    held = lax.dynamic_slice_in_dim(jnp.concatenate([held, held], axis=0), z_lo, 4, 0)
    held = jnp.concatenate([held[0:1], held[3:4], held[1:3]], axis=0).reshape(96, 1)
    slot_key = (held * 4 + jnp.arange(4, dtype=jnp.int32)[None, :]).reshape(384, 1)
    target = jnp.stack([jnp.arange(96, dtype=jnp.int32), kramers_map]).reshape(1, 2, 8, 12)
    target = target.transpose(2, 0, 1, 3)
    kind = jnp.arange(2, dtype=jnp.int32)[None, None, :, None]
    part = jnp.arange(2, dtype=jnp.int32)[None, :, None, None]
    real_key = (target * 4 + kind * 2 + part).reshape(1, 384)
    imag_key = (target * 4 + kind * 2 + 1 - part).reshape(1, 384)
    sign = jnp.broadcast_to((2 * part - 1).astype(F32), (8, 2, 2, 12)).reshape(1, 384)

    picks = make_picks([slot_key, real_key, imag_key, sign])
    shares = contract(place, tiles, right, right_table.T, picks)
    shares = lax.all_to_all(
        shares.reshape(256, 192), ("row", "wf", "col"), 0, 0, tiled=True
    )
    return jnp.sum(shares, axis=0).reshape(4, 2, 2, 12).transpose(1, 2, 3, 0)


def solution(mesh):
    return jax.shard_map(
        local,
        mesh=mesh,
        in_specs=(
            P(None, None, "wf", None),
            P("row", "col", None, None, None),
            P(None, "col", None, "wf", None),
            P("row", None),
            P(),
            P(),
            P(),
        ),
        out_specs=P(None, None, "row", ("col", "wf")),
        check_vma=False,
    )
```

```python
import functools

import jax
import jax.numpy as jnp
from jax import lax
from jax.experimental import pallas as pl
from jax.experimental.pallas import tpu as pltpu
from jax.sharding import PartitionSpec as P

BF = jnp.bfloat16
F32 = jnp.float32


def iota(shape, axis):
    return lax.broadcasted_iota(jnp.int32, shape, axis)


def params(mebibytes):
    return pltpu.CompilerParams(vmem_limit_bytes=mebibytes * 1024 * 1024)


def pick_right_kernel(place_ref, right_ref, out_ref, rows_ref, sem):
    copies = []
    for part in range(4):
        for second in range(2):
            copy = pltpu.make_async_copy(
                right_ref.at[pl.ds(part * 4, 4), place_ref[0], :, :, place_ref[1] ^ (2 * second)],
                rows_ref.at[second, pl.ds(part * 4, 4)],
                sem.at[part, second],
            )
            copy.start()
            copies.append(copy)
    for part in range(4):
        for second in range(2):
            copies[part * 2 + second].wait()
        for target in range(part * 4, part * 4 + 4):
            for second in range(2):
                rows = jnp.concatenate(
                    [rows_ref[second, target, j, c][None] for c in range(2) for j in range(8)],
                    axis=0,
                )
                rows = jnp.swapaxes(rows, 0, 1)
                if second:
                    out_ref[target, 16:24] = rows[8:16]
                else:
                    out_ref[target, 0:16] = rows


def pick_right(place, right_operators):
    return pl.pallas_call(
        pick_right_kernel,
        in_specs=[
            pl.BlockSpec(memory_space=pltpu.SMEM), pl.BlockSpec(memory_space=pltpu.HBM)
        ],
        out_specs=pl.BlockSpec(memory_space=pltpu.VMEM),
        out_shape=jax.ShapeDtypeStruct((16, 24, 16, 128), BF),
        scratch_shapes=[
            pltpu.VMEM((2, 16, 8, 2, 16, 128), BF),
            pltpu.SemaphoreType.DMA((4, 2)),
        ],
        compiler_params=params(54),
        name="pick_right",
    )(place, right_operators.reshape(16, 2, 8, 2, 4, 16, 128))


GROUPS = (6, 6, 6, 3, 3)
ROWS = (24, 16, 16, 8, 8)
STARTS = (0, 96, 192, 288, 336)
TILES = tuple(n * rows for n, rows in zip(GROUPS, ROWS))


def tiles_kernel(
    sent, place_ref, own_table, far_table, own_wave, far_wave, own_left, far_left, *refs
):
    outs, (sides, bras, kets) = refs[:-3], refs[-3:]
    z, q = place_ref[2], place_ref[3]
    low = z < 4

    def wave(c, o):
        mine, other = own_wave[c, o], far_wave[c, o]
        return jnp.concatenate(
            [jnp.where(low, mine, other), jnp.where(low, other, mine)], axis=0
        )

    for o in range(3):
        re, im = wave(0, o), wave(1, o)
        top = jnp.concatenate([re, im, re, im], axis=1)
        bottom = jnp.concatenate([-im, re, im, -re], axis=1)
        sides[o] = jnp.concatenate([top, bottom], axis=0)
        if o == 0:
            re_t, im_t = re.T, im.T
            bras[0] = jnp.concatenate([re_t, im_t], axis=1)
            bras[1] = jnp.concatenate([-im_t, re_t], axis=1)

    labels = [own_table[s, q] for s in range(12)] + [far_table[s, q] for s in range(12)]
    shifts = [lax.rem(label - q + 32, 32) for label in labels]
    for half in range(2):
        if sent:
            spots = [lax.rem(z + 1, 8), lax.rem(z + 7, 8), lax.rem(z + (6 if half else 2), 8)]
        else:
            spots = [z, z ^ 2]
        width = 16 * len(spots)
        left = jnp.concatenate(
            [
                bras[c, pl.ds(pl.multiple_of(spot * 16, 16), 16), :]
                for c in range(2)
                for spot in spots
            ],
            axis=0,
        )
        source = far_left if half else own_left
        for s in range(12):
            operator = jnp.concatenate([source[s, 0], source[s, 1]], axis=1)
            turned = jnp.dot(
                operator, sides[shifts[half * 12 + s]], preferred_element_type=F32
            ).astype(BF)
            kets[s] = jnp.concatenate(
                [
                    jnp.concatenate([turned[:, 0:128], turned[:, 256:384]], axis=1),
                    jnp.concatenate([turned[:, 128:256], turned[:, 384:512]], axis=1),
                ],
                axis=0,
            )
        for group in range(3):
            whole = half * 3 + group
            brackets = [
                jnp.dot(left, kets[group * 4 + s], preferred_element_type=F32).astype(BF)
                for s in range(4)
            ]
            for i in range(len(spots)):
                rows = jnp.concatenate(
                    [
                        brackets[s][
                            c * width + i * 16 : c * width + i * 16 + 16,
                            kind * 128 : kind * 128 + 128,
                        ][None]
                        for s in range(4)
                        for kind in range(2)
                        for c in range(2)
                    ],
                    axis=0,
                )
                rows = jnp.swapaxes(rows, 0, 1)
                if sent and i == 2:
                    outs[2 + half][group * 8 : group * 8 + 8] = rows[0:8]
                elif i == 1 and not sent:
                    outs[0][96 + whole * 8 : 96 + whole * 8 + 8] = rows[8:16]
                else:
                    outs[i][whole * 16 : whole * 16 + 16] = rows
    for out, spot in zip(outs, range(1, 5) if sent else range(1)):
        count = GROUPS[spot] * 4
        offset = 12 if spot == 4 else 0
        for tile in range(3):
            place = (iota((16, 128), 1) + tile * 128 - STARTS[spot]) // 4
            row = jnp.zeros((16, 128), F32)
            low_s, high_s = (tile * 128 - STARTS[spot]) // 4, (tile * 128 + 128 - STARTS[spot]) // 4
            for s in range(max(0, low_s), min(count, high_s)):
                row = jnp.where(place == s, labels[offset + s].astype(F32), row)
            out[TILES[spot] + tile] = row.astype(BF)


def make_tiles(sent, place, own_table, far_table, own_wave, far_wave, left_operators, far_left):
    full = lambda shape: pl.BlockSpec(shape, lambda i, place: (0,) * len(shape))
    table = pl.BlockSpec(memory_space=pltpu.SMEM)
    operators = pl.BlockSpec(
        (12, None, 2, 128, 128), lambda i, place: (0, place[0], 0, 0, 0)
    )
    shapes = [(n + 3, 16, 128) for n in (TILES[1:] if sent else TILES[:1])]
    return pl.pallas_call(
        functools.partial(tiles_kernel, sent),
        grid_spec=pltpu.PrefetchScalarGridSpec(
            num_scalar_prefetch=1,
            grid=(1,),
            in_specs=[
                table, table, full((2, 3, 64, 128)), full((2, 3, 64, 128)), operators, operators
            ],
            out_specs=[full(shape) for shape in shapes],
            scratch_shapes=[
                pltpu.VMEM((3, 256, 512), BF),
                pltpu.VMEM((2, 128, 256), BF),
                pltpu.VMEM((12, 256, 256), BF),
            ],
        ),
        out_shape=[jax.ShapeDtypeStruct(shape, BF) for shape in shapes],
        cost_estimate=pl.CostEstimate(
            flops=1000000000, bytes_accessed=4000000, transcendentals=0
        ),
        compiler_params=params(20),
        name="make_tiles" if sent else "make_home",
    )(place, own_table, far_table, own_wave, far_wave, left_operators, far_left)


def picks_kernel(slot_key, real_key, imag_key, sign, out):
    out[0:384] = (slot_key[...] == real_key[...]).astype(F32).astype(BF)
    out[384:768] = jnp.where(slot_key[...] == imag_key[...], sign[...], 0.0).astype(BF)


def make_picks(keys):
    return pl.pallas_call(
        picks_kernel,
        out_shape=jax.ShapeDtypeStruct((768, 384), BF),
        compiler_params=params(8),
        name="make_picks",
    )(*keys)


def contract_kernel(
    place_ref, home, up1, down1, up2, down2, right, right_table, picks, out, paired_ref
):
    arrays = (home, up1, down1, up2, down2)
    zero = jnp.zeros((96, 128), BF)

    def lefts(a):
        if a >= 16:
            return [home[96 + g * 8 + a - 16] for g in range(6)] + [zero[0:32]]
        tiles = [ref[g * 16 + a] for ref in arrays[0:3] for g in range(6)]
        if a >= 8:
            return tiles + [zero]
        return tiles + [ref[g * 8 + a] for ref in arrays[3:5] for g in range(3)]

    def product(start):
        total = 0.0
        for a in range(start, start + 8, 2):
            total += lax.dot_general(
                jnp.concatenate([right[:, a + i].reshape(256, 128) for i in range(2)], axis=1),
                jnp.concatenate(
                    [jnp.concatenate(lefts(a + i), axis=0) for i in range(2)], axis=1
                ),
                (((1,), (1,)), ((), ())),
                preferred_element_type=F32,
            )
        return total

    paired = product(0) + product(8)
    cross = product(16)
    for third in range(3):
        lanes = slice(third * 128, third * 128 + 128)
        paired_ref[third] = paired[:, lanes] + cross if third == 0 else paired[:, lanes]

    slot_label = jnp.concatenate(
        [
            sum(ref[n + tile].astype(F32)[0:1] for ref, n in zip(arrays, TILES))
            for tile in range(3)
        ],
        axis=1,
    )
    row = iota((128, 128), 0)
    j = (row % 16) * 8 + (row // 16 % 2) * 4 + row // 32
    labels = right_table[pl.ds(place_ref[3], 1), :].astype(F32)
    right_label = jnp.sum(jnp.where(iota((128, 128), 1) == j, labels, 0.0), axis=1, keepdims=True)
    match = right_label == slot_label

    def part(c):
        rows = [
            jnp.concatenate(
                [paired_ref[third, pl.ds(c * 8 + w * 4 + j, 16, 16), :] for third in range(3)],
                axis=1,
            )
            for j in range(4)
            for w in range(2)
        ]
        return jnp.where(match, jnp.concatenate(rows, axis=0), 0.0)

    rest = jnp.concatenate([part(0), part(1)], axis=1)
    pieces = []
    for _ in range(3):
        pieces.append(rest.astype(BF))
        rest = rest - pieces[-1].astype(F32)
    total = jnp.dot(jnp.concatenate(pieces, axis=0), picks[...], preferred_element_type=F32)
    total = total[0:128] + total[128:256] + total[256:384]
    for j in range(4):
        for row in range(8):
            out[row, :, j * 48 : j * 48 + 48] = total[j * 32 : j * 32 + 32, row * 48 : row * 48 + 48]


def contract(place, tiles, right, right_table, picks):
    whole = pl.BlockSpec(memory_space=pltpu.VMEM)
    return pl.pallas_call(
        contract_kernel,
        in_specs=[pl.BlockSpec(memory_space=pltpu.SMEM)] + [whole] * 8,
        out_specs=whole,
        out_shape=jax.ShapeDtypeStruct((8, 32, 192), F32),
        scratch_shapes=[pltpu.VMEM((3, 256, 128), F32)],
        compiler_params=params(16),
        name="contract",
    )(place, *tiles, right, right_table, picks)


def ring(step):
    pairs = []
    for z in range(8):
        for core in range(2):
            place = lambda z: ((z % 4) * 2 + core) * 2 + z // 4
            pairs.append((place(z), place(step(z))))
    return pairs


def local(
    wave_blocks, left_operators, right_operators, left_table, right_table, assignment, kramers_map
):
    line = ("row", "wf")
    row, col, wf = lax.axis_index("row"), lax.axis_index("col"), lax.axis_index("wf")
    core, z_lo = row % 2, row // 2
    z = wf * 4 + z_lo
    q = 2 * col + core

    own_wave = jnp.concatenate(
        [lax.dynamic_slice_in_dim(wave_blocks, (q + o) % 32, 1, 1) for o in range(3)], axis=1
    )
    far_wave = lax.ppermute(
        own_wave, line, ring(lambda z: (z + 2) % 8 if z in (2, 3, 6, 7) else (z - 2) % 8)
    )
    swap = [(i, i ^ 1) for i in range(8)]
    far_left = lax.ppermute(left_operators, "row", swap)
    far_table = lax.ppermute(left_table, "row", swap)
    place = jnp.stack([core, z_lo, z, q]).astype(jnp.int32)
    right = pick_right(place, right_operators)
    right = lax.all_to_all(right, "col", 0, 0, tiled=True)
    up1, down1, up2, down2 = make_tiles(
        True, place, left_table, far_table, own_wave, far_wave, left_operators, far_left
    )
    far_wave, assignment, kramers_map, up1 = lax.optimization_barrier(
        (far_wave, assignment, kramers_map, up1)
    )
    arrived = [
        lax.ppermute(up1, line, ring(lambda z: (z + 1) % 8)),
        lax.ppermute(down1, line, ring(lambda z: (z + 7) % 8)),
        lax.ppermute(up2, line, ring(lambda z: (z + 2) % 8)),
        lax.ppermute(down2, line, ring(lambda z: (z + 6) % 8)),
    ]
    (home,) = make_tiles(
        False, place, left_table, far_table, own_wave, far_wave, left_operators, far_left
    )
    tiles = [home] + arrived

    held = assignment.reshape(4, 2, 12)
    held = jnp.where(core == 0, held, held[:, ::-1])
    held = lax.dynamic_slice_in_dim(jnp.concatenate([held, held], axis=0), z_lo, 4, 0)
    held = jnp.concatenate([held[0:1], held[3:4], held[1:3]], axis=0).reshape(96, 1)
    slot_key = (held * 4 + jnp.arange(4, dtype=jnp.int32)[None, :]).reshape(384, 1)
    target = jnp.stack([jnp.arange(96, dtype=jnp.int32), kramers_map]).reshape(1, 2, 8, 12)
    target = target.transpose(2, 0, 1, 3)
    kind = jnp.arange(2, dtype=jnp.int32)[None, None, :, None]
    part = jnp.arange(2, dtype=jnp.int32)[None, :, None, None]
    real_key = (target * 4 + kind * 2 + part).reshape(1, 384)
    imag_key = (target * 4 + kind * 2 + 1 - part).reshape(1, 384)
    sign = jnp.broadcast_to((2 * part - 1).astype(F32), (8, 2, 2, 12)).reshape(1, 384)

    picks = make_picks([slot_key, real_key, imag_key, sign])
    shares = contract(place, tiles, right, right_table.T, picks)
    shares = lax.all_to_all(
        shares.reshape(256, 192), ("row", "wf", "col"), 0, 0, tiled=True
    )
    return jnp.sum(shares, axis=0).reshape(4, 2, 2, 12).transpose(1, 2, 3, 0)


def solution(mesh):
    return jax.shard_map(
        local,
        mesh=mesh,
        in_specs=(
            P(None, None, "wf", None),
            P("row", "col", None, None, None),
            P(None, "col", None, "wf", None),
            P("row", None),
            P(),
            P(),
            P(),
        ),
        out_specs=P(None, None, "row", ("col", "wf")),
        check_vma=False,
    )
```

```python
import functools

import jax
import jax.numpy as jnp
from jax import lax
from jax.experimental import pallas as pl
from jax.experimental.pallas import tpu as pltpu
from jax.sharding import PartitionSpec as P

BF = jnp.bfloat16
F32 = jnp.float32


def iota(shape, axis):
    return lax.broadcasted_iota(jnp.int32, shape, axis)


def where():
    row, col, wf = lax.axis_index("row"), lax.axis_index("col"), lax.axis_index("wf")
    return row & 1, row >> 1, wf * 4 + (row >> 1), 2 * col + (row & 1)


def params(mebibytes):
    return pltpu.CompilerParams(vmem_limit_bytes=mebibytes * 1024 * 1024)


def pick_right_kernel(right_ref, out_ref, rows_ref, sem):
    core, z_lo, _, _ = where()
    copies = []
    for part in range(4):
        for second in range(2):
            copy = pltpu.make_async_copy(
                right_ref.at[pl.ds(part * 4, 4), core, :, :, z_lo ^ (2 * second)],
                rows_ref.at[second, pl.ds(part * 4, 4)],
                sem.at[part, second],
            )
            copy.start()
            copies.append(copy)
    for part in range(4):
        for second in range(2):
            copies[part * 2 + second].wait()
        for target in range(part * 4, part * 4 + 4):
            for second in range(2):
                rows = jnp.concatenate(
                    [rows_ref[second, target, j, c][None] for c in range(2) for j in range(8)],
                    axis=0,
                )
                rows = jnp.swapaxes(rows, 0, 1)
                if second:
                    out_ref[target, 16:24] = rows[8:16]
                else:
                    out_ref[target, 0:16] = rows


def pick_right(right_operators):
    return pl.pallas_call(
        pick_right_kernel,
        in_specs=[pl.BlockSpec(memory_space=pltpu.HBM)],
        out_specs=pl.BlockSpec(memory_space=pltpu.VMEM),
        out_shape=jax.ShapeDtypeStruct((16, 24, 16, 128), BF),
        scratch_shapes=[
            pltpu.VMEM((2, 16, 8, 2, 16, 128), BF),
            pltpu.SemaphoreType.DMA((4, 2)),
        ],
        compiler_params=params(54),
        name="pick_right",
    )(right_operators.reshape(16, 2, 8, 2, 4, 16, 128))


GROUPS = (6, 6, 6, 3, 3)
ROWS = (24, 16, 16, 8, 8)
STARTS = (0, 96, 192, 288, 336)
TILES = tuple(n * rows for n, rows in zip(GROUPS, ROWS))


def tiles_kernel(
    sent, own_table_ref, far_table_ref, own_wave, far_wave, own_left, far_left, *refs
):
    outs, (sides, bras, kets, own_table, far_table, sem) = refs[:-6], refs[-6:]
    core, _, z, q = where()
    low = z < 4
    tables = [
        pltpu.make_async_copy(own_table_ref, own_table, sem.at[0]),
        pltpu.make_async_copy(far_table_ref, far_table, sem.at[1]),
    ]
    for table in tables:
        table.start()

    def wave(c, o):
        mine, other = own_wave[c, o], far_wave[c, o]
        return jnp.concatenate(
            [jnp.where(low, mine, other), jnp.where(low, other, mine)], axis=0
        )

    for o in range(3):
        re, im = wave(0, o), wave(1, o)
        top = jnp.concatenate([re, im, re, im], axis=1)
        bottom = jnp.concatenate([-im, re, im, -re], axis=1)
        sides[o] = jnp.concatenate([top, bottom], axis=0)
        if o == 0:
            re_t, im_t = re.T, im.T
            bras[0] = jnp.concatenate([re_t, im_t], axis=1)
            bras[1] = jnp.concatenate([-im_t, re_t], axis=1)

    for table in tables:
        table.wait()
    labels = [own_table[s, q] for s in range(12)] + [far_table[s, q] for s in range(12)]
    shifts = [lax.rem(label - q + 32, 32) for label in labels]
    for half in range(2):
        if sent:
            spots = [lax.rem(z + 1, 8), lax.rem(z + 7, 8), lax.rem(z + (6 if half else 2), 8)]
        else:
            spots = [z, z ^ 2]
        width = 16 * len(spots)
        left = jnp.concatenate(
            [
                bras[c, pl.ds(pl.multiple_of(spot * 16, 16), 16), :]
                for c in range(2)
                for spot in spots
            ],
            axis=0,
        )
        source = far_left if half else own_left
        for s in range(12):
            operator = jnp.concatenate([source[s, core, 0], source[s, core, 1]], axis=1)
            turned = jnp.dot(
                operator, sides[shifts[half * 12 + s]], preferred_element_type=F32
            ).astype(BF)
            kets[s] = jnp.concatenate(
                [
                    jnp.concatenate([turned[:, 0:128], turned[:, 256:384]], axis=1),
                    jnp.concatenate([turned[:, 128:256], turned[:, 384:512]], axis=1),
                ],
                axis=0,
            )
        for group in range(3):
            whole = half * 3 + group
            brackets = [
                jnp.dot(left, kets[group * 4 + s], preferred_element_type=F32).astype(BF)
                for s in range(4)
            ]
            for i in range(len(spots)):
                rows = jnp.concatenate(
                    [
                        brackets[s][
                            c * width + i * 16 : c * width + i * 16 + 16,
                            kind * 128 : kind * 128 + 128,
                        ][None]
                        for s in range(4)
                        for kind in range(2)
                        for c in range(2)
                    ],
                    axis=0,
                )
                rows = jnp.swapaxes(rows, 0, 1)
                if sent and i == 2:
                    outs[2 + half][group * 8 : group * 8 + 8] = rows[0:8]
                elif i == 1 and not sent:
                    outs[0][96 + whole * 8 : 96 + whole * 8 + 8] = rows[8:16]
                else:
                    outs[i][whole * 16 : whole * 16 + 16] = rows
    for out, spot in zip(outs, range(1, 5) if sent else range(1)):
        count = GROUPS[spot] * 4
        offset = 12 if spot == 4 else 0
        for tile in range(3):
            place = (iota((16, 128), 1) + tile * 128 - STARTS[spot]) // 4
            row = jnp.zeros((16, 128), F32)
            low_s, high_s = (tile * 128 - STARTS[spot]) // 4, (tile * 128 + 128 - STARTS[spot]) // 4
            for s in range(max(0, low_s), min(count, high_s)):
                row = jnp.where(place == s, labels[offset + s].astype(F32), row)
            out[TILES[spot] + tile] = row.astype(BF)


def make_tiles(sent, own_table, far_table, own_wave, far_wave, left_operators, far_left):
    anywhere, whole = pl.BlockSpec(memory_space=pl.ANY), pl.BlockSpec(memory_space=pltpu.VMEM)
    shapes = [(n + 3, 16, 128) for n in (TILES[1:] if sent else TILES[:1])]
    return pl.pallas_call(
        functools.partial(tiles_kernel, sent),
        in_specs=[anywhere] * 2 + [whole] * 4,
        out_specs=[whole] * len(shapes),
        out_shape=[jax.ShapeDtypeStruct(shape, BF) for shape in shapes],
        scratch_shapes=[
            pltpu.VMEM((3, 256, 512), BF),
            pltpu.VMEM((2, 128, 256), BF),
            pltpu.VMEM((12, 256, 256), BF),
            pltpu.SMEM((12, 32), jnp.int32),
            pltpu.SMEM((12, 32), jnp.int32),
            pltpu.SemaphoreType.DMA((2,)),
        ],
        cost_estimate=pl.CostEstimate(
            flops=1000000000, bytes_accessed=4000000, transcendentals=0
        ),
        compiler_params=params(20),
        name="make_tiles" if sent else "make_home",
    )(own_table, far_table, own_wave, far_wave, left_operators, far_left)


def picks_kernel(slot_key, real_key, imag_key, sign, out):
    out[0:384] = (slot_key[...] == real_key[...]).astype(F32).astype(BF)
    out[384:768] = jnp.where(slot_key[...] == imag_key[...], sign[...], 0.0).astype(BF)


def make_picks(keys):
    return pl.pallas_call(
        picks_kernel,
        out_shape=jax.ShapeDtypeStruct((768, 384), BF),
        compiler_params=params(8),
        name="make_picks",
    )(*keys)


def contract_kernel(
    home, up1, down1, up2, down2, right, right_table, picks, out, paired_ref
):
    arrays = (home, up1, down1, up2, down2)
    zero = jnp.zeros((96, 128), BF)

    def lefts(a):
        if a >= 16:
            return [home[96 + g * 8 + a - 16] for g in range(6)] + [zero[0:32]]
        tiles = [ref[g * 16 + a] for ref in arrays[0:3] for g in range(6)]
        if a >= 8:
            return tiles + [zero]
        return tiles + [ref[g * 8 + a] for ref in arrays[3:5] for g in range(3)]

    def product(start):
        total = 0.0
        for a in range(start, start + 8, 2):
            total += lax.dot_general(
                jnp.concatenate([right[:, a + i].reshape(256, 128) for i in range(2)], axis=1),
                jnp.concatenate(
                    [jnp.concatenate(lefts(a + i), axis=0) for i in range(2)], axis=1
                ),
                (((1,), (1,)), ((), ())),
                preferred_element_type=F32,
            )
        return total

    paired = product(0) + product(8)
    cross = product(16)
    for third in range(3):
        lanes = slice(third * 128, third * 128 + 128)
        paired_ref[third] = paired[:, lanes] + cross if third == 0 else paired[:, lanes]

    slot_label = jnp.concatenate(
        [
            sum(ref[n + tile].astype(F32)[0:1] for ref, n in zip(arrays, TILES))
            for tile in range(3)
        ],
        axis=1,
    )
    row = iota((128, 128), 0)
    j = (row % 16) * 8 + (row // 16 % 2) * 4 + row // 32
    labels = right_table[pl.ds(where()[3], 1), :].astype(F32)
    right_label = jnp.sum(jnp.where(iota((128, 128), 1) == j, labels, 0.0), axis=1, keepdims=True)
    match = right_label == slot_label

    def part(c):
        rows = [
            jnp.concatenate(
                [paired_ref[third, pl.ds(c * 8 + w * 4 + j, 16, 16), :] for third in range(3)],
                axis=1,
            )
            for j in range(4)
            for w in range(2)
        ]
        return jnp.where(match, jnp.concatenate(rows, axis=0), 0.0)

    rest = jnp.concatenate([part(0), part(1)], axis=1)
    pieces = []
    for _ in range(3):
        pieces.append(rest.astype(BF))
        rest = rest - pieces[-1].astype(F32)
    total = jnp.dot(jnp.concatenate(pieces, axis=0), picks[...], preferred_element_type=F32)
    total = total[0:128] + total[128:256] + total[256:384]
    for j in range(4):
        for row in range(8):
            out[row, :, j * 48 : j * 48 + 48] = total[j * 32 : j * 32 + 32, row * 48 : row * 48 + 48]


def contract(tiles, right, right_table, picks):
    whole = pl.BlockSpec(memory_space=pltpu.VMEM)
    return pl.pallas_call(
        contract_kernel,
        in_specs=[whole] * 8,
        out_specs=whole,
        out_shape=jax.ShapeDtypeStruct((8, 32, 192), F32),
        scratch_shapes=[pltpu.VMEM((3, 256, 128), F32)],
        compiler_params=params(16),
        name="contract",
    )(*tiles, right, right_table, picks)


def ring(step):
    pairs = []
    for z in range(8):
        for core in range(2):
            place = lambda z: ((z % 4) * 2 + core) * 2 + z // 4
            pairs.append((place(z), place(step(z))))
    return pairs


def local(
    wave_blocks, left_operators, right_operators, left_table, right_table, assignment, kramers_map
):
    line = ("row", "wf")
    core, z_lo, _, q = where()
    own_wave = jnp.concatenate(
        [lax.dynamic_slice_in_dim(wave_blocks, (q + o) % 32, 1, 1) for o in range(3)], axis=1
    )
    far_wave = lax.ppermute(
        own_wave, line, ring(lambda z: (z + 2) % 8 if z in (2, 3, 6, 7) else (z - 2) % 8)
    )
    swap = [(i, i ^ 1) for i in range(8)]
    far_left = lax.ppermute(left_operators, "row", swap)
    far_table = lax.ppermute(left_table, "row", swap)
    right = pick_right(right_operators)
    right = lax.all_to_all(right, "col", 0, 0, tiled=True)
    up1, down1, up2, down2 = make_tiles(
        True, left_table, far_table, own_wave, far_wave, left_operators, far_left
    )
    far_wave, assignment, kramers_map, up1 = lax.optimization_barrier(
        (far_wave, assignment, kramers_map, up1)
    )
    arrived = [
        lax.ppermute(up1, line, ring(lambda z: (z + 1) % 8)),
        lax.ppermute(down1, line, ring(lambda z: (z + 7) % 8)),
        lax.ppermute(up2, line, ring(lambda z: (z + 2) % 8)),
        lax.ppermute(down2, line, ring(lambda z: (z + 6) % 8)),
    ]
    (home,) = make_tiles(
        False, left_table, far_table, own_wave, far_wave, left_operators, far_left
    )
    tiles = [home] + arrived

    held = assignment.reshape(4, 2, 12)
    held = jnp.where(core == 0, held, held[:, ::-1])
    held = lax.dynamic_slice_in_dim(jnp.concatenate([held, held], axis=0), z_lo, 4, 0)
    held = jnp.concatenate([held[0:1], held[3:4], held[1:3]], axis=0).reshape(96, 1)
    slot_key = (held * 4 + jnp.arange(4, dtype=jnp.int32)[None, :]).reshape(384, 1)
    target = jnp.stack([jnp.arange(96, dtype=jnp.int32), kramers_map]).reshape(1, 2, 8, 12)
    target = target.transpose(2, 0, 1, 3)
    kind = jnp.arange(2, dtype=jnp.int32)[None, None, :, None]
    part = jnp.arange(2, dtype=jnp.int32)[None, :, None, None]
    real_key = (target * 4 + kind * 2 + part).reshape(1, 384)
    imag_key = (target * 4 + kind * 2 + 1 - part).reshape(1, 384)
    sign = jnp.broadcast_to((2 * part - 1).astype(F32), (8, 2, 2, 12)).reshape(1, 384)

    picks = make_picks([slot_key, real_key, imag_key, sign])
    shares = contract(tiles, right, right_table.T, picks)
    shares = lax.all_to_all(
        shares.reshape(256, 192), ("row", "wf", "col"), 0, 0, tiled=True
    )
    return jnp.sum(shares, axis=0).reshape(4, 2, 2, 12).transpose(1, 2, 3, 0)


def solution(mesh):
    return jax.shard_map(
        local,
        mesh=mesh,
        in_specs=(
            P(None, None, "wf", None),
            P("row", "col", None, None, None),
            P(None, "col", None, "wf", None),
            P("row", None),
            P(),
            P(),
            P(),
        ),
        out_specs=P(None, None, "row", ("col", "wf")),
        check_vma=False,
    )
```

```python
import functools

import jax
import jax.numpy as jnp
from jax import lax
from jax.experimental import pallas as pl
from jax.experimental.pallas import tpu as pltpu
from jax.sharding import PartitionSpec as P

BF = jnp.bfloat16
F32 = jnp.float32


def iota(shape, axis):
    return lax.broadcasted_iota(jnp.int32, shape, axis)


def where():
    row, col, wf = lax.axis_index("row"), lax.axis_index("col"), lax.axis_index("wf")
    return row & 1, row >> 1, wf * 4 + (row >> 1), 2 * col + (row & 1)


def params(mebibytes):
    return pltpu.CompilerParams(vmem_limit_bytes=mebibytes * 1024 * 1024)


def pick_right_kernel(right_ref, out_ref, rows_ref, sem):
    core, z_lo, _, _ = where()
    copies = []
    for part in range(4):
        for second in range(2):
            copy = pltpu.make_async_copy(
                right_ref.at[pl.ds(part * 4, 4), core, :, :, z_lo ^ (2 * second)],
                rows_ref.at[second, pl.ds(part * 4, 4)],
                sem.at[part, second],
            )
            copy.start()
            copies.append(copy)
    for part in range(4):
        for second in range(2):
            copies[part * 2 + second].wait()
        for target in range(part * 4, part * 4 + 4):
            for second in range(2):
                rows = jnp.concatenate(
                    [rows_ref[second, target, j, c][None] for c in range(2) for j in range(8)],
                    axis=0,
                )
                rows = jnp.swapaxes(rows, 0, 1)
                if second:
                    out_ref[target, 16:24] = rows[8:16]
                else:
                    out_ref[target, 0:16] = rows


def pick_right(right_operators):
    return pl.pallas_call(
        pick_right_kernel,
        in_specs=[pl.BlockSpec(memory_space=pltpu.HBM)],
        out_specs=pl.BlockSpec(memory_space=pltpu.VMEM),
        out_shape=jax.ShapeDtypeStruct((16, 24, 16, 128), BF),
        scratch_shapes=[
            pltpu.VMEM((2, 16, 8, 2, 16, 128), BF),
            pltpu.SemaphoreType.DMA((4, 2)),
        ],
        compiler_params=params(54),
        name="pick_right",
    )(right_operators.reshape(16, 2, 8, 2, 4, 16, 128))


GROUPS = (6, 6, 6, 3, 3)
ROWS = (24, 16, 16, 8, 8)
STARTS = (0, 96, 192, 288, 336)
TILES = tuple(n * rows for n, rows in zip(GROUPS, ROWS))


def tiles_kernel(
    sent, own_table_ref, far_table_ref, own_wave, far_wave, own_left, far_left, *refs
):
    count = 4 if sent else 1
    results, outs = refs[:count], refs[count : 2 * count] if sent else refs[:count]
    sides, bras, kets, operators, own_table, far_table, sem, out_sem = refs[-8:]
    core, _, z, q = where()
    low = z < 4
    copies = [
        pltpu.make_async_copy(own_table_ref, own_table, sem.at[0]),
        pltpu.make_async_copy(far_table_ref, far_table, sem.at[1]),
        pltpu.make_async_copy(own_left.at[:, core], operators.at[0], sem.at[2]),
        pltpu.make_async_copy(far_left.at[:, core], operators.at[1], sem.at[3]),
    ]
    for copy in copies:
        copy.start()

    def wave(c, o):
        mine, other = own_wave[c, o], far_wave[c, o]
        return jnp.concatenate(
            [jnp.where(low, mine, other), jnp.where(low, other, mine)], axis=0
        )

    for o in range(3):
        re, im = wave(0, o), wave(1, o)
        top = jnp.concatenate([re, im, re, im], axis=1)
        bottom = jnp.concatenate([-im, re, im, -re], axis=1)
        sides[o] = jnp.concatenate([top, bottom], axis=0)
        if o == 0:
            re_t, im_t = re.T, im.T
            bras[0] = jnp.concatenate([re_t, im_t], axis=1)
            bras[1] = jnp.concatenate([-im_t, re_t], axis=1)

    copies[0].wait()
    copies[1].wait()
    labels = [own_table[s, q] for s in range(12)] + [far_table[s, q] for s in range(12)]
    shifts = [lax.rem(label - q + 32, 32) for label in labels]
    for out, spot in zip(outs, range(1, 5) if sent else range(1)):
        members = GROUPS[spot] * 4
        offset = 12 if spot == 4 else 0
        for tile in range(3):
            place = (iota((16, 128), 1) + tile * 128 - STARTS[spot]) // 4
            row = jnp.zeros((16, 128), F32)
            low_s, high_s = (tile * 128 - STARTS[spot]) // 4, (tile * 128 + 128 - STARTS[spot]) // 4
            for s in range(max(0, low_s), min(members, high_s)):
                row = jnp.where(place == s, labels[offset + s].astype(F32), row)
            out[TILES[spot] + tile] = row.astype(BF)

    leaving = []
    for half in range(2):
        if sent:
            spots = [lax.rem(z + 1, 8), lax.rem(z + 7, 8), lax.rem(z + (6 if half else 2), 8)]
        else:
            spots = [z, z ^ 2]
        width = 16 * len(spots)
        left = jnp.concatenate(
            [
                bras[c, pl.ds(pl.multiple_of(spot * 16, 16), 16), :]
                for c in range(2)
                for spot in spots
            ],
            axis=0,
        )
        copies[2 + half].wait()
        for s in range(12):
            operator = jnp.concatenate(
                [operators[half, s, 0], operators[half, s, 1]], axis=1
            )
            turned = jnp.dot(
                operator, sides[shifts[half * 12 + s]], preferred_element_type=F32
            ).astype(BF)
            kets[s] = jnp.concatenate(
                [
                    jnp.concatenate([turned[:, 0:128], turned[:, 256:384]], axis=1),
                    jnp.concatenate([turned[:, 128:256], turned[:, 384:512]], axis=1),
                ],
                axis=0,
            )
        for group in range(3):
            whole = half * 3 + group
            brackets = [
                jnp.dot(left, kets[group * 4 + s], preferred_element_type=F32).astype(BF)
                for s in range(4)
            ]
            for i in range(len(spots)):
                rows = jnp.concatenate(
                    [
                        brackets[s][
                            c * width + i * 16 : c * width + i * 16 + 16,
                            kind * 128 : kind * 128 + 128,
                        ][None]
                        for s in range(4)
                        for kind in range(2)
                        for c in range(2)
                    ],
                    axis=0,
                )
                rows = jnp.swapaxes(rows, 0, 1)
                if sent and i == 2:
                    outs[2 + half][group * 8 : group * 8 + 8] = rows[0:8]
                elif i == 1 and not sent:
                    outs[0][96 + whole * 8 : 96 + whole * 8 + 8] = rows[8:16]
                else:
                    outs[i][whole * 16 : whole * 16 + 16] = rows
        if sent:
            part = slice(48, TILES[1] + 3) if half else slice(0, 48)
            for i, tiles in ((0, part), (1, part), (2 + half, slice(0, TILES[3] + 3))):
                size = tiles.stop - tiles.start
                copy = pltpu.make_async_copy(
                    outs[i].at[pl.ds(tiles.start, size)],
                    results[i].at[pl.ds(tiles.start, size)],
                    out_sem.at[half, min(i, 2)],
                )
                copy.start()
                leaving.append(copy)
    for copy in leaving:
        copy.wait()


def make_tiles(sent, own_table, far_table, own_wave, far_wave, left_operators, far_left):
    anywhere, whole = pl.BlockSpec(memory_space=pl.ANY), pl.BlockSpec(memory_space=pltpu.VMEM)
    shapes = [(n + 3, 16, 128) for n in (TILES[1:] if sent else TILES[:1])]
    return pl.pallas_call(
        functools.partial(tiles_kernel, sent),
        in_specs=[anywhere] * 2 + [whole] * 2 + [anywhere] * 2,
        out_specs=[anywhere if sent else whole] * len(shapes),
        out_shape=[jax.ShapeDtypeStruct(shape, BF) for shape in shapes],
        scratch_shapes=[pltpu.VMEM(shape, BF) for shape in shapes if sent]
        + [
            pltpu.VMEM((3, 256, 512), BF),
            pltpu.VMEM((2, 128, 256), BF),
            pltpu.VMEM((12, 256, 256), BF),
            pltpu.VMEM((2, 12, 2, 128, 128), BF),
            pltpu.SMEM((12, 32), jnp.int32),
            pltpu.SMEM((12, 32), jnp.int32),
            pltpu.SemaphoreType.DMA((4,)),
            pltpu.SemaphoreType.DMA((2, 3)),
        ],
        cost_estimate=pl.CostEstimate(
            flops=1000000000, bytes_accessed=4000000, transcendentals=0
        ),
        compiler_params=params(20),
        name="make_tiles" if sent else "make_home",
    )(own_table, far_table, own_wave, far_wave, left_operators, far_left)


def picks_kernel(slot_key, real_key, imag_key, sign, out):
    out[0:384] = (slot_key[...] == real_key[...]).astype(F32).astype(BF)
    out[384:768] = jnp.where(slot_key[...] == imag_key[...], sign[...], 0.0).astype(BF)


def make_picks(keys):
    return pl.pallas_call(
        picks_kernel,
        out_shape=jax.ShapeDtypeStruct((768, 384), BF),
        compiler_params=params(8),
        name="make_picks",
    )(*keys)


def contract_kernel(
    home, up1, down1, up2, down2, right, right_table, picks, out, paired_ref
):
    arrays = (home, up1, down1, up2, down2)
    zero = jnp.zeros((96, 128), BF)

    def lefts(a):
        if a >= 16:
            return [home[96 + g * 8 + a - 16] for g in range(6)] + [zero[0:32]]
        tiles = [ref[g * 16 + a] for ref in arrays[0:3] for g in range(6)]
        if a >= 8:
            return tiles + [zero]
        return tiles + [ref[g * 8 + a] for ref in arrays[3:5] for g in range(3)]

    def product(start):
        total = 0.0
        for a in range(start, start + 8, 2):
            total += lax.dot_general(
                jnp.concatenate([right[:, a + i].reshape(256, 128) for i in range(2)], axis=1),
                jnp.concatenate(
                    [jnp.concatenate(lefts(a + i), axis=0) for i in range(2)], axis=1
                ),
                (((1,), (1,)), ((), ())),
                preferred_element_type=F32,
            )
        return total

    paired = product(0) + product(8)
    cross = product(16)
    for third in range(3):
        lanes = slice(third * 128, third * 128 + 128)
        paired_ref[third] = paired[:, lanes] + cross if third == 0 else paired[:, lanes]

    slot_label = jnp.concatenate(
        [
            sum(ref[n + tile].astype(F32)[0:1] for ref, n in zip(arrays, TILES))
            for tile in range(3)
        ],
        axis=1,
    )
    row = iota((128, 128), 0)
    j = (row % 16) * 8 + (row // 16 % 2) * 4 + row // 32
    labels = right_table[pl.ds(where()[3], 1), :].astype(F32)
    right_label = jnp.sum(jnp.where(iota((128, 128), 1) == j, labels, 0.0), axis=1, keepdims=True)
    match = right_label == slot_label

    def part(c):
        rows = [
            jnp.concatenate(
                [paired_ref[third, pl.ds(c * 8 + w * 4 + j, 16, 16), :] for third in range(3)],
                axis=1,
            )
            for j in range(4)
            for w in range(2)
        ]
        return jnp.where(match, jnp.concatenate(rows, axis=0), 0.0)

    rest = jnp.concatenate([part(0), part(1)], axis=1)
    pieces = []
    for _ in range(3):
        pieces.append(rest.astype(BF))
        rest = rest - pieces[-1].astype(F32)
    total = jnp.dot(jnp.concatenate(pieces, axis=0), picks[...], preferred_element_type=F32)
    total = total[0:128] + total[128:256] + total[256:384]
    for j in range(4):
        for row in range(8):
            out[row, :, j * 48 : j * 48 + 48] = total[j * 32 : j * 32 + 32, row * 48 : row * 48 + 48]


def contract(tiles, right, right_table, picks):
    whole = pl.BlockSpec(memory_space=pltpu.VMEM)
    return pl.pallas_call(
        contract_kernel,
        in_specs=[whole] * 8,
        out_specs=whole,
        out_shape=jax.ShapeDtypeStruct((8, 32, 192), F32),
        scratch_shapes=[pltpu.VMEM((3, 256, 128), F32)],
        compiler_params=params(16),
        name="contract",
    )(*tiles, right, right_table, picks)


def ring(step):
    pairs = []
    for z in range(8):
        for core in range(2):
            place = lambda z: ((z % 4) * 2 + core) * 2 + z // 4
            pairs.append((place(z), place(step(z))))
    return pairs


def local(
    wave_blocks, left_operators, right_operators, left_table, right_table, assignment, kramers_map
):
    line = ("row", "wf")
    core, z_lo, _, q = where()
    own_wave = jnp.concatenate(
        [lax.dynamic_slice_in_dim(wave_blocks, (q + o) % 32, 1, 1) for o in range(3)], axis=1
    )
    far_wave = lax.ppermute(
        own_wave, line, ring(lambda z: (z + 2) % 8 if z in (2, 3, 6, 7) else (z - 2) % 8)
    )
    swap = [(i, i ^ 1) for i in range(8)]
    far_left = lax.ppermute(left_operators, "row", swap)
    far_table = lax.ppermute(left_table, "row", swap)
    right = pick_right(right_operators)
    right = lax.all_to_all(right, "col", 0, 0, tiled=True)
    up1, down1, up2, down2 = make_tiles(
        True, left_table, far_table, own_wave, far_wave, left_operators, far_left
    )
    far_wave, assignment, kramers_map, up1 = lax.optimization_barrier(
        (far_wave, assignment, kramers_map, up1)
    )
    arrived = [
        lax.ppermute(up1, line, ring(lambda z: (z + 1) % 8)),
        lax.ppermute(down1, line, ring(lambda z: (z + 7) % 8)),
        lax.ppermute(up2, line, ring(lambda z: (z + 2) % 8)),
        lax.ppermute(down2, line, ring(lambda z: (z + 6) % 8)),
    ]
    (home,) = make_tiles(
        False, left_table, far_table, own_wave, far_wave, left_operators, far_left
    )
    tiles = [home] + arrived

    held = assignment.reshape(4, 2, 12)
    held = jnp.where(core == 0, held, held[:, ::-1])
    held = lax.dynamic_slice_in_dim(jnp.concatenate([held, held], axis=0), z_lo, 4, 0)
    held = jnp.concatenate([held[0:1], held[3:4], held[1:3]], axis=0).reshape(96, 1)
    slot_key = (held * 4 + jnp.arange(4, dtype=jnp.int32)[None, :]).reshape(384, 1)
    target = jnp.stack([jnp.arange(96, dtype=jnp.int32), kramers_map]).reshape(1, 2, 8, 12)
    target = target.transpose(2, 0, 1, 3)
    kind = jnp.arange(2, dtype=jnp.int32)[None, None, :, None]
    part = jnp.arange(2, dtype=jnp.int32)[None, :, None, None]
    real_key = (target * 4 + kind * 2 + part).reshape(1, 384)
    imag_key = (target * 4 + kind * 2 + 1 - part).reshape(1, 384)
    sign = jnp.broadcast_to((2 * part - 1).astype(F32), (8, 2, 2, 12)).reshape(1, 384)

    picks = make_picks([slot_key, real_key, imag_key, sign])
    shares = contract(tiles, right, right_table.T, picks)
    shares = lax.all_to_all(
        shares.reshape(256, 192), ("row", "wf", "col"), 0, 0, tiled=True
    )
    return jnp.sum(shares, axis=0).reshape(4, 2, 2, 12).transpose(1, 2, 3, 0)


def solution(mesh):
    return jax.shard_map(
        local,
        mesh=mesh,
        in_specs=(
            P(None, None, "wf", None),
            P("row", "col", None, None, None),
            P(None, "col", None, "wf", None),
            P("row", None),
            P(),
            P(),
            P(),
        ),
        out_specs=P(None, None, "row", ("col", "wf")),
        check_vma=False,
    )
```

```python
import functools

import jax
import jax.numpy as jnp
from jax import lax
from jax.experimental import pallas as pl
from jax.experimental.pallas import tpu as pltpu
from jax.sharding import PartitionSpec as P

BF = jnp.bfloat16
F32 = jnp.float32


def iota(shape, axis):
    return lax.broadcasted_iota(jnp.int32, shape, axis)


def where():
    row, col, wf = lax.axis_index("row"), lax.axis_index("col"), lax.axis_index("wf")
    return row & 1, row >> 1, wf * 4 + (row >> 1), 2 * col + (row & 1)


def params(mebibytes):
    return pltpu.CompilerParams(vmem_limit_bytes=mebibytes * 1024 * 1024)


def pick_right_kernel(right_ref, out_ref, rows_ref, sem):
    core, z_lo, _, _ = where()
    copies = []
    for part in range(4):
        for second in range(2):
            copy = pltpu.make_async_copy(
                right_ref.at[pl.ds(part * 4, 4), core, :, :, z_lo ^ (2 * second)],
                rows_ref.at[second, pl.ds(part * 4, 4)],
                sem.at[part, second],
            )
            copy.start()
            copies.append(copy)
    for part in range(4):
        for second in range(2):
            copies[part * 2 + second].wait()
        for target in range(part * 4, part * 4 + 4):
            for second in range(2):
                rows = jnp.concatenate(
                    [
                        rows_ref[second, target, 4 * w + 2 * h + t, c][None]
                        for h in range(2)
                        for c in range(2)
                        for w in range(2)
                        for t in range(2)
                    ],
                    axis=0,
                )
                rows = jnp.swapaxes(rows, 0, 1)
                if second:
                    out_ref[target, 16:24] = rows[8:16]
                else:
                    out_ref[target, 0:16] = rows


def pick_right(right_operators):
    return pl.pallas_call(
        pick_right_kernel,
        in_specs=[pl.BlockSpec(memory_space=pltpu.HBM)],
        out_specs=pl.BlockSpec(memory_space=pltpu.VMEM),
        out_shape=jax.ShapeDtypeStruct((16, 24, 16, 128), BF),
        scratch_shapes=[
            pltpu.VMEM((2, 16, 8, 2, 16, 128), BF),
            pltpu.SemaphoreType.DMA((4, 2)),
        ],
        compiler_params=params(54),
        name="pick_right",
    )(right_operators.reshape(16, 2, 8, 2, 4, 16, 128))


GROUPS = (6, 6, 6, 3, 3)
ROWS = (24, 16, 16, 8, 8)
STARTS = (0, 96, 192, 288, 336)
TILES = tuple(n * rows for n, rows in zip(GROUPS, ROWS))


def tiles_kernel(
    sent, own_table_ref, far_table_ref, own_wave, far_wave, own_left, far_left, *refs
):
    count = 4 if sent else 1
    results, outs = refs[:count], refs[count : 2 * count] if sent else refs[:count]
    sides, bras, kets, operators, own_table, far_table, sem, out_sem = refs[-8:]
    core, _, z, q = where()
    low = z < 4
    copies = [
        pltpu.make_async_copy(own_table_ref, own_table, sem.at[0]),
        pltpu.make_async_copy(far_table_ref, far_table, sem.at[1]),
        pltpu.make_async_copy(own_left.at[:, core], operators.at[0], sem.at[2]),
        pltpu.make_async_copy(far_left.at[:, core], operators.at[1], sem.at[3]),
    ]
    for copy in copies:
        copy.start()

    def wave(c, o):
        mine, other = own_wave[c, o], far_wave[c, o]
        return jnp.concatenate(
            [jnp.where(low, mine, other), jnp.where(low, other, mine)], axis=0
        )

    for o in range(3):
        re, im = wave(0, o), wave(1, o)
        top = jnp.concatenate([re, im, re, im], axis=1)
        bottom = jnp.concatenate([-im, re, im, -re], axis=1)
        sides[o] = jnp.concatenate([top, bottom], axis=0)
        if o == 0:
            re_t, im_t = re.T, im.T
            bras[0] = jnp.concatenate([re_t, im_t], axis=1)
            bras[1] = jnp.concatenate([-im_t, re_t], axis=1)

    copies[0].wait()
    copies[1].wait()
    labels = [own_table[s, q] for s in range(12)] + [far_table[s, q] for s in range(12)]
    shifts = [lax.rem(label - q + 32, 32) for label in labels]
    for out, spot in zip(outs, range(1, 5) if sent else range(1)):
        members = GROUPS[spot] * 4
        offset = 12 if spot == 4 else 0
        for tile in range(3):
            place = (iota((16, 128), 1) + tile * 128 - STARTS[spot]) // 4
            row = jnp.zeros((16, 128), F32)
            low_s, high_s = (tile * 128 - STARTS[spot]) // 4, (tile * 128 + 128 - STARTS[spot]) // 4
            for s in range(max(0, low_s), min(members, high_s)):
                row = jnp.where(place == s, labels[offset + s].astype(F32), row)
            out[TILES[spot] + tile] = row.astype(BF)

    leaving = []
    for half in range(2):
        if sent:
            spots = [lax.rem(z + 1, 8), lax.rem(z + 7, 8), lax.rem(z + (6 if half else 2), 8)]
        else:
            spots = [z, z ^ 2]
        width = 16 * len(spots)
        left = jnp.concatenate(
            [
                bras[c, pl.ds(pl.multiple_of(spot * 16, 16), 16), :]
                for c in range(2)
                for spot in spots
            ],
            axis=0,
        )
        copies[2 + half].wait()
        for s in range(12):
            operator = jnp.concatenate(
                [operators[half, s, 0], operators[half, s, 1]], axis=1
            )
            turned = jnp.dot(
                operator, sides[shifts[half * 12 + s]], preferred_element_type=F32
            ).astype(BF)
            kets[s] = jnp.concatenate(
                [
                    jnp.concatenate([turned[:, 0:128], turned[:, 256:384]], axis=1),
                    jnp.concatenate([turned[:, 128:256], turned[:, 384:512]], axis=1),
                ],
                axis=0,
            )
        for group in range(3):
            whole = half * 3 + group
            brackets = [
                jnp.dot(left, kets[group * 4 + s], preferred_element_type=F32).astype(BF)
                for s in range(4)
            ]
            for i in range(len(spots)):
                rows = jnp.concatenate(
                    [
                        brackets[s][
                            c * width + i * 16 : c * width + i * 16 + 16,
                            kind * 128 : kind * 128 + 128,
                        ][None]
                        for s in range(4)
                        for kind in range(2)
                        for c in range(2)
                    ],
                    axis=0,
                )
                rows = jnp.swapaxes(rows, 0, 1)
                if sent and i == 2:
                    outs[2 + half][group * 8 : group * 8 + 8] = rows[0:8]
                elif i == 1 and not sent:
                    outs[0][96 + whole * 8 : 96 + whole * 8 + 8] = rows[8:16]
                else:
                    outs[i][whole * 16 : whole * 16 + 16] = rows
        if sent:
            part = slice(48, TILES[1] + 3) if half else slice(0, 48)
            for i, tiles in ((0, part), (1, part), (2 + half, slice(0, TILES[3] + 3))):
                size = tiles.stop - tiles.start
                copy = pltpu.make_async_copy(
                    outs[i].at[pl.ds(tiles.start, size)],
                    results[i].at[pl.ds(tiles.start, size)],
                    out_sem.at[half, min(i, 2)],
                )
                copy.start()
                leaving.append(copy)
    for copy in leaving:
        copy.wait()


def make_tiles(sent, own_table, far_table, own_wave, far_wave, left_operators, far_left):
    anywhere, whole = pl.BlockSpec(memory_space=pl.ANY), pl.BlockSpec(memory_space=pltpu.VMEM)
    shapes = [(n + 3, 16, 128) for n in (TILES[1:] if sent else TILES[:1])]
    return pl.pallas_call(
        functools.partial(tiles_kernel, sent),
        in_specs=[anywhere] * 2 + [whole] * 2 + [anywhere] * 2,
        out_specs=[anywhere if sent else whole] * len(shapes),
        out_shape=[jax.ShapeDtypeStruct(shape, BF) for shape in shapes],
        scratch_shapes=[pltpu.VMEM(shape, BF) for shape in shapes if sent]
        + [
            pltpu.VMEM((3, 256, 512), BF),
            pltpu.VMEM((2, 128, 256), BF),
            pltpu.VMEM((12, 256, 256), BF),
            pltpu.VMEM((2, 12, 2, 128, 128), BF),
            pltpu.SMEM((12, 32), jnp.int32),
            pltpu.SMEM((12, 32), jnp.int32),
            pltpu.SemaphoreType.DMA((4,)),
            pltpu.SemaphoreType.DMA((2, 3)),
        ],
        cost_estimate=pl.CostEstimate(
            flops=1000000000, bytes_accessed=4000000, transcendentals=0
        ),
        compiler_params=params(20),
        name="make_tiles" if sent else "make_home",
    )(own_table, far_table, own_wave, far_wave, left_operators, far_left)


def picks_kernel(slot_key, real_key, imag_key, sign, out):
    out[0:384] = (slot_key[...] == real_key[...]).astype(F32).astype(BF)
    out[384:768] = jnp.where(slot_key[...] == imag_key[...], sign[...], 0.0).astype(BF)


def make_picks(keys):
    return pl.pallas_call(
        picks_kernel,
        out_shape=jax.ShapeDtypeStruct((768, 384), BF),
        compiler_params=params(8),
        name="make_picks",
    )(*keys)


def contract_kernel(
    home, up1, down1, up2, down2, right, right_table, picks, out, paired_ref
):
    arrays = (home, up1, down1, up2, down2)
    zero = jnp.zeros((96, 128), BF)

    def lefts(a):
        if a >= 16:
            return [home[96 + g * 8 + a - 16] for g in range(6)] + [zero[0:32]]
        tiles = [ref[g * 16 + a] for ref in arrays[0:3] for g in range(6)]
        if a >= 8:
            return tiles + [zero]
        return tiles + [ref[g * 8 + a] for ref in arrays[3:5] for g in range(3)]

    def product(start):
        total = 0.0
        for a in range(start, start + 8, 2):
            total += lax.dot_general(
                jnp.concatenate([right[:, a + i].reshape(256, 128) for i in range(2)], axis=1),
                jnp.concatenate(
                    [jnp.concatenate(lefts(a + i), axis=0) for i in range(2)], axis=1
                ),
                (((1,), (1,)), ((), ())),
                preferred_element_type=F32,
            )
        return total

    paired = product(0) + product(8)
    cross = product(16)
    for third in range(3):
        lanes = slice(third * 128, third * 128 + 128)
        paired_ref[third] = paired[:, lanes] + cross if third == 0 else paired[:, lanes]

    slot_label = jnp.concatenate(
        [
            sum(ref[n + tile].astype(F32)[0:1] for ref, n in zip(arrays, TILES))
            for tile in range(3)
        ],
        axis=1,
    )
    row = iota((128, 128), 0)
    j = row % 32 // 2 * 8 + row // 32 % 2 * 4 + row % 2 * 2 + row // 64
    labels = right_table[pl.ds(where()[3], 1), :].astype(F32)
    right_label = jnp.sum(jnp.where(iota((128, 128), 1) == j, labels, 0.0), axis=1, keepdims=True)
    match = right_label == slot_label

    def part(c):
        rows = [
            jnp.concatenate(
                [paired_ref[third, pl.ds(c * 4 + w * 2 + t, 32, 8), :] for third in range(3)],
                axis=1,
            )
            for t in range(2)
            for w in range(2)
        ]
        return jnp.where(match, jnp.concatenate(rows, axis=0), 0.0)

    rest = jnp.concatenate([part(0), part(1)], axis=1)
    pieces = []
    for _ in range(3):
        pieces.append(rest.astype(BF))
        rest = rest - pieces[-1].astype(F32)
    total = jnp.dot(jnp.concatenate(pieces, axis=0), picks[...], preferred_element_type=F32)
    total = total[0:128] + total[128:256] + total[256:384]
    total = total.astype(out.dtype)
    out[...] = jnp.zeros(out.shape, out.dtype)
    for t in range(2):
        for row in range(8):
            out[row, :, t * 48 : t * 48 + 48] = total[
                t * 64 : t * 64 + 64, row * 48 : row * 48 + 48
            ]


def contract(tiles, right, right_table, picks):
    whole = pl.BlockSpec(memory_space=pltpu.VMEM)
    return pl.pallas_call(
        contract_kernel,
        in_specs=[whole] * 8,
        out_specs=whole,
        out_shape=jax.ShapeDtypeStruct((8, 64, 128), BF),
        scratch_shapes=[pltpu.VMEM((3, 256, 128), F32)],
        compiler_params=params(16),
        name="contract",
    )(*tiles, right, right_table, picks)


def ring(step):
    pairs = []
    for z in range(8):
        for core in range(2):
            place = lambda z: ((z % 4) * 2 + core) * 2 + z // 4
            pairs.append((place(z), place(step(z))))
    return pairs


def local(
    wave_blocks, left_operators, right_operators, left_table, right_table, assignment, kramers_map
):
    line = ("row", "wf")
    core, z_lo, _, q = where()
    own_wave = jnp.concatenate(
        [lax.dynamic_slice_in_dim(wave_blocks, (q + o) % 32, 1, 1) for o in range(3)], axis=1
    )
    far_wave = lax.ppermute(
        own_wave, line, ring(lambda z: (z + 2) % 8 if z in (2, 3, 6, 7) else (z - 2) % 8)
    )
    swap = [(i, i ^ 1) for i in range(8)]
    far_left = lax.ppermute(left_operators, "row", swap)
    far_table = lax.ppermute(left_table, "row", swap)
    right = pick_right(right_operators)
    right = lax.all_to_all(right, "col", 0, 0, tiled=True)
    up1, down1, up2, down2 = make_tiles(
        True, left_table, far_table, own_wave, far_wave, left_operators, far_left
    )
    far_wave, assignment, kramers_map, up1 = lax.optimization_barrier(
        (far_wave, assignment, kramers_map, up1)
    )
    arrived = [
        lax.ppermute(up1, line, ring(lambda z: (z + 1) % 8)),
        lax.ppermute(down1, line, ring(lambda z: (z + 7) % 8)),
        lax.ppermute(up2, line, ring(lambda z: (z + 2) % 8)),
        lax.ppermute(down2, line, ring(lambda z: (z + 6) % 8)),
    ]
    (home,) = make_tiles(
        False, left_table, far_table, own_wave, far_wave, left_operators, far_left
    )
    tiles = [home] + arrived

    held = assignment.reshape(4, 2, 12)
    held = jnp.where(core == 0, held, held[:, ::-1])
    held = lax.dynamic_slice_in_dim(jnp.concatenate([held, held], axis=0), z_lo, 4, 0)
    held = jnp.concatenate([held[0:1], held[3:4], held[1:3]], axis=0).reshape(96, 1)
    slot_key = (held * 4 + jnp.arange(4, dtype=jnp.int32)[None, :]).reshape(384, 1)
    target = jnp.stack([jnp.arange(96, dtype=jnp.int32), kramers_map]).reshape(1, 2, 8, 12)
    target = target.transpose(2, 0, 1, 3)
    kind = jnp.arange(2, dtype=jnp.int32)[None, None, :, None]
    part = jnp.arange(2, dtype=jnp.int32)[None, :, None, None]
    real_key = (target * 4 + kind * 2 + part).reshape(1, 384)
    imag_key = (target * 4 + kind * 2 + 1 - part).reshape(1, 384)
    sign = jnp.broadcast_to((2 * part - 1).astype(F32), (8, 2, 2, 12)).reshape(1, 384)

    picks = make_picks([slot_key, real_key, imag_key, sign])
    shares = contract(tiles, right, right_table.T, picks)
    shares = lax.all_to_all(
        shares.reshape(256, 2, 128), ("row", "wf", "col"), 0, 0, tiled=True
    )
    total = jnp.sum(shares.astype(F32), axis=0)[:, 0:96]
    return total.reshape(2, 2, 2, 2, 12).transpose(2, 3, 4, 0, 1).reshape(2, 2, 12, 4)


def solution(mesh):
    return jax.shard_map(
        local,
        mesh=mesh,
        in_specs=(
            P(None, None, "wf", None),
            P("row", "col", None, None, None),
            P(None, "col", None, "wf", None),
            P("row", None),
            P(),
            P(),
            P(),
        ),
        out_specs=P(None, None, "row", ("col", "wf")),
        check_vma=False,
    )
```

```python
import functools

import jax
import jax.numpy as jnp
from jax import lax
from jax.experimental import pallas as pl
from jax.experimental.pallas import tpu as pltpu
from jax.sharding import PartitionSpec as P

BF = jnp.bfloat16
F32 = jnp.float32


def iota(shape, axis):
    return lax.broadcasted_iota(jnp.int32, shape, axis)


def where():
    row, col, wf = lax.axis_index("row"), lax.axis_index("col"), lax.axis_index("wf")
    return row & 1, row >> 1, wf * 4 + (row >> 1), 2 * col + (row & 1)


def params(mebibytes):
    return pltpu.CompilerParams(vmem_limit_bytes=mebibytes * 1024 * 1024)


def pick_right_kernel(right_ref, out_ref, rows_ref, sem):
    core, z_lo, _, _ = where()
    copies = []
    for part in range(4):
        for second in range(2):
            copy = pltpu.make_async_copy(
                right_ref.at[pl.ds(part * 4, 4), core, :, :, z_lo ^ (2 * second)],
                rows_ref.at[second, pl.ds(part * 4, 4)],
                sem.at[part, second],
            )
            copy.start()
            copies.append(copy)
    for part in range(4):
        for second in range(2):
            copies[part * 2 + second].wait()
        for target in range(part * 4, part * 4 + 4):
            for second in range(2):
                rows = jnp.concatenate(
                    [
                        rows_ref[second, target, 4 * w + 2 * h + t, c][None]
                        for h in range(2)
                        for c in range(2)
                        for w in range(2)
                        for t in range(2)
                    ],
                    axis=0,
                )
                rows = jnp.swapaxes(rows, 0, 1)
                if second:
                    out_ref[target, 16:24] = rows[8:16]
                else:
                    out_ref[target, 0:16] = rows


def pick_right(right_operators):
    return pl.pallas_call(
        pick_right_kernel,
        in_specs=[pl.BlockSpec(memory_space=pltpu.HBM)],
        out_specs=pl.BlockSpec(memory_space=pltpu.VMEM),
        out_shape=jax.ShapeDtypeStruct((16, 24, 16, 128), BF),
        scratch_shapes=[
            pltpu.VMEM((2, 16, 8, 2, 16, 128), BF),
            pltpu.SemaphoreType.DMA((4, 2)),
        ],
        compiler_params=params(54),
        name="pick_right",
    )(right_operators.reshape(16, 2, 8, 2, 4, 16, 128))


GROUPS = (6, 6, 6, 3, 3)
ROWS = (24, 16, 16, 8, 8)
STARTS = (0, 96, 192, 288, 336)
TILES = tuple(n * rows for n, rows in zip(GROUPS, ROWS))


def tiles_kernel(
    sent, own_table_ref, far_table_ref, own_wave, far_wave, own_left, far_left, *refs
):
    count = 4 if sent else 1
    results, outs = refs[:count], refs[count : 2 * count] if sent else refs[:count]
    sides, bras, kets, operators, own_table, far_table, sem, out_sem = refs[-8:]
    core, _, z, q = where()
    ahead = 1 - 2 * core
    low = z < 4
    copies = [
        pltpu.make_async_copy(own_table_ref, own_table, sem.at[0]),
        pltpu.make_async_copy(far_table_ref, far_table, sem.at[1]),
        pltpu.make_async_copy(own_left.at[:, core], operators.at[0], sem.at[2]),
        pltpu.make_async_copy(far_left.at[:, core], operators.at[1], sem.at[3]),
    ]
    for copy in copies:
        copy.start()

    def wave(c, o):
        mine, other = own_wave[c, o], far_wave[c, o]
        return jnp.concatenate(
            [jnp.where(low, mine, other), jnp.where(low, other, mine)], axis=0
        )

    for o in range(3):
        re, im = wave(0, o), wave(1, o)
        top = jnp.concatenate([re, im, re, im], axis=1)
        bottom = jnp.concatenate([-im, re, im, -re], axis=1)
        sides[o] = jnp.concatenate([top, bottom], axis=0)
        if o == 0:
            re_t, im_t = re.T, im.T
            bras[0] = jnp.concatenate([re_t, im_t], axis=1)
            bras[1] = jnp.concatenate([-im_t, re_t], axis=1)

    copies[0].wait()
    copies[1].wait()
    labels = [own_table[s, q] for s in range(12)] + [far_table[s, q] for s in range(12)]
    shifts = [lax.rem(label - q + 32, 32) for label in labels]
    for out, spot in zip(outs, range(1, 5) if sent else range(1)):
        members = GROUPS[spot] * 4
        offset = 12 if spot == 4 else 0
        for tile in range(3):
            place = (iota((16, 128), 1) + tile * 128 - STARTS[spot]) // 4
            row = jnp.zeros((16, 128), F32)
            low_s, high_s = (tile * 128 - STARTS[spot]) // 4, (tile * 128 + 128 - STARTS[spot]) // 4
            for s in range(max(0, low_s), min(members, high_s)):
                row = jnp.where(place == s, labels[offset + s].astype(F32), row)
            out[TILES[spot] + tile] = row.astype(BF)

    leaving = []
    for half in range(2):
        if sent:
            spots = [(z + ahead) & 7, (z - ahead) & 7, (z - 2 * ahead if half else z + 2 * ahead) & 7]
        else:
            spots = [z, z ^ 2]
        width = 16 * len(spots)
        left = jnp.concatenate(
            [
                bras[c, pl.ds(pl.multiple_of(spot * 16, 16), 16), :]
                for c in range(2)
                for spot in spots
            ],
            axis=0,
        )
        copies[2 + half].wait()
        for s in range(12):
            operator = jnp.concatenate(
                [operators[half, s, 0], operators[half, s, 1]], axis=1
            )
            turned = jnp.dot(
                operator, sides[shifts[half * 12 + s]], preferred_element_type=F32
            ).astype(BF)
            kets[s] = jnp.concatenate(
                [
                    jnp.concatenate([turned[:, 0:128], turned[:, 256:384]], axis=1),
                    jnp.concatenate([turned[:, 128:256], turned[:, 384:512]], axis=1),
                ],
                axis=0,
            )
        for group in range(3):
            whole = half * 3 + group
            brackets = [
                jnp.dot(left, kets[group * 4 + s], preferred_element_type=F32).astype(BF)
                for s in range(4)
            ]
            for i in range(len(spots)):
                rows = jnp.concatenate(
                    [
                        brackets[s][
                            c * width + i * 16 : c * width + i * 16 + 16,
                            kind * 128 : kind * 128 + 128,
                        ][None]
                        for s in range(4)
                        for kind in range(2)
                        for c in range(2)
                    ],
                    axis=0,
                )
                rows = jnp.swapaxes(rows, 0, 1)
                if sent and i == 2:
                    outs[2 + half][group * 8 : group * 8 + 8] = rows[0:8]
                elif i == 1 and not sent:
                    outs[0][96 + whole * 8 : 96 + whole * 8 + 8] = rows[8:16]
                else:
                    outs[i][whole * 16 : whole * 16 + 16] = rows
        if sent:
            part = slice(48, TILES[1] + 3) if half else slice(0, 48)
            for i, tiles in ((0, part), (1, part), (2 + half, slice(0, TILES[3] + 3))):
                size = tiles.stop - tiles.start
                copy = pltpu.make_async_copy(
                    outs[i].at[pl.ds(tiles.start, size)],
                    results[i].at[pl.ds(tiles.start, size)],
                    out_sem.at[half, min(i, 2)],
                )
                copy.start()
                leaving.append(copy)
    for copy in leaving:
        copy.wait()


def make_tiles(sent, own_table, far_table, own_wave, far_wave, left_operators, far_left):
    anywhere, whole = pl.BlockSpec(memory_space=pl.ANY), pl.BlockSpec(memory_space=pltpu.VMEM)
    shapes = [(n + 3, 16, 128) for n in (TILES[1:] if sent else TILES[:1])]
    return pl.pallas_call(
        functools.partial(tiles_kernel, sent),
        in_specs=[anywhere] * 2 + [whole] * 2 + [anywhere] * 2,
        out_specs=[anywhere if sent else whole] * len(shapes),
        out_shape=[jax.ShapeDtypeStruct(shape, BF) for shape in shapes],
        scratch_shapes=[pltpu.VMEM(shape, BF) for shape in shapes if sent]
        + [
            pltpu.VMEM((3, 256, 512), BF),
            pltpu.VMEM((2, 128, 256), BF),
            pltpu.VMEM((12, 256, 256), BF),
            pltpu.VMEM((2, 12, 2, 128, 128), BF),
            pltpu.SMEM((12, 32), jnp.int32),
            pltpu.SMEM((12, 32), jnp.int32),
            pltpu.SemaphoreType.DMA((4,)),
            pltpu.SemaphoreType.DMA((2, 3)),
        ],
        cost_estimate=pl.CostEstimate(
            flops=1000000000, bytes_accessed=4000000, transcendentals=0
        ),
        compiler_params=params(20),
        name="make_tiles" if sent else "make_home",
    )(own_table, far_table, own_wave, far_wave, left_operators, far_left)


def picks_kernel(slot_key, real_key, imag_key, sign, out):
    out[0:384] = (slot_key[...] == real_key[...]).astype(F32).astype(BF)
    out[384:768] = jnp.where(slot_key[...] == imag_key[...], sign[...], 0.0).astype(BF)


def make_picks(keys):
    return pl.pallas_call(
        picks_kernel,
        out_shape=jax.ShapeDtypeStruct((768, 384), BF),
        compiler_params=params(8),
        name="make_picks",
    )(*keys)


def contract_kernel(
    home, ahead1, back1, ahead2, back2, right, right_table, picks, out, paired_ref
):
    arrays = (home, ahead1, back1, ahead2, back2)
    zero = jnp.zeros((96, 128), BF)

    def lefts(a):
        if a >= 16:
            return [home[96 + g * 8 + a - 16] for g in range(6)] + [zero[0:32]]
        tiles = [ref[g * 16 + a] for ref in arrays[0:3] for g in range(6)]
        if a >= 8:
            return tiles + [zero]
        return tiles + [ref[g * 8 + a] for ref in arrays[3:5] for g in range(3)]

    def product(start):
        total = 0.0
        for a in range(start, start + 8, 2):
            total += lax.dot_general(
                jnp.concatenate([right[:, a + i].reshape(256, 128) for i in range(2)], axis=1),
                jnp.concatenate(
                    [jnp.concatenate(lefts(a + i), axis=0) for i in range(2)], axis=1
                ),
                (((1,), (1,)), ((), ())),
                preferred_element_type=F32,
            )
        return total

    paired = product(0) + product(8)
    cross = product(16)
    for third in range(3):
        lanes = slice(third * 128, third * 128 + 128)
        paired_ref[third] = paired[:, lanes] + cross if third == 0 else paired[:, lanes]

    slot_label = jnp.concatenate(
        [
            sum(ref[n + tile].astype(F32)[0:1] for ref, n in zip(arrays, TILES))
            for tile in range(3)
        ],
        axis=1,
    )
    row = iota((128, 128), 0)
    j = row % 32 // 2 * 8 + row // 32 % 2 * 4 + row % 2 * 2 + row // 64
    labels = right_table[pl.ds(where()[3], 1), :].astype(F32)
    right_label = jnp.sum(jnp.where(iota((128, 128), 1) == j, labels, 0.0), axis=1, keepdims=True)
    match = right_label == slot_label

    def part(c):
        rows = [
            jnp.concatenate(
                [paired_ref[third, pl.ds(c * 4 + w * 2 + t, 32, 8), :] for third in range(3)],
                axis=1,
            )
            for t in range(2)
            for w in range(2)
        ]
        return jnp.where(match, jnp.concatenate(rows, axis=0), 0.0)

    rest = jnp.concatenate([part(0), part(1)], axis=1)
    pieces = []
    for _ in range(2):
        pieces.append(rest.astype(BF))
        rest = rest - pieces[-1].astype(F32)
    total = jnp.dot(jnp.concatenate(pieces, axis=0), picks[...], preferred_element_type=F32)
    total = total[0:128] + total[128:256]
    total = total.astype(out.dtype)
    out[...] = jnp.zeros(out.shape, out.dtype)
    for t in range(2):
        for row in range(8):
            out[row, :, t * 48 : t * 48 + 48] = total[
                t * 64 : t * 64 + 64, row * 48 : row * 48 + 48
            ]


def contract(tiles, right, right_table, picks):
    whole = pl.BlockSpec(memory_space=pltpu.VMEM)
    return pl.pallas_call(
        contract_kernel,
        in_specs=[whole] * 8,
        out_specs=whole,
        out_shape=jax.ShapeDtypeStruct((8, 64, 128), BF),
        scratch_shapes=[pltpu.VMEM((3, 256, 128), F32)],
        compiler_params=params(16),
        name="contract",
    )(*tiles, right, right_table, picks)


def ring(step):
    pairs = []
    for z in range(8):
        for core in range(2):
            place = lambda z: ((z % 4) * 2 + core) * 2 + z // 4
            pairs.append((place(z), place(step(z, core))))
    return pairs


def local(
    wave_blocks, left_operators, right_operators, left_table, right_table, assignment, kramers_map
):
    line = ("row", "wf")
    core, z_lo, _, q = where()
    own_wave = jnp.concatenate(
        [lax.dynamic_slice_in_dim(wave_blocks, (q + o) % 32, 1, 1) for o in range(3)], axis=1
    )
    far_wave = lax.ppermute(
        own_wave, line, ring(lambda z, core: (z + 2) % 8 if z in (2, 3, 6, 7) else (z - 2) % 8)
    )
    swap = [(i, i ^ 1) for i in range(8)]
    far_left = lax.ppermute(left_operators, "row", swap)
    far_table = lax.ppermute(left_table, "row", swap)
    right = pick_right(right_operators)
    right = lax.all_to_all(right, "col", 0, 0, tiled=True)
    ahead1, back1, ahead2, back2 = make_tiles(
        True, left_table, far_table, own_wave, far_wave, left_operators, far_left
    )
    far_wave, assignment, kramers_map, ahead1 = lax.optimization_barrier(
        (far_wave, assignment, kramers_map, ahead1)
    )
    ahead = lambda steps: ring(lambda z, core: (z + steps * (1 - 2 * core)) % 8)
    arrived = [
        lax.ppermute(ahead1, line, ahead(1)),
        lax.ppermute(back1, line, ahead(-1)),
        lax.ppermute(ahead2, line, ahead(2)),
        lax.ppermute(back2, line, ahead(-2)),
    ]
    (home,) = make_tiles(
        False, left_table, far_table, own_wave, far_wave, left_operators, far_left
    )
    tiles = [home] + arrived

    held = assignment.reshape(4, 2, 12)
    held = jnp.where(core == 0, held, held[:, ::-1])
    held = lax.dynamic_slice_in_dim(jnp.concatenate([held, held], axis=0), z_lo, 4, 0)
    turned = jnp.concatenate([held[0:1], held[3:4], held[1:3]], axis=0)
    straight = jnp.concatenate([held[0:2], held[3:4], held[2:3]], axis=0)
    held = jnp.where(core == 0, turned, straight).reshape(96, 1)
    slot_key = (held * 4 + jnp.arange(4, dtype=jnp.int32)[None, :]).reshape(384, 1)
    target = jnp.stack([jnp.arange(96, dtype=jnp.int32), kramers_map]).reshape(1, 2, 8, 12)
    target = target.transpose(2, 0, 1, 3)
    kind = jnp.arange(2, dtype=jnp.int32)[None, None, :, None]
    part = jnp.arange(2, dtype=jnp.int32)[None, :, None, None]
    real_key = (target * 4 + kind * 2 + part).reshape(1, 384)
    imag_key = (target * 4 + kind * 2 + 1 - part).reshape(1, 384)
    sign = jnp.broadcast_to((2 * part - 1).astype(F32), (8, 2, 2, 12)).reshape(1, 384)

    picks = make_picks([slot_key, real_key, imag_key, sign])
    shares = contract(tiles, right, right_table.T, picks)
    shares = lax.all_to_all(
        shares.reshape(256, 2, 128), ("row", "wf", "col"), 0, 0, tiled=True
    )
    total = jnp.sum(shares.astype(F32), axis=0)[:, 0:96]
    return total.reshape(2, 2, 2, 2, 12).transpose(2, 3, 4, 0, 1).reshape(2, 2, 12, 4)


def solution(mesh):
    return jax.shard_map(
        local,
        mesh=mesh,
        in_specs=(
            P(None, None, "wf", None),
            P("row", "col", None, None, None),
            P(None, "col", None, "wf", None),
            P("row", None),
            P(),
            P(),
            P(),
        ),
        out_specs=P(None, None, "row", ("col", "wf")),
        check_vma=False,
    )
```

```python
import functools

import jax
import jax.numpy as jnp
from jax import lax
from jax.experimental import pallas as pl
from jax.experimental.pallas import tpu as pltpu
from jax.sharding import PartitionSpec as P

BF = jnp.bfloat16
F32 = jnp.float32


def iota(shape, axis):
    return lax.broadcasted_iota(jnp.int32, shape, axis)


def where():
    row, col, wf = lax.axis_index("row"), lax.axis_index("col"), lax.axis_index("wf")
    return row & 1, row >> 1, wf * 4 + (row >> 1), 2 * col + (row & 1)


def params(mebibytes):
    return pltpu.CompilerParams(vmem_limit_bytes=mebibytes * 1024 * 1024)


def pick_kernel(right_ref, wave_ref, out_ref, wave_out, rows_ref, sem, wave_sem):
    core, z_lo, _, q = where()
    waves = [
        pltpu.make_async_copy(wave_ref.at[:, (q + o) & 31], wave_out.at[:, o], wave_sem.at[o])
        for o in range(3)
    ]
    for copy in waves:
        copy.start()
    copies = []
    for part in range(4):
        for second in range(2):
            copy = pltpu.make_async_copy(
                right_ref.at[pl.ds(part * 4, 4), core, :, :, z_lo ^ (2 * second)],
                rows_ref.at[second, pl.ds(part * 4, 4)],
                sem.at[part, second],
            )
            copy.start()
            copies.append(copy)
    for part in range(4):
        for second in range(2):
            copies[part * 2 + second].wait()
        for target in range(part * 4, part * 4 + 4):
            for second in range(2):
                rows = jnp.concatenate(
                    [
                        rows_ref[second, target, 4 * w + 2 * h + t, c][None]
                        for h in range(2)
                        for c in range(2)
                        for w in range(2)
                        for t in range(2)
                    ],
                    axis=0,
                )
                rows = jnp.swapaxes(rows, 0, 1)
                if second:
                    out_ref[target, 16:24] = rows[8:16]
                else:
                    out_ref[target, 0:16] = rows
    for copy in waves:
        copy.wait()


def pick(right_operators, wave_blocks):
    whole = pl.BlockSpec(memory_space=pltpu.VMEM)
    return pl.pallas_call(
        pick_kernel,
        in_specs=[pl.BlockSpec(memory_space=pltpu.HBM)] * 2,
        out_specs=[whole] * 2,
        out_shape=[
            jax.ShapeDtypeStruct((16, 24, 16, 128), BF),
            jax.ShapeDtypeStruct((2, 3, 64, 128), BF),
        ],
        scratch_shapes=[
            pltpu.VMEM((2, 16, 8, 2, 16, 128), BF),
            pltpu.SemaphoreType.DMA((4, 2)),
            pltpu.SemaphoreType.DMA((3,)),
        ],
        compiler_params=params(54),
        name="pick",
    )(right_operators.reshape(16, 2, 8, 2, 4, 16, 128), wave_blocks)


GROUPS = (6, 6, 6, 3, 3)
ROWS = (24, 16, 16, 8, 8)
STARTS = (0, 96, 192, 288, 336)
TILES = tuple(n * rows for n, rows in zip(GROUPS, ROWS))


def tiles_kernel(
    sent, own_table_ref, far_table_ref, own_wave, far_wave, own_left, far_left, *refs
):
    count = 4 if sent else 1
    results, outs = refs[:count], refs[count : 2 * count] if sent else refs[:count]
    sides, bras, kets, operators, own_table, far_table, sem, out_sem = refs[-8:]
    core, _, z, q = where()
    ahead = 1 - 2 * core
    low = z < 4
    copies = [
        pltpu.make_async_copy(own_table_ref, own_table, sem.at[0]),
        pltpu.make_async_copy(far_table_ref, far_table, sem.at[1]),
        pltpu.make_async_copy(own_left.at[:, core], operators.at[0], sem.at[2]),
        pltpu.make_async_copy(far_left.at[:, core], operators.at[1], sem.at[3]),
    ]
    for copy in copies:
        copy.start()

    def wave(c, o):
        mine, other = own_wave[c, o], far_wave[c, o]
        return jnp.concatenate(
            [jnp.where(low, mine, other), jnp.where(low, other, mine)], axis=0
        )

    for o in range(3):
        re, im = wave(0, o), wave(1, o)
        top = jnp.concatenate([re, im, re, im], axis=1)
        bottom = jnp.concatenate([-im, re, im, -re], axis=1)
        sides[o] = jnp.concatenate([top, bottom], axis=0)
        if o == 0:
            re_t, im_t = re.T, im.T
            bras[0] = jnp.concatenate([re_t, im_t], axis=1)
            bras[1] = jnp.concatenate([-im_t, re_t], axis=1)

    copies[0].wait()
    copies[1].wait()
    labels = [own_table[s, q] for s in range(12)] + [far_table[s, q] for s in range(12)]
    shifts = [lax.rem(label - q + 32, 32) for label in labels]
    for out, spot in zip(outs, range(1, 5) if sent else range(1)):
        members = GROUPS[spot] * 4
        offset = 12 if spot == 4 else 0
        for tile in range(3):
            place = (iota((16, 128), 1) + tile * 128 - STARTS[spot]) // 4
            row = jnp.zeros((16, 128), F32)
            low_s, high_s = (tile * 128 - STARTS[spot]) // 4, (tile * 128 + 128 - STARTS[spot]) // 4
            for s in range(max(0, low_s), min(members, high_s)):
                row = jnp.where(place == s, labels[offset + s].astype(F32), row)
            out[TILES[spot] + tile] = row.astype(BF)

    leaving = []
    for half in range(2):
        if sent:
            spots = [(z + ahead) & 7, (z - ahead) & 7, (z - 2 * ahead if half else z + 2 * ahead) & 7]
        else:
            spots = [z, z ^ 2]
        width = 16 * len(spots)
        left = jnp.concatenate(
            [
                bras[c, pl.ds(pl.multiple_of(spot * 16, 16), 16), :]
                for c in range(2)
                for spot in spots
            ],
            axis=0,
        )
        copies[2 + half].wait()
        for s in range(12):
            operator = jnp.concatenate(
                [operators[half, s, 0], operators[half, s, 1]], axis=1
            )
            turned = jnp.dot(
                operator, sides[shifts[half * 12 + s]], preferred_element_type=F32
            ).astype(BF)
            kets[s] = jnp.concatenate(
                [
                    jnp.concatenate([turned[:, 0:128], turned[:, 256:384]], axis=1),
                    jnp.concatenate([turned[:, 128:256], turned[:, 384:512]], axis=1),
                ],
                axis=0,
            )
        for group in range(3):
            whole = half * 3 + group
            brackets = [
                jnp.dot(left, kets[group * 4 + s], preferred_element_type=F32).astype(BF)
                for s in range(4)
            ]
            for i in range(len(spots)):
                rows = jnp.concatenate(
                    [
                        brackets[s][
                            c * width + i * 16 : c * width + i * 16 + 16,
                            kind * 128 : kind * 128 + 128,
                        ][None]
                        for s in range(4)
                        for kind in range(2)
                        for c in range(2)
                    ],
                    axis=0,
                )
                rows = jnp.swapaxes(rows, 0, 1)
                if sent and i == 2:
                    outs[2 + half][group * 8 : group * 8 + 8] = rows[0:8]
                elif i == 1 and not sent:
                    outs[0][96 + whole * 8 : 96 + whole * 8 + 8] = rows[8:16]
                else:
                    outs[i][whole * 16 : whole * 16 + 16] = rows
        if sent:
            part = slice(48, TILES[1] + 3) if half else slice(0, 48)
            for i, tiles in ((0, part), (1, part), (2 + half, slice(0, TILES[3] + 3))):
                size = tiles.stop - tiles.start
                copy = pltpu.make_async_copy(
                    outs[i].at[pl.ds(tiles.start, size)],
                    results[i].at[pl.ds(tiles.start, size)],
                    out_sem.at[half, min(i, 2)],
                )
                copy.start()
                leaving.append(copy)
    for copy in leaving:
        copy.wait()


def make_tiles(sent, own_table, far_table, own_wave, far_wave, left_operators, far_left):
    anywhere, whole = pl.BlockSpec(memory_space=pl.ANY), pl.BlockSpec(memory_space=pltpu.VMEM)
    shapes = [(n + 3, 16, 128) for n in (TILES[1:] if sent else TILES[:1])]
    return pl.pallas_call(
        functools.partial(tiles_kernel, sent),
        in_specs=[anywhere] * 2 + [whole] * 2 + [anywhere] * 2,
        out_specs=[anywhere if sent else whole] * len(shapes),
        out_shape=[jax.ShapeDtypeStruct(shape, BF) for shape in shapes],
        scratch_shapes=[pltpu.VMEM(shape, BF) for shape in shapes if sent]
        + [
            pltpu.VMEM((3, 256, 512), BF),
            pltpu.VMEM((2, 128, 256), BF),
            pltpu.VMEM((12, 256, 256), BF),
            pltpu.VMEM((2, 12, 2, 128, 128), BF),
            pltpu.SMEM((12, 32), jnp.int32),
            pltpu.SMEM((12, 32), jnp.int32),
            pltpu.SemaphoreType.DMA((4,)),
            pltpu.SemaphoreType.DMA((2, 3)),
        ],
        cost_estimate=pl.CostEstimate(
            flops=1000000000, bytes_accessed=4000000, transcendentals=0
        ),
        compiler_params=params(20),
        name="make_tiles" if sent else "make_home",
    )(own_table, far_table, own_wave, far_wave, left_operators, far_left)


def picks_kernel(slot_key, real_key, imag_key, sign, out):
    out[0:384] = (slot_key[...] == real_key[...]).astype(F32).astype(BF)
    out[384:768] = jnp.where(slot_key[...] == imag_key[...], sign[...], 0.0).astype(BF)


def make_picks(keys):
    return pl.pallas_call(
        picks_kernel,
        out_shape=jax.ShapeDtypeStruct((768, 384), BF),
        compiler_params=params(8),
        name="make_picks",
    )(*keys)


def contract_kernel(
    home, ahead1, back1, ahead2, back2, right, right_table, picks, out, paired_ref
):
    arrays = (home, ahead1, back1, ahead2, back2)
    zero = jnp.zeros((96, 128), BF)

    def lefts(a):
        if a >= 16:
            return [home[96 + g * 8 + a - 16] for g in range(6)] + [zero[0:32]]
        tiles = [ref[g * 16 + a] for ref in arrays[0:3] for g in range(6)]
        if a >= 8:
            return tiles + [zero]
        return tiles + [ref[g * 8 + a] for ref in arrays[3:5] for g in range(3)]

    def product(start):
        total = 0.0
        for a in range(start, start + 8, 2):
            total += lax.dot_general(
                jnp.concatenate([right[:, a + i].reshape(256, 128) for i in range(2)], axis=1),
                jnp.concatenate(
                    [jnp.concatenate(lefts(a + i), axis=0) for i in range(2)], axis=1
                ),
                (((1,), (1,)), ((), ())),
                preferred_element_type=F32,
            )
        return total

    paired = product(0) + product(8)
    cross = product(16)
    for third in range(3):
        lanes = slice(third * 128, third * 128 + 128)
        paired_ref[third] = paired[:, lanes] + cross if third == 0 else paired[:, lanes]

    slot_label = jnp.concatenate(
        [
            sum(ref[n + tile].astype(F32)[0:1] for ref, n in zip(arrays, TILES))
            for tile in range(3)
        ],
        axis=1,
    )
    row = iota((128, 128), 0)
    j = row % 32 // 2 * 8 + row // 32 % 2 * 4 + row % 2 * 2 + row // 64
    labels = right_table[pl.ds(where()[3], 1), :].astype(F32)
    right_label = jnp.sum(jnp.where(iota((128, 128), 1) == j, labels, 0.0), axis=1, keepdims=True)
    match = right_label == slot_label

    def part(c):
        rows = [
            jnp.concatenate(
                [paired_ref[third, pl.ds(c * 4 + w * 2 + t, 32, 8), :] for third in range(3)],
                axis=1,
            )
            for t in range(2)
            for w in range(2)
        ]
        return jnp.where(match, jnp.concatenate(rows, axis=0), 0.0)

    rest = jnp.concatenate([part(0), part(1)], axis=1)
    pieces = []
    for _ in range(2):
        pieces.append(rest.astype(BF))
        rest = rest - pieces[-1].astype(F32)
    total = jnp.dot(jnp.concatenate(pieces, axis=0), picks[...], preferred_element_type=F32)
    total = total[0:128] + total[128:256]
    total = total.astype(out.dtype)
    out[...] = jnp.zeros(out.shape, out.dtype)
    for t in range(2):
        for row in range(8):
            out[row, :, t * 48 : t * 48 + 48] = total[
                t * 64 : t * 64 + 64, row * 48 : row * 48 + 48
            ]


def contract(tiles, right, right_table, picks):
    whole = pl.BlockSpec(memory_space=pltpu.VMEM)
    return pl.pallas_call(
        contract_kernel,
        in_specs=[whole] * 8,
        out_specs=whole,
        out_shape=jax.ShapeDtypeStruct((8, 64, 128), BF),
        scratch_shapes=[pltpu.VMEM((3, 256, 128), F32)],
        compiler_params=params(16),
        name="contract",
    )(*tiles, right, right_table, picks)


def ring(step):
    pairs = []
    for z in range(8):
        for core in range(2):
            place = lambda z: ((z % 4) * 2 + core) * 2 + z // 4
            pairs.append((place(z), place(step(z, core))))
    return pairs


def local(
    wave_blocks, left_operators, right_operators, left_table, right_table, assignment, kramers_map
):
    line = ("row", "wf")
    core, z_lo, _, _ = where()
    right, own_wave = pick(right_operators, wave_blocks)
    far_wave = lax.ppermute(
        own_wave, line, ring(lambda z, core: (z + 2) % 8 if z in (2, 3, 6, 7) else (z - 2) % 8)
    )
    swap = [(i, i ^ 1) for i in range(8)]
    far_left = lax.ppermute(left_operators, "row", swap)
    far_table = lax.ppermute(left_table, "row", swap)
    right = lax.all_to_all(right, "col", 0, 0, tiled=True)
    ahead1, back1, ahead2, back2 = make_tiles(
        True, left_table, far_table, own_wave, far_wave, left_operators, far_left
    )
    far_wave, assignment, kramers_map, ahead1 = lax.optimization_barrier(
        (far_wave, assignment, kramers_map, ahead1)
    )
    ahead = lambda steps: ring(lambda z, core: (z + steps * (1 - 2 * core)) % 8)
    arrived = [
        lax.ppermute(ahead1, line, ahead(1)),
        lax.ppermute(back1, line, ahead(-1)),
        lax.ppermute(ahead2, line, ahead(2)),
        lax.ppermute(back2, line, ahead(-2)),
    ]
    (home,) = make_tiles(
        False, left_table, far_table, own_wave, far_wave, left_operators, far_left
    )
    tiles = [home] + arrived

    held = assignment.reshape(4, 2, 12)
    held = jnp.where(core == 0, held, held[:, ::-1])
    held = lax.dynamic_slice_in_dim(jnp.concatenate([held, held], axis=0), z_lo, 4, 0)
    turned = jnp.concatenate([held[0:1], held[3:4], held[1:3]], axis=0)
    straight = jnp.concatenate([held[0:2], held[3:4], held[2:3]], axis=0)
    held = jnp.where(core == 0, turned, straight).reshape(96, 1)
    slot_key = (held * 4 + jnp.arange(4, dtype=jnp.int32)[None, :]).reshape(384, 1)
    target = jnp.stack([jnp.arange(96, dtype=jnp.int32), kramers_map]).reshape(1, 2, 8, 12)
    target = target.transpose(2, 0, 1, 3)
    kind = jnp.arange(2, dtype=jnp.int32)[None, None, :, None]
    part = jnp.arange(2, dtype=jnp.int32)[None, :, None, None]
    real_key = (target * 4 + kind * 2 + part).reshape(1, 384)
    imag_key = (target * 4 + kind * 2 + 1 - part).reshape(1, 384)
    sign = jnp.broadcast_to((2 * part - 1).astype(F32), (8, 2, 2, 12)).reshape(1, 384)

    picks = make_picks([slot_key, real_key, imag_key, sign])
    shares = contract(tiles, right, right_table.T, picks)
    shares = lax.all_to_all(
        shares.reshape(256, 2, 128), ("row", "wf", "col"), 0, 0, tiled=True
    )
    total = jnp.sum(shares.astype(F32), axis=0)[:, 0:96]
    return total.reshape(2, 2, 2, 2, 12).transpose(2, 3, 4, 0, 1).reshape(2, 2, 12, 4)


def solution(mesh):
    return jax.shard_map(
        local,
        mesh=mesh,
        in_specs=(
            P(None, None, "wf", None),
            P("row", "col", None, None, None),
            P(None, "col", None, "wf", None),
            P("row", None),
            P(),
            P(),
            P(),
        ),
        out_specs=P(None, None, "row", ("col", "wf")),
        check_vma=False,
    )
```

```python
import functools

import jax
import jax.numpy as jnp
from jax import lax
from jax.experimental import pallas as pl
from jax.experimental.pallas import tpu as pltpu
from jax.sharding import PartitionSpec as P

BF = jnp.bfloat16
F32 = jnp.float32


def iota(shape, axis):
    return lax.broadcasted_iota(jnp.int32, shape, axis)


def where():
    row, col, wf = lax.axis_index("row"), lax.axis_index("col"), lax.axis_index("wf")
    return row & 1, row >> 1, wf * 4 + (row >> 1), 2 * col + (row & 1)


def params(mebibytes):
    return pltpu.CompilerParams(vmem_limit_bytes=mebibytes * 1024 * 1024)


def pick_kernel(right_ref, wave_ref, out_ref, wave_out, rows_ref, sem, wave_sem):
    core, z_lo, _, q = where()
    waves = [
        pltpu.make_async_copy(wave_ref.at[:, (q + o) & 31], wave_out.at[:, o], wave_sem.at[o])
        for o in range(3)
    ]
    for copy in waves:
        copy.start()
    copies = []
    for part in range(4):
        for second in range(2):
            copy = pltpu.make_async_copy(
                right_ref.at[pl.ds(part * 4, 4), core, :, :, z_lo ^ (2 * second)],
                rows_ref.at[second, pl.ds(part * 4, 4)],
                sem.at[part, second],
            )
            copy.start()
            copies.append(copy)
    for part in range(4):
        for second in range(2):
            copies[part * 2 + second].wait()
        for target in range(part * 4, part * 4 + 4):
            for second in range(2):
                rows = jnp.concatenate(
                    [
                        rows_ref[second, target, 4 * w + 2 * h + t, c][None]
                        for h in range(2)
                        for c in range(2)
                        for w in range(2)
                        for t in range(2)
                    ],
                    axis=0,
                )
                rows = jnp.swapaxes(rows, 0, 1)
                if second:
                    out_ref[target, 16:24] = rows[8:16]
                else:
                    out_ref[target, 0:16] = rows
    for copy in waves:
        copy.wait()


def pick(right_operators, wave_blocks):
    whole = pl.BlockSpec(memory_space=pltpu.VMEM)
    return pl.pallas_call(
        pick_kernel,
        in_specs=[pl.BlockSpec(memory_space=pltpu.HBM)] * 2,
        out_specs=[whole] * 2,
        out_shape=[
            jax.ShapeDtypeStruct((16, 24, 16, 128), BF),
            jax.ShapeDtypeStruct((2, 3, 64, 128), BF),
        ],
        scratch_shapes=[
            pltpu.VMEM((2, 16, 8, 2, 16, 128), BF),
            pltpu.SemaphoreType.DMA((4, 2)),
            pltpu.SemaphoreType.DMA((3,)),
        ],
        compiler_params=params(54),
        name="pick",
    )(right_operators.reshape(16, 2, 8, 2, 4, 16, 128), wave_blocks)


GROUPS = (6, 6, 6, 3, 3)
ROWS = (24, 16, 16, 8, 8)
STARTS = (0, 96, 192, 288, 336)
TILES = tuple(n * rows for n, rows in zip(GROUPS, ROWS))


def tiles_kernel(
    sent, own_table, far_table, own_wave, far_wave, own_left, far_left, *refs
):
    count = 4 if sent else 1
    results, outs = refs[:count], refs[count : 2 * count] if sent else refs[:count]
    sides, bras, kets, operators, sem, out_sem = refs[-6:]
    core, _, z, q = where()
    ahead = 1 - 2 * core
    low = z < 4
    copies = [
        pltpu.make_async_copy(own_left.at[:, core], operators.at[0], sem.at[0]),
        pltpu.make_async_copy(far_left.at[:, core], operators.at[1], sem.at[1]),
    ]
    for copy in copies:
        copy.start()

    def wave(c, o):
        mine, other = own_wave[c, o], far_wave[c, o]
        return jnp.concatenate(
            [jnp.where(low, mine, other), jnp.where(low, other, mine)], axis=0
        )

    for o in range(3):
        re, im = wave(0, o), wave(1, o)
        top = jnp.concatenate([re, im, re, im], axis=1)
        bottom = jnp.concatenate([-im, re, im, -re], axis=1)
        sides[o] = jnp.concatenate([top, bottom], axis=0)
        if o == 0:
            re_t, im_t = re.T, im.T
            bras[0] = jnp.concatenate([re_t, im_t], axis=1)
            bras[1] = jnp.concatenate([-im_t, re_t], axis=1)

    columns = [
        jnp.sum(jnp.where(iota((12, 32), 1) == q, table[...], 0), axis=1, keepdims=True)
        for table in (own_table, far_table)
    ]
    labels = [column[s, 0] for column in columns for s in range(12)]
    shifts = [lax.rem(label - q + 32, 32) for label in labels]
    for out, spot in zip(outs, range(1, 5) if sent else range(1)):
        members = GROUPS[spot] * 4
        offset = 12 if spot == 4 else 0
        for tile in range(3):
            place = (iota((16, 128), 1) + tile * 128 - STARTS[spot]) // 4
            row = jnp.zeros((16, 128), F32)
            low_s, high_s = (tile * 128 - STARTS[spot]) // 4, (tile * 128 + 128 - STARTS[spot]) // 4
            for s in range(max(0, low_s), min(members, high_s)):
                row = jnp.where(place == s, labels[offset + s].astype(F32), row)
            out[TILES[spot] + tile] = row.astype(BF)

    leaving = []
    for copy in copies:
        copy.wait()
    for half in range(2):
        if sent:
            spots = [(z + ahead) & 7, (z - ahead) & 7, (z - 2 * ahead if half else z + 2 * ahead) & 7]
        else:
            spots = [z, z ^ 2]
        width = 16 * len(spots)
        left = jnp.concatenate(
            [
                bras[c, pl.ds(pl.multiple_of(spot * 16, 16), 16), :]
                for c in range(2)
                for spot in spots
            ],
            axis=0,
        )
        for s in range(12):
            operator = jnp.concatenate(
                [operators[half, s, 0], operators[half, s, 1]], axis=1
            )
            turned = jnp.dot(
                operator, sides[shifts[half * 12 + s]], preferred_element_type=F32
            ).astype(BF)
            kets[half * 12 + s] = jnp.concatenate(
                [
                    jnp.concatenate([turned[:, 0:128], turned[:, 256:384]], axis=1),
                    jnp.concatenate([turned[:, 128:256], turned[:, 384:512]], axis=1),
                ],
                axis=0,
            )
        for group in range(3):
            whole = half * 3 + group
            brackets = [
                jnp.dot(left, kets[whole * 4 + s], preferred_element_type=F32).astype(BF)
                for s in range(4)
            ]
            for i in range(len(spots)):
                rows = jnp.concatenate(
                    [
                        brackets[s][
                            c * width + i * 16 : c * width + i * 16 + 16,
                            kind * 128 : kind * 128 + 128,
                        ][None]
                        for s in range(4)
                        for kind in range(2)
                        for c in range(2)
                    ],
                    axis=0,
                )
                rows = jnp.swapaxes(rows, 0, 1)
                if sent and i == 2:
                    outs[2 + half][group * 8 : group * 8 + 8] = rows[0:8]
                elif i == 1 and not sent:
                    outs[0][96 + whole * 8 : 96 + whole * 8 + 8] = rows[8:16]
                else:
                    outs[i][whole * 16 : whole * 16 + 16] = rows
        if sent:
            part = slice(48, TILES[1] + 3) if half else slice(0, 48)
            for i, tiles in ((0, part), (1, part), (2 + half, slice(0, TILES[3] + 3))):
                size = tiles.stop - tiles.start
                copy = pltpu.make_async_copy(
                    outs[i].at[pl.ds(tiles.start, size)],
                    results[i].at[pl.ds(tiles.start, size)],
                    out_sem.at[half, min(i, 2)],
                )
                copy.start()
                leaving.append(copy)
    for copy in leaving:
        copy.wait()


def make_tiles(sent, own_table, far_table, own_wave, far_wave, left_operators, far_left):
    anywhere, whole = pl.BlockSpec(memory_space=pl.ANY), pl.BlockSpec(memory_space=pltpu.VMEM)
    shapes = [(n + 3, 16, 128) for n in (TILES[1:] if sent else TILES[:1])]
    return pl.pallas_call(
        functools.partial(tiles_kernel, sent),
        in_specs=[whole] * 4 + [anywhere] * 2,
        out_specs=[anywhere if sent else whole] * len(shapes),
        out_shape=[jax.ShapeDtypeStruct(shape, BF) for shape in shapes],
        scratch_shapes=[pltpu.VMEM(shape, BF) for shape in shapes if sent]
        + [
            pltpu.VMEM((3, 256, 512), BF),
            pltpu.VMEM((2, 128, 256), BF),
            pltpu.VMEM((24, 256, 256), BF),
            pltpu.VMEM((2, 12, 2, 128, 128), BF),
            pltpu.SemaphoreType.DMA((2,)),
            pltpu.SemaphoreType.DMA((2, 3)),
        ],
        cost_estimate=pl.CostEstimate(
            flops=1000000000, bytes_accessed=4000000, transcendentals=0
        ),
        compiler_params=params(20),
        name="make_tiles" if sent else "make_home",
    )(own_table, far_table, own_wave, far_wave, left_operators, far_left)


def picks_kernel(slot_key, real_key, imag_key, sign, out):
    out[0:384] = (slot_key[...] == real_key[...]).astype(F32).astype(BF)
    out[384:768] = jnp.where(slot_key[...] == imag_key[...], sign[...], 0.0).astype(BF)


def make_picks(keys):
    return pl.pallas_call(
        picks_kernel,
        out_shape=jax.ShapeDtypeStruct((768, 384), BF),
        compiler_params=params(8),
        name="make_picks",
    )(*keys)


def contract_kernel(
    home, ahead1, back1, ahead2, back2, right, right_table, picks, out, paired_ref
):
    arrays = (home, ahead1, back1, ahead2, back2)
    zero = jnp.zeros((96, 128), BF)

    def lefts(a):
        if a >= 16:
            return [home[96 + g * 8 + a - 16] for g in range(6)] + [zero[0:32]]
        tiles = [ref[g * 16 + a] for ref in arrays[0:3] for g in range(6)]
        if a >= 8:
            return tiles + [zero]
        return tiles + [ref[g * 8 + a] for ref in arrays[3:5] for g in range(3)]

    def product(start):
        total = 0.0
        for a in range(start, start + 8, 2):
            total += lax.dot_general(
                jnp.concatenate([right[:, a + i].reshape(256, 128) for i in range(2)], axis=1),
                jnp.concatenate(
                    [jnp.concatenate(lefts(a + i), axis=0) for i in range(2)], axis=1
                ),
                (((1,), (1,)), ((), ())),
                preferred_element_type=F32,
            )
        return total

    paired = product(0) + product(8)
    cross = product(16)
    for third in range(3):
        lanes = slice(third * 128, third * 128 + 128)
        paired_ref[third] = paired[:, lanes] + cross if third == 0 else paired[:, lanes]

    slot_label = jnp.concatenate(
        [
            sum(ref[n + tile].astype(F32)[0:1] for ref, n in zip(arrays, TILES))
            for tile in range(3)
        ],
        axis=1,
    )
    row = iota((128, 128), 0)
    j = row % 32 // 2 * 8 + row // 32 % 2 * 4 + row % 2 * 2 + row // 64
    labels = right_table[pl.ds(where()[3], 1), :].astype(F32)
    right_label = jnp.sum(jnp.where(iota((128, 128), 1) == j, labels, 0.0), axis=1, keepdims=True)
    match = right_label == slot_label

    def part(c):
        rows = [
            jnp.concatenate(
                [paired_ref[third, pl.ds(c * 4 + w * 2 + t, 32, 8), :] for third in range(3)],
                axis=1,
            )
            for t in range(2)
            for w in range(2)
        ]
        return jnp.where(match, jnp.concatenate(rows, axis=0), 0.0)

    rest = jnp.concatenate([part(0), part(1)], axis=1)
    pieces = []
    for _ in range(2):
        pieces.append(rest.astype(BF))
        rest = rest - pieces[-1].astype(F32)
    total = jnp.dot(jnp.concatenate(pieces, axis=0), picks[...], preferred_element_type=F32)
    total = total[0:128] + total[128:256]
    total = total.astype(out.dtype)
    out[...] = jnp.zeros(out.shape, out.dtype)
    for t in range(2):
        for row in range(8):
            out[row, :, t * 48 : t * 48 + 48] = total[
                t * 64 : t * 64 + 64, row * 48 : row * 48 + 48
            ]


def contract(tiles, right, right_table, picks):
    whole = pl.BlockSpec(memory_space=pltpu.VMEM)
    return pl.pallas_call(
        contract_kernel,
        in_specs=[whole] * 8,
        out_specs=whole,
        out_shape=jax.ShapeDtypeStruct((8, 64, 128), BF),
        scratch_shapes=[pltpu.VMEM((3, 256, 128), F32)],
        compiler_params=params(16),
        name="contract",
    )(*tiles, right, right_table, picks)


def ring(step):
    pairs = []
    for z in range(8):
        for core in range(2):
            place = lambda z: ((z % 4) * 2 + core) * 2 + z // 4
            pairs.append((place(z), place(step(z, core))))
    return pairs


def local(
    wave_blocks, left_operators, right_operators, left_table, right_table, assignment, kramers_map
):
    line = ("row", "wf")
    core, z_lo, _, _ = where()
    right, own_wave = pick(right_operators, wave_blocks)
    far_wave = lax.ppermute(
        own_wave, line, ring(lambda z, core: (z + 2) % 8 if z in (2, 3, 6, 7) else (z - 2) % 8)
    )
    swap = [(i, i ^ 1) for i in range(8)]
    far_left = lax.ppermute(left_operators, "row", swap)
    far_table = lax.ppermute(left_table, "row", swap)
    right = lax.all_to_all(right, "col", 0, 0, tiled=True)
    ahead1, back1, ahead2, back2 = make_tiles(
        True, left_table, far_table, own_wave, far_wave, left_operators, far_left
    )
    far_wave, assignment, kramers_map, ahead1 = lax.optimization_barrier(
        (far_wave, assignment, kramers_map, ahead1)
    )
    ahead = lambda steps: ring(lambda z, core: (z + steps * (1 - 2 * core)) % 8)
    arrived = [
        lax.ppermute(ahead1, line, ahead(1)),
        lax.ppermute(back1, line, ahead(-1)),
        lax.ppermute(ahead2, line, ahead(2)),
        lax.ppermute(back2, line, ahead(-2)),
    ]
    (home,) = make_tiles(
        False, left_table, far_table, own_wave, far_wave, left_operators, far_left
    )
    tiles = [home] + arrived

    held = assignment.reshape(4, 2, 12)
    held = jnp.where(core == 0, held, held[:, ::-1])
    held = lax.dynamic_slice_in_dim(jnp.concatenate([held, held], axis=0), z_lo, 4, 0)
    turned = jnp.concatenate([held[0:1], held[3:4], held[1:3]], axis=0)
    straight = jnp.concatenate([held[0:2], held[3:4], held[2:3]], axis=0)
    held = jnp.where(core == 0, turned, straight).reshape(96, 1)
    slot_key = (held * 4 + jnp.arange(4, dtype=jnp.int32)[None, :]).reshape(384, 1)
    target = jnp.stack([jnp.arange(96, dtype=jnp.int32), kramers_map]).reshape(1, 2, 8, 12)
    target = target.transpose(2, 0, 1, 3)
    kind = jnp.arange(2, dtype=jnp.int32)[None, None, :, None]
    part = jnp.arange(2, dtype=jnp.int32)[None, :, None, None]
    real_key = (target * 4 + kind * 2 + part).reshape(1, 384)
    imag_key = (target * 4 + kind * 2 + 1 - part).reshape(1, 384)
    sign = jnp.broadcast_to((2 * part - 1).astype(F32), (8, 2, 2, 12)).reshape(1, 384)

    picks = make_picks([slot_key, real_key, imag_key, sign])
    shares = contract(tiles, right, right_table.T, picks)
    shares = lax.all_to_all(
        shares.reshape(256, 2, 128), ("row", "wf", "col"), 0, 0, tiled=True
    )
    total = jnp.sum(shares.astype(F32), axis=0)[:, 0:96]
    return total.reshape(2, 2, 2, 2, 12).transpose(2, 3, 4, 0, 1).reshape(2, 2, 12, 4)


def solution(mesh):
    return jax.shard_map(
        local,
        mesh=mesh,
        in_specs=(
            P(None, None, "wf", None),
            P("row", "col", None, None, None),
            P(None, "col", None, "wf", None),
            P("row", None),
            P(),
            P(),
            P(),
        ),
        out_specs=P(None, None, "row", ("col", "wf")),
        check_vma=False,
    )
```

```python
import functools

import jax
import jax.numpy as jnp
from jax import lax
from jax.experimental import pallas as pl
from jax.experimental.pallas import tpu as pltpu
from jax.sharding import PartitionSpec as P

BF = jnp.bfloat16
F32 = jnp.float32


def iota(shape, axis):
    return lax.broadcasted_iota(jnp.int32, shape, axis)


def where():
    row, col, wf = lax.axis_index("row"), lax.axis_index("col"), lax.axis_index("wf")
    return row & 1, row >> 1, wf * 4 + (row >> 1), 2 * col + (row & 1)


def params(mebibytes):
    return pltpu.CompilerParams(vmem_limit_bytes=mebibytes * 1024 * 1024)


def pick_kernel(right_ref, wave_ref, out_ref, wave_out, rows_ref, sem, wave_sem):
    core, z_lo, _, q = where()
    waves = [
        pltpu.make_async_copy(wave_ref.at[:, (q + o) & 31], wave_out.at[:, o], wave_sem.at[o])
        for o in range(3)
    ]
    for copy in waves:
        copy.start()
    copies = []
    for part in range(4):
        for second in range(2):
            copy = pltpu.make_async_copy(
                right_ref.at[pl.ds(part * 4, 4), core, :, :, z_lo ^ (2 * second)],
                rows_ref.at[second, pl.ds(part * 4, 4)],
                sem.at[part, second],
            )
            copy.start()
            copies.append(copy)
    for part in range(4):
        for second in range(2):
            copies[part * 2 + second].wait()
        for target in range(part * 4, part * 4 + 4):
            for second in range(2):
                rows = jnp.concatenate(
                    [
                        rows_ref[second, target, 4 * w + 2 * h + t, c][None]
                        for h in range(2)
                        for c in range(2)
                        for w in range(2)
                        for t in range(2)
                    ],
                    axis=0,
                )
                rows = jnp.swapaxes(rows, 0, 1)
                if second:
                    out_ref[target, 16:24] = rows[8:16]
                else:
                    out_ref[target, 0:16] = rows
    for copy in waves:
        copy.wait()


def pick(right_operators, wave_blocks):
    whole = pl.BlockSpec(memory_space=pltpu.VMEM)
    return pl.pallas_call(
        pick_kernel,
        in_specs=[pl.BlockSpec(memory_space=pltpu.HBM)] * 2,
        out_specs=[whole] * 2,
        out_shape=[
            jax.ShapeDtypeStruct((16, 24, 16, 128), BF),
            jax.ShapeDtypeStruct((2, 3, 64, 128), BF),
        ],
        scratch_shapes=[
            pltpu.VMEM((2, 16, 8, 2, 16, 128), BF),
            pltpu.SemaphoreType.DMA((4, 2)),
            pltpu.SemaphoreType.DMA((3,)),
        ],
        compiler_params=params(54),
        name="pick",
    )(right_operators.reshape(16, 2, 8, 2, 4, 16, 128), wave_blocks)


GROUPS = (6, 6, 6, 3, 3)
ROWS = (24, 16, 16, 8, 8)
STARTS = (0, 96, 192, 288, 336)
TILES = tuple(n * rows for n, rows in zip(GROUPS, ROWS))


def tiles_kernel(
    sent, own_table, far_table, own_wave, far_wave, own_left, far_left, *refs
):
    count = 4 if sent else 1
    results, outs = refs[:count], refs[count : 2 * count] if sent else refs[:count]
    sides, bras, kets, operators, sem, out_sem = refs[-6:]
    core, _, z, q = where()
    ahead = 1 - 2 * core
    low = z < 4
    copies = [
        pltpu.make_async_copy(own_left.at[:, core], operators.at[0], sem.at[0]),
        pltpu.make_async_copy(far_left.at[:, core], operators.at[1], sem.at[1]),
    ]
    for copy in copies:
        copy.start()

    def wave(c, o):
        mine, other = own_wave[c, o], far_wave[c, o]
        return jnp.concatenate(
            [jnp.where(low, mine, other), jnp.where(low, other, mine)], axis=0
        )

    for o in range(3):
        re, im = wave(0, o), wave(1, o)
        top = jnp.concatenate([re, im, re, im], axis=1)
        bottom = jnp.concatenate([-im, re, im, -re], axis=1)
        sides[o] = jnp.concatenate([top, bottom], axis=0)
        if o == 0:
            re_t, im_t = re.T, im.T
            bras[0] = jnp.concatenate([re_t, im_t], axis=1)
            bras[1] = jnp.concatenate([-im_t, re_t], axis=1)

    columns = [
        jnp.sum(jnp.where(iota((12, 32), 1) == q, table[...], 0), axis=1, keepdims=True)
        for table in (own_table, far_table)
    ]
    labels = [column[s, 0] for column in columns for s in range(12)]
    shifts = [lax.rem(label - q + 32, 32) for label in labels]
    for out, spot in zip(outs, range(1, 5) if sent else range(1)):
        members = GROUPS[spot] * 4
        offset = 12 if spot == 4 else 0
        for tile in range(3):
            place = (iota((16, 128), 1) + tile * 128 - STARTS[spot]) // 4
            row = jnp.zeros((16, 128), F32)
            low_s, high_s = (tile * 128 - STARTS[spot]) // 4, (tile * 128 + 128 - STARTS[spot]) // 4
            for s in range(max(0, low_s), min(members, high_s)):
                row = jnp.where(place == s, labels[offset + s].astype(F32), row)
            out[TILES[spot] + tile] = row.astype(BF)

    leaving = []
    for half in range(2):
        if sent:
            spots = [(z + ahead) & 7, (z - ahead) & 7, (z - 2 * ahead if half else z + 2 * ahead) & 7]
        else:
            spots = [z, z ^ 2]
        width = 16 * len(spots)
        left = jnp.concatenate(
            [
                bras[c, pl.ds(pl.multiple_of(spot * 16, 16), 16), :]
                for c in range(2)
                for spot in spots
            ],
            axis=0,
        )
        copies[half].wait()
        for s in range(12):
            operator = jnp.concatenate(
                [operators[half, s, 0], operators[half, s, 1]], axis=1
            )
            turned = jnp.dot(
                operator, sides[shifts[half * 12 + s]], preferred_element_type=F32
            ).astype(BF)
            kets[half * 12 + s] = jnp.concatenate(
                [
                    jnp.concatenate([turned[:, 0:128], turned[:, 256:384]], axis=1),
                    jnp.concatenate([turned[:, 128:256], turned[:, 384:512]], axis=1),
                ],
                axis=0,
            )
        for group in range(3):
            whole = half * 3 + group
            brackets = [
                jnp.dot(left, kets[whole * 4 + s], preferred_element_type=F32).astype(BF)
                for s in range(4)
            ]
            for i in range(len(spots)):
                rows = jnp.concatenate(
                    [
                        brackets[s][
                            c * width + i * 16 : c * width + i * 16 + 16,
                            kind * 128 : kind * 128 + 128,
                        ][None]
                        for s in range(4)
                        for kind in range(2)
                        for c in range(2)
                    ],
                    axis=0,
                )
                rows = jnp.swapaxes(rows, 0, 1)
                if sent and i == 2:
                    outs[2 + half][group * 8 : group * 8 + 8] = rows[0:8]
                elif i == 1 and not sent:
                    outs[0][96 + whole * 8 : 96 + whole * 8 + 8] = rows[8:16]
                else:
                    outs[i][whole * 16 : whole * 16 + 16] = rows
        if sent:
            part = slice(48, TILES[1] + 3) if half else slice(0, 48)
            for i, tiles in ((0, part), (1, part), (2 + half, slice(0, TILES[3] + 3))):
                size = tiles.stop - tiles.start
                copy = pltpu.make_async_copy(
                    outs[i].at[pl.ds(tiles.start, size)],
                    results[i].at[pl.ds(tiles.start, size)],
                    out_sem.at[half, min(i, 2)],
                )
                copy.start()
                leaving.append(copy)
    for copy in leaving:
        copy.wait()


def make_tiles(sent, own_table, far_table, own_wave, far_wave, left_operators, far_left):
    anywhere, whole = pl.BlockSpec(memory_space=pl.ANY), pl.BlockSpec(memory_space=pltpu.VMEM)
    shapes = [(n + 3, 16, 128) for n in (TILES[1:] if sent else TILES[:1])]
    return pl.pallas_call(
        functools.partial(tiles_kernel, sent),
        in_specs=[whole] * 4 + [anywhere] * 2,
        out_specs=[anywhere if sent else whole] * len(shapes),
        out_shape=[jax.ShapeDtypeStruct(shape, BF) for shape in shapes],
        scratch_shapes=[pltpu.VMEM(shape, BF) for shape in shapes if sent]
        + [
            pltpu.VMEM((3, 256, 512), BF),
            pltpu.VMEM((2, 128, 256), BF),
            pltpu.VMEM((24, 256, 256), BF),
            pltpu.VMEM((2, 12, 2, 128, 128), BF),
            pltpu.SemaphoreType.DMA((2,)),
            pltpu.SemaphoreType.DMA((2, 3)),
        ],
        cost_estimate=pl.CostEstimate(
            flops=1000000000, bytes_accessed=4000000, transcendentals=0
        ),
        compiler_params=params(20),
        name="make_tiles" if sent else "make_home",
    )(own_table, far_table, own_wave, far_wave, left_operators, far_left)


def picks_kernel(slot_key, real_key, imag_key, sign, out):
    out[0:384] = (slot_key[...] == real_key[...]).astype(F32).astype(BF)
    out[384:768] = jnp.where(slot_key[...] == imag_key[...], sign[...], 0.0).astype(BF)


def make_picks(keys):
    return pl.pallas_call(
        picks_kernel,
        out_shape=jax.ShapeDtypeStruct((768, 384), BF),
        compiler_params=params(8),
        name="make_picks",
    )(*keys)


def contract_kernel(
    home, ahead1, back1, ahead2, back2, right, right_table, picks, out, paired_ref
):
    arrays = (home, ahead1, back1, ahead2, back2)
    zero = jnp.zeros((96, 128), BF)

    def lefts(a):
        if a >= 16:
            return [home[96 + g * 8 + a - 16] for g in range(6)] + [zero[0:32]]
        tiles = [ref[g * 16 + a] for ref in arrays[0:3] for g in range(6)]
        if a >= 8:
            return tiles + [zero]
        return tiles + [ref[g * 8 + a] for ref in arrays[3:5] for g in range(3)]

    def product(start):
        total = 0.0
        for a in range(start, start + 8, 2):
            total += lax.dot_general(
                jnp.concatenate([right[:, a + i].reshape(256, 128) for i in range(2)], axis=1),
                jnp.concatenate(
                    [jnp.concatenate(lefts(a + i), axis=0) for i in range(2)], axis=1
                ),
                (((1,), (1,)), ((), ())),
                preferred_element_type=F32,
            )
        return total

    paired = product(0) + product(8)
    cross = product(16)
    for third in range(3):
        lanes = slice(third * 128, third * 128 + 128)
        paired_ref[third] = paired[:, lanes] + cross if third == 0 else paired[:, lanes]

    slot_label = jnp.concatenate(
        [
            sum(ref[n + tile].astype(F32)[0:1] for ref, n in zip(arrays, TILES))
            for tile in range(3)
        ],
        axis=1,
    )
    row = iota((128, 128), 0)
    j = row % 32 // 2 * 8 + row // 32 % 2 * 4 + row % 2 * 2 + row // 64
    labels = right_table[pl.ds(where()[3], 1), :].astype(F32)
    right_label = jnp.sum(jnp.where(iota((128, 128), 1) == j, labels, 0.0), axis=1, keepdims=True)
    match = right_label == slot_label

    def part(c):
        rows = [
            jnp.concatenate(
                [paired_ref[third, pl.ds(c * 4 + w * 2 + t, 32, 8), :] for third in range(3)],
                axis=1,
            )
            for t in range(2)
            for w in range(2)
        ]
        return jnp.where(match, jnp.concatenate(rows, axis=0), 0.0)

    rest = jnp.concatenate([part(0), part(1)], axis=1)
    pieces = []
    for _ in range(2):
        pieces.append(rest.astype(BF))
        rest = rest - pieces[-1].astype(F32)
    total = jnp.dot(jnp.concatenate(pieces, axis=0), picks[...], preferred_element_type=F32)
    total = total[0:128] + total[128:256]
    total = total.astype(out.dtype)
    out[...] = jnp.zeros(out.shape, out.dtype)
    for t in range(2):
        for row in range(8):
            out[row, :, t * 48 : t * 48 + 48] = total[
                t * 64 : t * 64 + 64, row * 48 : row * 48 + 48
            ]


def contract(tiles, right, right_table, picks):
    whole = pl.BlockSpec(memory_space=pltpu.VMEM)
    return pl.pallas_call(
        contract_kernel,
        in_specs=[whole] * 8,
        out_specs=whole,
        out_shape=jax.ShapeDtypeStruct((8, 64, 128), BF),
        scratch_shapes=[pltpu.VMEM((3, 256, 128), F32)],
        compiler_params=params(16),
        name="contract",
    )(*tiles, right, right_table, picks)


def ring(step):
    pairs = []
    for z in range(8):
        for core in range(2):
            place = lambda z: ((z % 4) * 2 + core) * 2 + z // 4
            pairs.append((place(z), place(step(z, core))))
    return pairs


def local(
    wave_blocks, left_operators, right_operators, left_table, right_table, assignment, kramers_map
):
    line = ("row", "wf")
    core, z_lo, _, _ = where()
    right, own_wave = pick(right_operators, wave_blocks)
    far_wave = lax.ppermute(
        own_wave, line, ring(lambda z, core: (z + 2) % 8 if z in (2, 3, 6, 7) else (z - 2) % 8)
    )
    swap = [(i, i ^ 1) for i in range(8)]
    far_left = lax.ppermute(left_operators, "row", swap)
    far_table = lax.ppermute(left_table, "row", swap)
    right = lax.all_to_all(right, "col", 0, 0, tiled=True)
    ahead1, back1, ahead2, back2 = make_tiles(
        True, left_table, far_table, own_wave, far_wave, left_operators, far_left
    )
    far_wave, assignment, kramers_map, ahead1 = lax.optimization_barrier(
        (far_wave, assignment, kramers_map, ahead1)
    )
    ahead = lambda steps: ring(lambda z, core: (z + steps * (1 - 2 * core)) % 8)
    arrived = [
        lax.ppermute(ahead1, line, ahead(1)),
        lax.ppermute(back1, line, ahead(-1)),
        lax.ppermute(ahead2, line, ahead(2)),
        lax.ppermute(back2, line, ahead(-2)),
    ]
    (home,) = make_tiles(
        False, left_table, far_table, own_wave, far_wave, left_operators, far_left
    )
    tiles = [home] + arrived

    held = assignment.reshape(4, 2, 12)
    held = jnp.where(core == 0, held, held[:, ::-1])
    held = lax.dynamic_slice_in_dim(jnp.concatenate([held, held], axis=0), z_lo, 4, 0)
    turned = jnp.concatenate([held[0:1], held[3:4], held[1:3]], axis=0)
    straight = jnp.concatenate([held[0:2], held[3:4], held[2:3]], axis=0)
    held = jnp.where(core == 0, turned, straight).reshape(96, 1)
    slot_key = (held * 4 + jnp.arange(4, dtype=jnp.int32)[None, :]).reshape(384, 1)
    target = jnp.stack([jnp.arange(96, dtype=jnp.int32), kramers_map]).reshape(1, 2, 8, 12)
    target = target.transpose(2, 0, 1, 3)
    kind = jnp.arange(2, dtype=jnp.int32)[None, None, :, None]
    part = jnp.arange(2, dtype=jnp.int32)[None, :, None, None]
    real_key = (target * 4 + kind * 2 + part).reshape(1, 384)
    imag_key = (target * 4 + kind * 2 + 1 - part).reshape(1, 384)
    sign = jnp.broadcast_to((2 * part - 1).astype(F32), (8, 2, 2, 12)).reshape(1, 384)

    picks = make_picks([slot_key, real_key, imag_key, sign])
    shares = contract(tiles, right, right_table.T, picks)
    shares = lax.all_to_all(
        shares.reshape(256, 2, 128), ("row", "wf", "col"), 0, 0, tiled=True
    )
    total = jnp.sum(shares.astype(F32), axis=0)[:, 0:96]
    return total.reshape(2, 2, 2, 2, 12).transpose(2, 3, 4, 0, 1).reshape(2, 2, 12, 4)


def solution(mesh):
    return jax.shard_map(
        local,
        mesh=mesh,
        in_specs=(
            P(None, None, "wf", None),
            P("row", "col", None, None, None),
            P(None, "col", None, "wf", None),
            P("row", None),
            P(),
            P(),
            P(),
        ),
        out_specs=P(None, None, "row", ("col", "wf")),
        check_vma=False,
    )
```

```python
import functools

import jax
import jax.numpy as jnp
from jax import lax
from jax.experimental import pallas as pl
from jax.experimental.pallas import tpu as pltpu
from jax.sharding import PartitionSpec as P

BF = jnp.bfloat16
F32 = jnp.float32


def iota(shape, axis):
    return lax.broadcasted_iota(jnp.int32, shape, axis)


def where():
    row, col, wf = lax.axis_index("row"), lax.axis_index("col"), lax.axis_index("wf")
    return row & 1, row >> 1, wf * 4 + (row >> 1), 2 * col + (row & 1)


def params(mebibytes):
    return pltpu.CompilerParams(vmem_limit_bytes=mebibytes * 1024 * 1024)


SPLIT = 8
CROSS = 16 - SPLIT
ROWS = (16 + CROSS, 16, 16, SPLIT)
TILES = tuple(6 * rows for rows in ROWS)


def pick_kernel(right_ref, wave_ref, out_ref, wave_out, rows_ref, sem, wave_sem):
    core, z_lo, _, q = where()
    waves = [
        pltpu.make_async_copy(wave_ref.at[:, (q + o) & 31], wave_out.at[:, o], wave_sem.at[o])
        for o in range(3)
    ]
    for copy in waves:
        copy.start()
    copies = []
    for part in range(4):
        for second in range(2):
            copy = pltpu.make_async_copy(
                right_ref.at[pl.ds(part * 4, 4), core, :, :, z_lo ^ (2 * second)],
                rows_ref.at[second, pl.ds(part * 4, 4)],
                sem.at[part, second],
            )
            copy.start()
            copies.append(copy)
    for part in range(4):
        for second in range(2):
            copies[part * 2 + second].wait()
        for target in range(part * 4, part * 4 + 4):
            for second in range(2):
                rows = jnp.concatenate(
                    [
                        rows_ref[second, target, 4 * w + 2 * h + t, c][None]
                        for h in range(2)
                        for c in range(2)
                        for w in range(2)
                        for t in range(2)
                    ],
                    axis=0,
                )
                rows = jnp.swapaxes(rows, 0, 1)
                if second:
                    out_ref[target, 16 : 16 + CROSS] = rows[SPLIT:16]
                else:
                    out_ref[target, 0:16] = rows
    for copy in waves:
        copy.wait()


def pick(right_operators, wave_blocks):
    whole = pl.BlockSpec(memory_space=pltpu.VMEM)
    return pl.pallas_call(
        pick_kernel,
        in_specs=[pl.BlockSpec(memory_space=pltpu.HBM)] * 2,
        out_specs=[whole] * 2,
        out_shape=[
            jax.ShapeDtypeStruct((16, 16 + CROSS, 16, 128), BF),
            jax.ShapeDtypeStruct((2, 3, 64, 128), BF),
        ],
        scratch_shapes=[
            pltpu.VMEM((2, 16, 8, 2, 16, 128), BF),
            pltpu.SemaphoreType.DMA((4, 2)),
            pltpu.SemaphoreType.DMA((3,)),
        ],
        compiler_params=params(54),
        name="pick",
    )(right_operators.reshape(16, 2, 8, 2, 4, 16, 128), wave_blocks)


def tiles_kernel(
    sent, own_table, far_table, own_wave, far_wave, own_left, far_left, *refs
):
    count = 3 if sent else 1
    results, outs = refs[:count], refs[count : 2 * count] if sent else refs[:count]
    sides, bras, kets, operators, sem, out_sem = refs[-6:]
    core, _, z, q = where()
    ahead = 1 - 2 * core
    low = z < 4
    copies = [
        pltpu.make_async_copy(own_left.at[:, core], operators.at[0], sem.at[0]),
        pltpu.make_async_copy(far_left.at[:, core], operators.at[1], sem.at[1]),
    ]
    for copy in copies:
        copy.start()

    def wave(c, o):
        mine, other = own_wave[c, o], far_wave[c, o]
        return jnp.concatenate(
            [jnp.where(low, mine, other), jnp.where(low, other, mine)], axis=0
        )

    for o in range(3):
        re, im = wave(0, o), wave(1, o)
        top = jnp.concatenate([re, im, re, im], axis=1)
        bottom = jnp.concatenate([-im, re, im, -re], axis=1)
        sides[o] = jnp.concatenate([top, bottom], axis=0)
        if o == 0:
            re_t, im_t = re.T, im.T
            bras[0] = jnp.concatenate([re_t, im_t], axis=1)
            bras[1] = jnp.concatenate([-im_t, re_t], axis=1)

    columns = [
        jnp.sum(jnp.where(iota((12, 32), 1) == q, table[...], 0), axis=1, keepdims=True)
        for table in (own_table, far_table)
    ]
    labels = [column[s, 0] for column in columns for s in range(12)]
    shifts = [lax.rem(label - q + 32, 32) for label in labels]
    for i, out in enumerate(outs):
        start = 96 * (i + 1 if sent else 0)
        for tile in range(3):
            place = (iota((16, 128), 1) + tile * 128 - start) // 4
            row = jnp.zeros((16, 128), F32)
            for s in range(max(0, (tile * 128 - start) // 4), min(24, (tile * 128 + 128 - start) // 4)):
                row = jnp.where(place == s, labels[s].astype(F32), row)
            out[out.shape[0] - 3 + tile] = row.astype(BF)

    leaving = []
    for half in range(2):
        if sent:
            spots = [(z + ahead) & 7, (z - ahead) & 7, (z + 2 * ahead) & 7]
        else:
            spots = [z, z ^ 2]
        width = 16 * len(spots)
        left = jnp.concatenate(
            [
                bras[c, pl.ds(pl.multiple_of(spot * 16, 16), 16), :]
                for c in range(2)
                for spot in spots
            ],
            axis=0,
        )
        copies[half].wait()
        for s in range(12):
            operator = jnp.concatenate(
                [operators[half, s, 0], operators[half, s, 1]], axis=1
            )
            turned = jnp.dot(
                operator, sides[shifts[half * 12 + s]], preferred_element_type=F32
            ).astype(BF)
            kets[half * 12 + s] = jnp.concatenate(
                [
                    jnp.concatenate([turned[:, 0:128], turned[:, 256:384]], axis=1),
                    jnp.concatenate([turned[:, 128:256], turned[:, 384:512]], axis=1),
                ],
                axis=0,
            )
        for group in range(3):
            whole = half * 3 + group
            brackets = [
                jnp.dot(left, kets[whole * 4 + s], preferred_element_type=F32).astype(BF)
                for s in range(4)
            ]
            for i in range(len(spots)):
                rows = jnp.concatenate(
                    [
                        brackets[s][
                            c * width + i * 16 : c * width + i * 16 + 16,
                            kind * 128 : kind * 128 + 128,
                        ][None]
                        for s in range(4)
                        for kind in range(2)
                        for c in range(2)
                    ],
                    axis=0,
                )
                rows = jnp.swapaxes(rows, 0, 1)
                if sent and i == 2:
                    outs[2][whole * SPLIT : whole * SPLIT + SPLIT] = rows[0:SPLIT]
                elif i == 1 and not sent:
                    outs[0][96 + whole * CROSS : 96 + whole * CROSS + CROSS] = rows[SPLIT:16]
                else:
                    outs[i][whole * 16 : whole * 16 + 16] = rows
        if sent:
            for i, out in enumerate(outs):
                middle = TILES[i + 1] // 2
                size = middle + 3 if half else middle
                copy = pltpu.make_async_copy(
                    out.at[pl.ds(middle * half, size)],
                    results[i].at[pl.ds(middle * half, size)],
                    out_sem.at[half, i],
                )
                copy.start()
                leaving.append(copy)
    for copy in leaving:
        copy.wait()


def make_tiles(sent, own_table, far_table, own_wave, far_wave, left_operators, far_left):
    anywhere, whole = pl.BlockSpec(memory_space=pl.ANY), pl.BlockSpec(memory_space=pltpu.VMEM)
    shapes = [(n + 3, 16, 128) for n in (TILES[1:] if sent else TILES[:1])]
    return pl.pallas_call(
        functools.partial(tiles_kernel, sent),
        in_specs=[whole] * 4 + [anywhere] * 2,
        out_specs=[anywhere if sent else whole] * len(shapes),
        out_shape=[jax.ShapeDtypeStruct(shape, BF) for shape in shapes],
        scratch_shapes=[pltpu.VMEM(shape, BF) for shape in shapes if sent]
        + [
            pltpu.VMEM((3, 256, 512), BF),
            pltpu.VMEM((2, 128, 256), BF),
            pltpu.VMEM((24, 256, 256), BF),
            pltpu.VMEM((2, 12, 2, 128, 128), BF),
            pltpu.SemaphoreType.DMA((2,)),
            pltpu.SemaphoreType.DMA((2, 3)),
        ],
        cost_estimate=pl.CostEstimate(
            flops=1000000000, bytes_accessed=4000000, transcendentals=0
        ),
        compiler_params=params(20),
        name="make_tiles" if sent else "make_home",
    )(own_table, far_table, own_wave, far_wave, left_operators, far_left)


def picks_kernel(slot_key, real_key, imag_key, sign, out):
    out[0:384] = (slot_key[...] == real_key[...]).astype(F32).astype(BF)
    out[384:768] = jnp.where(slot_key[...] == imag_key[...], sign[...], 0.0).astype(BF)


def make_picks(keys):
    return pl.pallas_call(
        picks_kernel,
        out_shape=jax.ShapeDtypeStruct((768, 384), BF),
        compiler_params=params(8),
        name="make_picks",
    )(*keys)


def contract_kernel(
    home, ahead1, back1, ahead2, right, right_table, picks, out, paired_ref
):
    arrays = (home, ahead1, back1, ahead2)
    zero = jnp.zeros((96, 128), BF)

    def lefts(a):
        if a >= 16:
            return [home[96 + g * CROSS + a - 16] for g in range(6)] + [zero[0:32]]
        tiles = [ref[g * 16 + a] for ref in arrays[0:3] for g in range(6)]
        if a >= SPLIT:
            return tiles + [zero]
        return tiles + [ahead2[g * SPLIT + a] for g in range(6)]

    def product(start, stop):
        total = 0.0
        for first in range(start, stop, 2):
            pair = range(first, min(first + 2, stop))
            total += lax.dot_general(
                jnp.concatenate([right[:, a].reshape(256, 128) for a in pair], axis=1),
                jnp.concatenate([jnp.concatenate(lefts(a), axis=0) for a in pair], axis=1),
                (((1,), (1,)), ((), ())),
                preferred_element_type=F32,
            )
        return total

    paired = product(0, 16)
    cross = product(16, 16 + CROSS)
    for third in range(3):
        lanes = slice(third * 128, third * 128 + 128)
        paired_ref[third] = paired[:, lanes] + cross if third == 0 else paired[:, lanes]

    slot_label = jnp.concatenate(
        [
            sum(ref[n + tile].astype(F32)[0:1] for ref, n in zip(arrays, TILES))
            for tile in range(3)
        ],
        axis=1,
    )
    row = iota((128, 128), 0)
    j = row % 32 // 2 * 8 + row // 32 % 2 * 4 + row % 2 * 2 + row // 64
    labels = right_table[pl.ds(where()[3], 1), :].astype(F32)
    right_label = jnp.sum(jnp.where(iota((128, 128), 1) == j, labels, 0.0), axis=1, keepdims=True)
    match = right_label == slot_label

    def part(c):
        rows = [
            jnp.concatenate(
                [paired_ref[third, pl.ds(c * 4 + w * 2 + t, 32, 8), :] for third in range(3)],
                axis=1,
            )
            for t in range(2)
            for w in range(2)
        ]
        return jnp.where(match, jnp.concatenate(rows, axis=0), 0.0)

    rest = jnp.concatenate([part(0), part(1)], axis=1)
    pieces = []
    for _ in range(2):
        pieces.append(rest.astype(BF))
        rest = rest - pieces[-1].astype(F32)
    total = jnp.dot(jnp.concatenate(pieces, axis=0), picks[...], preferred_element_type=F32)
    total = total[0:128] + total[128:256]
    total = total.astype(out.dtype)
    out[...] = jnp.zeros(out.shape, out.dtype)
    for t in range(2):
        for row in range(8):
            out[row, :, t * 48 : t * 48 + 48] = total[
                t * 64 : t * 64 + 64, row * 48 : row * 48 + 48
            ]


def contract(tiles, right, right_table, picks):
    whole = pl.BlockSpec(memory_space=pltpu.VMEM)
    return pl.pallas_call(
        contract_kernel,
        in_specs=[whole] * 7,
        out_specs=whole,
        out_shape=jax.ShapeDtypeStruct((8, 64, 128), BF),
        scratch_shapes=[pltpu.VMEM((3, 256, 128), F32)],
        compiler_params=params(16),
        name="contract",
    )(*tiles, right, right_table, picks)


def ring(step):
    pairs = []
    for z in range(8):
        for core in range(2):
            place = lambda z: ((z % 4) * 2 + core) * 2 + z // 4
            pairs.append((place(z), place(step(z, core))))
    return pairs


def local(
    wave_blocks, left_operators, right_operators, left_table, right_table, assignment, kramers_map
):
    line = ("row", "wf")
    core, z_lo, _, _ = where()
    right, own_wave = pick(right_operators, wave_blocks)
    far_wave = lax.ppermute(
        own_wave, line, ring(lambda z, core: (z + 2) % 8 if z in (2, 3, 6, 7) else (z - 2) % 8)
    )
    swap = [(i, i ^ 1) for i in range(8)]
    far_left = lax.ppermute(left_operators, "row", swap)
    far_table = lax.ppermute(left_table, "row", swap)
    right = lax.all_to_all(right, "col", 0, 0, tiled=True)
    ahead1, back1, ahead2 = make_tiles(
        True, left_table, far_table, own_wave, far_wave, left_operators, far_left
    )
    far_wave, assignment, kramers_map, ahead1 = lax.optimization_barrier(
        (far_wave, assignment, kramers_map, ahead1)
    )
    ahead = lambda steps: ring(lambda z, core: (z + steps * (1 - 2 * core)) % 8)
    arrived = [
        lax.ppermute(ahead1, line, ahead(1)),
        lax.ppermute(back1, line, ahead(-1)),
        lax.ppermute(ahead2, line, ahead(2)),
    ]
    (home,) = make_tiles(
        False, left_table, far_table, own_wave, far_wave, left_operators, far_left
    )
    tiles = [home] + arrived

    held = assignment.reshape(4, 2, 12)
    held = jnp.where(core == 0, held, held[:, ::-1])
    held = lax.dynamic_slice_in_dim(jnp.concatenate([held, held], axis=0), z_lo, 4, 0)
    turned = jnp.concatenate([held[0:1], held[3:4], held[1:3]], axis=0)
    straight = jnp.concatenate([held[0:2], held[3:4], held[2:3]], axis=0)
    held = jnp.where(core == 0, turned, straight).reshape(96, 1)
    slot_key = (held * 4 + jnp.arange(4, dtype=jnp.int32)[None, :]).reshape(384, 1)
    target = jnp.stack([jnp.arange(96, dtype=jnp.int32), kramers_map]).reshape(1, 2, 8, 12)
    target = target.transpose(2, 0, 1, 3)
    kind = jnp.arange(2, dtype=jnp.int32)[None, None, :, None]
    part = jnp.arange(2, dtype=jnp.int32)[None, :, None, None]
    real_key = (target * 4 + kind * 2 + part).reshape(1, 384)
    imag_key = (target * 4 + kind * 2 + 1 - part).reshape(1, 384)
    sign = jnp.broadcast_to((2 * part - 1).astype(F32), (8, 2, 2, 12)).reshape(1, 384)

    picks = make_picks([slot_key, real_key, imag_key, sign])
    shares = contract(tiles, right, right_table.T, picks)
    shares = lax.all_to_all(
        shares.reshape(256, 2, 128), ("row", "wf", "col"), 0, 0, tiled=True
    )
    total = jnp.sum(shares.astype(F32), axis=0)[:, 0:96]
    return total.reshape(2, 2, 2, 2, 12).transpose(2, 3, 4, 0, 1).reshape(2, 2, 12, 4)


def solution(mesh):
    return jax.shard_map(
        local,
        mesh=mesh,
        in_specs=(
            P(None, None, "wf", None),
            P("row", "col", None, None, None),
            P(None, "col", None, "wf", None),
            P("row", None),
            P(),
            P(),
            P(),
        ),
        out_specs=P(None, None, "row", ("col", "wf")),
        check_vma=False,
    )
```

```python
import functools

import jax
import jax.numpy as jnp
from jax import lax
from jax.experimental import pallas as pl
from jax.experimental.pallas import tpu as pltpu
from jax.sharding import PartitionSpec as P

BF = jnp.bfloat16
F32 = jnp.float32


def iota(shape, axis):
    return lax.broadcasted_iota(jnp.int32, shape, axis)


def where():
    row, col, wf = lax.axis_index("row"), lax.axis_index("col"), lax.axis_index("wf")
    return row & 1, row >> 1, wf * 4 + (row >> 1), 2 * col + (row & 1)


def params(mebibytes):
    return pltpu.CompilerParams(vmem_limit_bytes=mebibytes * 1024 * 1024)


SPLIT = 7
CROSS = 16 - SPLIT
ROWS = (16 + CROSS, 16, 16, SPLIT)
TILES = tuple(6 * rows for rows in ROWS)


def pick_kernel(right_ref, wave_ref, out_ref, wave_out, rows_ref, sem, wave_sem):
    core, z_lo, _, q = where()
    waves = [
        pltpu.make_async_copy(wave_ref.at[:, (q + o) & 31], wave_out.at[:, o], wave_sem.at[o])
        for o in range(3)
    ]
    for copy in waves:
        copy.start()
    copies = []
    for part in range(4):
        for second in range(2):
            copy = pltpu.make_async_copy(
                right_ref.at[pl.ds(part * 4, 4), core, :, :, z_lo ^ (2 * second)],
                rows_ref.at[second, pl.ds(part * 4, 4)],
                sem.at[part, second],
            )
            copy.start()
            copies.append(copy)
    for part in range(4):
        for second in range(2):
            copies[part * 2 + second].wait()
        for target in range(part * 4, part * 4 + 4):
            for second in range(2):
                rows = jnp.concatenate(
                    [
                        rows_ref[second, target, 4 * w + 2 * h + t, c][None]
                        for h in range(2)
                        for c in range(2)
                        for w in range(2)
                        for t in range(2)
                    ],
                    axis=0,
                )
                rows = jnp.swapaxes(rows, 0, 1)
                if second:
                    out_ref[target, 16 : 16 + CROSS] = rows[SPLIT:16]
                else:
                    out_ref[target, 0:16] = rows
    for copy in waves:
        copy.wait()


def pick(right_operators, wave_blocks):
    whole = pl.BlockSpec(memory_space=pltpu.VMEM)
    return pl.pallas_call(
        pick_kernel,
        in_specs=[pl.BlockSpec(memory_space=pltpu.HBM)] * 2,
        out_specs=[whole] * 2,
        out_shape=[
            jax.ShapeDtypeStruct((16, 16 + CROSS, 16, 128), BF),
            jax.ShapeDtypeStruct((2, 3, 64, 128), BF),
        ],
        scratch_shapes=[
            pltpu.VMEM((2, 16, 8, 2, 16, 128), BF),
            pltpu.SemaphoreType.DMA((4, 2)),
            pltpu.SemaphoreType.DMA((3,)),
        ],
        compiler_params=params(54),
        name="pick",
    )(right_operators.reshape(16, 2, 8, 2, 4, 16, 128), wave_blocks)


def tiles_kernel(
    sent, own_table, far_table, own_wave, far_wave, own_left, far_left, *refs
):
    count = 3 if sent else 1
    results, outs = refs[:count], refs[count : 2 * count] if sent else refs[:count]
    sides, bras, kets, operators, sem, out_sem = refs[-6:]
    core, _, z, q = where()
    ahead = 1 - 2 * core
    low = z < 4
    copies = [
        pltpu.make_async_copy(own_left.at[:, core], operators.at[0], sem.at[0]),
        pltpu.make_async_copy(far_left.at[:, core], operators.at[1], sem.at[1]),
    ]
    for copy in copies:
        copy.start()

    def wave(c, o):
        mine, other = own_wave[c, o], far_wave[c, o]
        return jnp.concatenate(
            [jnp.where(low, mine, other), jnp.where(low, other, mine)], axis=0
        )

    for o in range(3):
        re, im = wave(0, o), wave(1, o)
        top = jnp.concatenate([re, im, re, im], axis=1)
        bottom = jnp.concatenate([-im, re, im, -re], axis=1)
        sides[o] = jnp.concatenate([top, bottom], axis=0)
        if o == 0:
            re_t, im_t = re.T, im.T
            bras[0] = jnp.concatenate([re_t, im_t], axis=1)
            bras[1] = jnp.concatenate([-im_t, re_t], axis=1)

    columns = [
        jnp.sum(jnp.where(iota((12, 32), 1) == q, table[...], 0), axis=1, keepdims=True)
        for table in (own_table, far_table)
    ]
    labels = [column[s, 0] for column in columns for s in range(12)]
    shifts = [lax.rem(label - q + 32, 32) for label in labels]
    for i, out in enumerate(outs):
        start = 96 * (i + 1 if sent else 0)
        place = (iota((16, 128), 0) * 128 + iota((16, 128), 1) - start) >> 2
        label = jnp.zeros((16, 128), F32)
        for s in range(24):
            label = jnp.where(place == s, labels[s].astype(F32), label)
        out[out.shape[0] - 1] = label.astype(BF)

    leaving = []
    for half in range(2):
        if sent:
            spots = [(z + ahead) & 7, (z - ahead) & 7, (z + 2 * ahead) & 7]
        else:
            spots = [z, z ^ 2]
        width = 16 * len(spots)
        left = jnp.concatenate(
            [
                bras[c, pl.ds(pl.multiple_of(spot * 16, 16), 16), :]
                for c in range(2)
                for spot in spots
            ],
            axis=0,
        )
        copies[half].wait()
        for s in range(12):
            operator = jnp.concatenate(
                [operators[half, s, 0], operators[half, s, 1]], axis=1
            )
            turned = jnp.dot(
                operator, sides[shifts[half * 12 + s]], preferred_element_type=F32
            ).astype(BF)
            kets[half * 12 + s] = jnp.concatenate(
                [
                    jnp.concatenate([turned[:, 0:128], turned[:, 256:384]], axis=1),
                    jnp.concatenate([turned[:, 128:256], turned[:, 384:512]], axis=1),
                ],
                axis=0,
            )
        for group in range(3):
            whole = half * 3 + group
            brackets = [
                jnp.dot(left, kets[whole * 4 + s], preferred_element_type=F32).astype(BF)
                for s in range(4)
            ]
            for i in range(len(spots)):
                rows = jnp.concatenate(
                    [
                        brackets[s][
                            c * width + i * 16 : c * width + i * 16 + 16,
                            kind * 128 : kind * 128 + 128,
                        ][None]
                        for s in range(4)
                        for kind in range(2)
                        for c in range(2)
                    ],
                    axis=0,
                )
                rows = jnp.swapaxes(rows, 0, 1)
                if sent and i == 2:
                    outs[2][whole * SPLIT : whole * SPLIT + SPLIT] = rows[0:SPLIT]
                elif i == 1 and not sent:
                    outs[0][96 + whole * CROSS : 96 + whole * CROSS + CROSS] = rows[SPLIT:16]
                else:
                    outs[i][whole * 16 : whole * 16 + 16] = rows
        if sent:
            for i, out in enumerate(outs):
                middle = TILES[i + 1] // 2
                size = middle + 1 if half else middle
                copy = pltpu.make_async_copy(
                    out.at[pl.ds(middle * half, size)],
                    results[i].at[pl.ds(middle * half, size)],
                    out_sem.at[half, i],
                )
                copy.start()
                leaving.append(copy)
    for copy in leaving:
        copy.wait()


def make_tiles(sent, own_table, far_table, own_wave, far_wave, left_operators, far_left):
    anywhere, whole = pl.BlockSpec(memory_space=pl.ANY), pl.BlockSpec(memory_space=pltpu.VMEM)
    shapes = [(n + 1, 16, 128) for n in (TILES[1:] if sent else TILES[:1])]
    return pl.pallas_call(
        functools.partial(tiles_kernel, sent),
        in_specs=[whole] * 4 + [anywhere] * 2,
        out_specs=[anywhere if sent else whole] * len(shapes),
        out_shape=[jax.ShapeDtypeStruct(shape, BF) for shape in shapes],
        scratch_shapes=[pltpu.VMEM(shape, BF) for shape in shapes if sent]
        + [
            pltpu.VMEM((3, 256, 512), BF),
            pltpu.VMEM((2, 128, 256), BF),
            pltpu.VMEM((24, 256, 256), BF),
            pltpu.VMEM((2, 12, 2, 128, 128), BF),
            pltpu.SemaphoreType.DMA((2,)),
            pltpu.SemaphoreType.DMA((2, 3)),
        ],
        cost_estimate=pl.CostEstimate(
            flops=1000000000, bytes_accessed=4000000, transcendentals=0
        ),
        compiler_params=params(20),
        name="make_tiles" if sent else "make_home",
    )(own_table, far_table, own_wave, far_wave, left_operators, far_left)


def picks_kernel(slot_key, real_key, imag_key, sign, out):
    out[0:384] = (slot_key[...] == real_key[...]).astype(F32).astype(BF)
    out[384:768] = jnp.where(slot_key[...] == imag_key[...], sign[...], 0.0).astype(BF)


def make_picks(keys):
    return pl.pallas_call(
        picks_kernel,
        out_shape=jax.ShapeDtypeStruct((768, 384), BF),
        compiler_params=params(8),
        name="make_picks",
    )(*keys)


def contract_kernel(
    home, ahead1, back1, ahead2, right, right_table, picks, out, paired_ref
):
    arrays = (home, ahead1, back1, ahead2)
    zero = jnp.zeros((96, 128), BF)

    def lefts(a):
        if a >= 16:
            return [home[96 + g * CROSS + a - 16] for g in range(6)] + [zero[0:32]]
        tiles = [ref[g * 16 + a] for ref in arrays[0:3] for g in range(6)]
        if a >= SPLIT:
            return tiles + [zero]
        return tiles + [ahead2[g * SPLIT + a] for g in range(6)]

    def product(start, stop):
        total = 0.0
        for first in range(start, stop, 2):
            pair = range(first, min(first + 2, stop))
            total += lax.dot_general(
                jnp.concatenate([right[:, a].reshape(256, 128) for a in pair], axis=1),
                jnp.concatenate([jnp.concatenate(lefts(a), axis=0) for a in pair], axis=1),
                (((1,), (1,)), ((), ())),
                preferred_element_type=F32,
            )
        return total

    paired = product(0, 16)
    cross = product(16, 16 + CROSS)
    for third in range(3):
        lanes = slice(third * 128, third * 128 + 128)
        paired_ref[third] = paired[:, lanes] + cross if third == 0 else paired[:, lanes]

    slot_label = sum(ref[n].astype(F32) for ref, n in zip(arrays, TILES))
    slot_label = jnp.concatenate([slot_label[i : i + 1] for i in range(3)], axis=1)
    row = iota((128, 128), 0)
    j = row % 32 // 2 * 8 + row // 32 % 2 * 4 + row % 2 * 2 + row // 64
    labels = right_table[pl.ds(where()[3], 1), :].astype(F32)
    right_label = jnp.sum(jnp.where(iota((128, 128), 1) == j, labels, 0.0), axis=1, keepdims=True)
    match = right_label == slot_label

    def part(c):
        rows = [
            jnp.concatenate(
                [paired_ref[third, pl.ds(c * 4 + w * 2 + t, 32, 8), :] for third in range(3)],
                axis=1,
            )
            for t in range(2)
            for w in range(2)
        ]
        return jnp.where(match, jnp.concatenate(rows, axis=0), 0.0)

    rest = jnp.concatenate([part(0), part(1)], axis=1)
    pieces = []
    for _ in range(2):
        pieces.append(rest.astype(BF))
        rest = rest - pieces[-1].astype(F32)
    total = jnp.dot(jnp.concatenate(pieces, axis=0), picks[...], preferred_element_type=F32)
    total = total[0:128] + total[128:256]
    total = total.astype(out.dtype)
    out[...] = jnp.zeros(out.shape, out.dtype)
    for t in range(2):
        for row in range(8):
            out[row, :, t * 48 : t * 48 + 48] = total[
                t * 64 : t * 64 + 64, row * 48 : row * 48 + 48
            ]


def contract(tiles, right, right_table, picks):
    whole = pl.BlockSpec(memory_space=pltpu.VMEM)
    return pl.pallas_call(
        contract_kernel,
        in_specs=[whole] * 7,
        out_specs=whole,
        out_shape=jax.ShapeDtypeStruct((8, 64, 128), BF),
        scratch_shapes=[pltpu.VMEM((3, 256, 128), F32)],
        compiler_params=params(16),
        name="contract",
    )(*tiles, right, right_table, picks)


def ring(step):
    pairs = []
    for z in range(8):
        for core in range(2):
            place = lambda z: ((z % 4) * 2 + core) * 2 + z // 4
            pairs.append((place(z), place(step(z, core))))
    return pairs


def local(
    wave_blocks, left_operators, right_operators, left_table, right_table, assignment, kramers_map
):
    line = ("row", "wf")
    core, z_lo, _, _ = where()
    right, own_wave = pick(right_operators, wave_blocks)
    far_wave = lax.ppermute(
        own_wave, line, ring(lambda z, core: (z + 2) % 8 if z in (2, 3, 6, 7) else (z - 2) % 8)
    )
    swap = [(i, i ^ 1) for i in range(8)]
    far_left = lax.ppermute(left_operators, "row", swap)
    far_table = lax.ppermute(left_table, "row", swap)
    right = lax.all_to_all(right, "col", 0, 0, tiled=True)
    ahead1, back1, ahead2 = make_tiles(
        True, left_table, far_table, own_wave, far_wave, left_operators, far_left
    )
    far_wave, assignment, kramers_map, ahead1 = lax.optimization_barrier(
        (far_wave, assignment, kramers_map, ahead1)
    )
    ahead = lambda steps: ring(lambda z, core: (z + steps * (1 - 2 * core)) % 8)
    arrived = [
        lax.ppermute(ahead1, line, ahead(1)),
        lax.ppermute(back1, line, ahead(-1)),
        lax.ppermute(ahead2, line, ahead(2)),
    ]
    (home,) = make_tiles(
        False, left_table, far_table, own_wave, far_wave, left_operators, far_left
    )
    tiles = [home] + arrived

    held = assignment.reshape(4, 2, 12)
    held = jnp.where(core == 0, held, held[:, ::-1])
    held = lax.dynamic_slice_in_dim(jnp.concatenate([held, held], axis=0), z_lo, 4, 0)
    turned = jnp.concatenate([held[0:1], held[3:4], held[1:3]], axis=0)
    straight = jnp.concatenate([held[0:2], held[3:4], held[2:3]], axis=0)
    held = jnp.where(core == 0, turned, straight).reshape(96, 1)
    slot_key = (held * 4 + jnp.arange(4, dtype=jnp.int32)[None, :]).reshape(384, 1)
    target = jnp.stack([jnp.arange(96, dtype=jnp.int32), kramers_map]).reshape(1, 2, 8, 12)
    target = target.transpose(2, 0, 1, 3)
    kind = jnp.arange(2, dtype=jnp.int32)[None, None, :, None]
    part = jnp.arange(2, dtype=jnp.int32)[None, :, None, None]
    real_key = (target * 4 + kind * 2 + part).reshape(1, 384)
    imag_key = (target * 4 + kind * 2 + 1 - part).reshape(1, 384)
    sign = jnp.broadcast_to((2 * part - 1).astype(F32), (8, 2, 2, 12)).reshape(1, 384)

    picks = make_picks([slot_key, real_key, imag_key, sign])
    shares = contract(tiles, right, right_table.T, picks)
    shares = lax.all_to_all(
        shares.reshape(256, 2, 128), ("row", "wf", "col"), 0, 0, tiled=True
    )
    total = jnp.sum(shares.astype(F32), axis=0)[:, 0:96]
    return total.reshape(2, 2, 2, 2, 12).transpose(2, 3, 4, 0, 1).reshape(2, 2, 12, 4)


def solution(mesh):
    return jax.shard_map(
        local,
        mesh=mesh,
        in_specs=(
            P(None, None, "wf", None),
            P("row", "col", None, None, None),
            P(None, "col", None, "wf", None),
            P("row", None),
            P(),
            P(),
            P(),
        ),
        out_specs=P(None, None, "row", ("col", "wf")),
        check_vma=False,
    )
```

```python
import functools

import jax
import jax.numpy as jnp
from jax import lax
from jax.experimental import pallas as pl
from jax.experimental.pallas import tpu as pltpu
from jax.sharding import PartitionSpec as P

BF = jnp.bfloat16
F32 = jnp.float32


def iota(shape, axis):
    return lax.broadcasted_iota(jnp.int32, shape, axis)


def where():
    row, col, wf = lax.axis_index("row"), lax.axis_index("col"), lax.axis_index("wf")
    return row & 1, row >> 1, wf * 4 + (row >> 1), 2 * col + (row & 1)


def params(mebibytes):
    return pltpu.CompilerParams(vmem_limit_bytes=mebibytes * 1024 * 1024)


SPLIT = 7
CROSS = 16 - SPLIT
ROWS = (16 + CROSS, 16, 16, SPLIT)
TILES = tuple(6 * rows for rows in ROWS)


def pick_kernel(right_ref, wave_ref, result, wave_out, rows_ref, out_ref, sem, out_sem, wave_sem):
    core, z_lo, _, q = where()
    waves = [
        pltpu.make_async_copy(wave_ref.at[:, (q + o) & 31], wave_out.at[:, o], wave_sem.at[o])
        for o in range(3)
    ]
    for copy in waves:
        copy.start()
    copies = []
    for part in range(8):
        for second in range(2):
            copy = pltpu.make_async_copy(
                right_ref.at[pl.ds(part * 2, 2), core, :, :, z_lo ^ (2 * second)],
                rows_ref.at[second, pl.ds(part * 2, 2)],
                sem.at[part, second],
            )
            copy.start()
            copies.append(copy)
    leaving = []
    for part in range(8):
        for second in range(2):
            copies[part * 2 + second].wait()
        for target in range(part * 2, part * 2 + 2):
            for second in range(2):
                rows = jnp.concatenate(
                    [
                        rows_ref[second, target, 4 * w + 2 * h + t, c][None]
                        for h in range(2)
                        for c in range(2)
                        for w in range(2)
                        for t in range(2)
                    ],
                    axis=0,
                )
                rows = jnp.swapaxes(rows, 0, 1)
                if second:
                    out_ref[target, 16 : 16 + CROSS] = rows[SPLIT:16]
                else:
                    out_ref[target, 0:16] = rows
        copy = pltpu.make_async_copy(
            out_ref.at[pl.ds(part * 2, 2)], result.at[pl.ds(part * 2, 2)], out_sem.at[part]
        )
        copy.start()
        leaving.append(copy)
    for copy in waves + leaving:
        copy.wait()


def pick(right_operators, wave_blocks):
    return pl.pallas_call(
        pick_kernel,
        in_specs=[pl.BlockSpec(memory_space=pltpu.HBM)] * 2,
        out_specs=[pl.BlockSpec(memory_space=pl.ANY)] * 2,
        out_shape=[
            jax.ShapeDtypeStruct((16, 16 + CROSS, 16, 128), BF),
            jax.ShapeDtypeStruct((2, 3, 64, 128), BF),
        ],
        scratch_shapes=[
            pltpu.VMEM((2, 16, 8, 2, 16, 128), BF),
            pltpu.VMEM((16, 16 + CROSS, 16, 128), BF),
            pltpu.SemaphoreType.DMA((8, 2)),
            pltpu.SemaphoreType.DMA((8,)),
            pltpu.SemaphoreType.DMA((3,)),
        ],
        compiler_params=params(54),
        name="pick",
    )(right_operators.reshape(16, 2, 8, 2, 4, 16, 128), wave_blocks)


def tiles_kernel(
    sent, own_table, far_table, own_wave, far_wave, own_left, far_left, *refs
):
    count = 3 if sent else 1
    results, outs = refs[:count], refs[count : 2 * count] if sent else refs[:count]
    sides, bras, kets, operators, sem, out_sem = refs[-6:]
    core, _, z, q = where()
    ahead = 1 - 2 * core
    low = z < 4
    copies = [
        pltpu.make_async_copy(own_left.at[:, core], operators.at[0], sem.at[0]),
        pltpu.make_async_copy(far_left.at[:, core], operators.at[1], sem.at[1]),
    ]
    for copy in copies:
        copy.start()

    def wave(c, o):
        mine, other = own_wave[c, o], far_wave[c, o]
        return jnp.concatenate(
            [jnp.where(low, mine, other), jnp.where(low, other, mine)], axis=0
        )

    for o in range(3):
        re, im = wave(0, o), wave(1, o)
        top = jnp.concatenate([re, im, re, im], axis=1)
        bottom = jnp.concatenate([-im, re, im, -re], axis=1)
        sides[o] = jnp.concatenate([top, bottom], axis=0)
        if o == 0:
            re_t, im_t = re.T, im.T
            bras[0] = jnp.concatenate([re_t, im_t], axis=1)
            bras[1] = jnp.concatenate([-im_t, re_t], axis=1)

    columns = [
        jnp.sum(jnp.where(iota((12, 32), 1) == q, table[...], 0), axis=1, keepdims=True)
        for table in (own_table, far_table)
    ]
    labels = [column[s, 0] for column in columns for s in range(12)]
    shifts = [lax.rem(label - q + 32, 32) for label in labels]
    for i, out in enumerate(outs):
        start = 96 * (i + 1 if sent else 0)
        place = (iota((16, 128), 0) * 128 + iota((16, 128), 1) - start) >> 2
        label = jnp.zeros((16, 128), F32)
        for s in range(24):
            label = jnp.where(place == s, labels[s].astype(F32), label)
        out[out.shape[0] - 1] = label.astype(BF)

    leaving = []
    for half in range(2):
        if sent:
            spots = [(z + ahead) & 7, (z - ahead) & 7, (z + 2 * ahead) & 7]
        else:
            spots = [z, z ^ 2]
        width = 16 * len(spots)
        left = jnp.concatenate(
            [
                bras[c, pl.ds(pl.multiple_of(spot * 16, 16), 16), :]
                for c in range(2)
                for spot in spots
            ],
            axis=0,
        )
        copies[half].wait()
        for s in range(12):
            operator = jnp.concatenate(
                [operators[half, s, 0], operators[half, s, 1]], axis=1
            )
            turned = jnp.dot(
                operator, sides[shifts[half * 12 + s]], preferred_element_type=F32
            ).astype(BF)
            kets[half * 12 + s] = jnp.concatenate(
                [
                    jnp.concatenate([turned[:, 0:128], turned[:, 256:384]], axis=1),
                    jnp.concatenate([turned[:, 128:256], turned[:, 384:512]], axis=1),
                ],
                axis=0,
            )
        for group in range(3):
            whole = half * 3 + group
            brackets = [
                jnp.dot(left, kets[whole * 4 + s], preferred_element_type=F32).astype(BF)
                for s in range(4)
            ]
            for i in range(len(spots)):
                rows = jnp.concatenate(
                    [
                        brackets[s][
                            c * width + i * 16 : c * width + i * 16 + 16,
                            kind * 128 : kind * 128 + 128,
                        ][None]
                        for s in range(4)
                        for kind in range(2)
                        for c in range(2)
                    ],
                    axis=0,
                )
                rows = jnp.swapaxes(rows, 0, 1)
                if sent and i == 2:
                    outs[2][whole * SPLIT : whole * SPLIT + SPLIT] = rows[0:SPLIT]
                elif i == 1 and not sent:
                    outs[0][96 + whole * CROSS : 96 + whole * CROSS + CROSS] = rows[SPLIT:16]
                else:
                    outs[i][whole * 16 : whole * 16 + 16] = rows
        if sent:
            for i, out in enumerate(outs):
                middle = TILES[i + 1] // 2
                size = middle + 1 if half else middle
                copy = pltpu.make_async_copy(
                    out.at[pl.ds(middle * half, size)],
                    results[i].at[pl.ds(middle * half, size)],
                    out_sem.at[half, i],
                )
                copy.start()
                leaving.append(copy)
    for copy in leaving:
        copy.wait()


def make_tiles(sent, own_table, far_table, own_wave, far_wave, left_operators, far_left):
    anywhere, whole = pl.BlockSpec(memory_space=pl.ANY), pl.BlockSpec(memory_space=pltpu.VMEM)
    shapes = [(n + 1, 16, 128) for n in (TILES[1:] if sent else TILES[:1])]
    return pl.pallas_call(
        functools.partial(tiles_kernel, sent),
        in_specs=[whole] * 4 + [anywhere] * 2,
        out_specs=[anywhere if sent else whole] * len(shapes),
        out_shape=[jax.ShapeDtypeStruct(shape, BF) for shape in shapes],
        scratch_shapes=[pltpu.VMEM(shape, BF) for shape in shapes if sent]
        + [
            pltpu.VMEM((3, 256, 512), BF),
            pltpu.VMEM((2, 128, 256), BF),
            pltpu.VMEM((24, 256, 256), BF),
            pltpu.VMEM((2, 12, 2, 128, 128), BF),
            pltpu.SemaphoreType.DMA((2,)),
            pltpu.SemaphoreType.DMA((2, 3)),
        ],
        cost_estimate=pl.CostEstimate(
            flops=1000000000, bytes_accessed=4000000, transcendentals=0
        ),
        compiler_params=params(20),
        name="make_tiles" if sent else "make_home",
    )(own_table, far_table, own_wave, far_wave, left_operators, far_left)


def picks_kernel(slot_key, real_key, imag_key, sign, out):
    out[0:384] = (slot_key[...] == real_key[...]).astype(F32).astype(BF)
    out[384:768] = jnp.where(slot_key[...] == imag_key[...], sign[...], 0.0).astype(BF)


def make_picks(keys):
    return pl.pallas_call(
        picks_kernel,
        out_shape=jax.ShapeDtypeStruct((768, 384), BF),
        compiler_params=params(8),
        name="make_picks",
    )(*keys)


def contract_kernel(
    home, ahead1, back1_ref, ahead2, right, right_table, picks, out, paired_ref, back1, sem
):
    arriving = pltpu.make_async_copy(back1_ref, back1, sem.at[0])
    arriving.start()
    arrays = (home, ahead1, back1, ahead2)
    zero = jnp.zeros((96, 128), BF)

    def lefts(a):
        if a >= 16:
            return [home[96 + g * CROSS + a - 16] for g in range(6)] + [zero[0:32]]
        tiles = [ref[g * 16 + a] for ref in arrays[0:3] for g in range(6)]
        if a >= SPLIT:
            return tiles + [zero]
        return tiles + [ahead2[g * SPLIT + a] for g in range(6)]

    def product(start, stop):
        total = 0.0
        for first in range(start, stop, 2):
            pair = range(first, min(first + 2, stop))
            total += lax.dot_general(
                jnp.concatenate([right[:, a].reshape(256, 128) for a in pair], axis=1),
                jnp.concatenate([jnp.concatenate(lefts(a), axis=0) for a in pair], axis=1),
                (((1,), (1,)), ((), ())),
                preferred_element_type=F32,
            )
        return total

    cross = product(16, 16 + CROSS)
    arriving.wait()
    paired = product(0, 16)
    for third in range(3):
        lanes = slice(third * 128, third * 128 + 128)
        paired_ref[third] = paired[:, lanes] + cross if third == 0 else paired[:, lanes]

    slot_label = sum(ref[n].astype(F32) for ref, n in zip(arrays, TILES))
    slot_label = jnp.concatenate([slot_label[i : i + 1] for i in range(3)], axis=1)
    row = iota((128, 128), 0)
    j = row % 32 // 2 * 8 + row // 32 % 2 * 4 + row % 2 * 2 + row // 64
    labels = right_table[pl.ds(where()[3], 1), :].astype(F32)
    right_label = jnp.sum(jnp.where(iota((128, 128), 1) == j, labels, 0.0), axis=1, keepdims=True)
    match = right_label == slot_label

    def part(c):
        rows = [
            jnp.concatenate(
                [paired_ref[third, pl.ds(c * 4 + w * 2 + t, 32, 8), :] for third in range(3)],
                axis=1,
            )
            for t in range(2)
            for w in range(2)
        ]
        return jnp.where(match, jnp.concatenate(rows, axis=0), 0.0)

    rest = jnp.concatenate([part(0), part(1)], axis=1)
    pieces = []
    for _ in range(2):
        pieces.append(rest.astype(BF))
        rest = rest - pieces[-1].astype(F32)
    total = jnp.dot(jnp.concatenate(pieces, axis=0), picks[...], preferred_element_type=F32)
    total = total[0:128] + total[128:256]
    total = total.astype(out.dtype)
    out[...] = jnp.zeros(out.shape, out.dtype)
    for t in range(2):
        for row in range(8):
            out[row, :, t * 48 : t * 48 + 48] = total[
                t * 64 : t * 64 + 64, row * 48 : row * 48 + 48
            ]


def contract(tiles, right, right_table, picks):
    whole = pl.BlockSpec(memory_space=pltpu.VMEM)
    return pl.pallas_call(
        contract_kernel,
        in_specs=[whole] * 2 + [pl.BlockSpec(memory_space=pl.ANY)] + [whole] * 4,
        out_specs=whole,
        out_shape=jax.ShapeDtypeStruct((8, 64, 128), BF),
        scratch_shapes=[
            pltpu.VMEM((3, 256, 128), F32),
            pltpu.VMEM((TILES[2] + 1, 16, 128), BF),
            pltpu.SemaphoreType.DMA((1,)),
        ],
        compiler_params=params(16),
        name="contract",
    )(*tiles, right, right_table, picks)


def ring(step):
    pairs = []
    for z in range(8):
        for core in range(2):
            place = lambda z: ((z % 4) * 2 + core) * 2 + z // 4
            pairs.append((place(z), place(step(z, core))))
    return pairs


def local(
    wave_blocks, left_operators, right_operators, left_table, right_table, assignment, kramers_map
):
    line = ("row", "wf")
    core, z_lo, _, _ = where()
    right, own_wave = pick(right_operators, wave_blocks)
    far_wave = lax.ppermute(
        own_wave, line, ring(lambda z, core: (z + 2) % 8 if z in (2, 3, 6, 7) else (z - 2) % 8)
    )
    swap = [(i, i ^ 1) for i in range(8)]
    far_left = lax.ppermute(left_operators, "row", swap)
    far_table = lax.ppermute(left_table, "row", swap)
    right = lax.all_to_all(right, "col", 0, 0, tiled=True)
    ahead1, back1, ahead2 = make_tiles(
        True, left_table, far_table, own_wave, far_wave, left_operators, far_left
    )
    far_wave, assignment, kramers_map, ahead1 = lax.optimization_barrier(
        (far_wave, assignment, kramers_map, ahead1)
    )
    ahead = lambda steps: ring(lambda z, core: (z + steps * (1 - 2 * core)) % 8)
    arrived = [
        lax.ppermute(ahead1, line, ahead(1)),
        lax.ppermute(back1, line, ahead(-1)),
        lax.ppermute(ahead2, line, ahead(2)),
    ]
    (home,) = make_tiles(
        False, left_table, far_table, own_wave, far_wave, left_operators, far_left
    )
    tiles = [home] + arrived

    held = assignment.reshape(4, 2, 12)
    held = jnp.where(core == 0, held, held[:, ::-1])
    held = lax.dynamic_slice_in_dim(jnp.concatenate([held, held], axis=0), z_lo, 4, 0)
    turned = jnp.concatenate([held[0:1], held[3:4], held[1:3]], axis=0)
    straight = jnp.concatenate([held[0:2], held[3:4], held[2:3]], axis=0)
    held = jnp.where(core == 0, turned, straight).reshape(96, 1)
    slot_key = (held * 4 + jnp.arange(4, dtype=jnp.int32)[None, :]).reshape(384, 1)
    target = jnp.stack([jnp.arange(96, dtype=jnp.int32), kramers_map]).reshape(1, 2, 8, 12)
    target = target.transpose(2, 0, 1, 3)
    kind = jnp.arange(2, dtype=jnp.int32)[None, None, :, None]
    part = jnp.arange(2, dtype=jnp.int32)[None, :, None, None]
    real_key = (target * 4 + kind * 2 + part).reshape(1, 384)
    imag_key = (target * 4 + kind * 2 + 1 - part).reshape(1, 384)
    sign = jnp.broadcast_to((2 * part - 1).astype(F32), (8, 2, 2, 12)).reshape(1, 384)

    picks = make_picks([slot_key, real_key, imag_key, sign])
    shares = contract(tiles, right, right_table.T, picks)
    shares = lax.all_to_all(
        shares.reshape(256, 2, 128), ("row", "wf", "col"), 0, 0, tiled=True
    )
    total = jnp.sum(shares.astype(F32), axis=0)[:, 0:96]
    return total.reshape(2, 2, 2, 2, 12).transpose(2, 3, 4, 0, 1).reshape(2, 2, 12, 4)


def solution(mesh):
    return jax.shard_map(
        local,
        mesh=mesh,
        in_specs=(
            P(None, None, "wf", None),
            P("row", "col", None, None, None),
            P(None, "col", None, "wf", None),
            P("row", None),
            P(),
            P(),
            P(),
        ),
        out_specs=P(None, None, "row", ("col", "wf")),
        check_vma=False,
    )
```

```python
import functools

import jax
import jax.numpy as jnp
from jax import lax
from jax.experimental import pallas as pl
from jax.experimental.pallas import tpu as pltpu
from jax.sharding import PartitionSpec as P

BF = jnp.bfloat16
F32 = jnp.float32


def iota(shape, axis):
    return lax.broadcasted_iota(jnp.int32, shape, axis)


def where():
    row, col, wf = lax.axis_index("row"), lax.axis_index("col"), lax.axis_index("wf")
    return row & 1, row >> 1, wf * 4 + (row >> 1), 2 * col + (row & 1)


def params(mebibytes):
    return pltpu.CompilerParams(vmem_limit_bytes=mebibytes * 1024 * 1024)


SPLIT = 7
CROSS = 16 - SPLIT
ROWS = (16 + CROSS, 16, 16, SPLIT)
TILES = tuple(6 * rows for rows in ROWS)


def pick_kernel(right_ref, wave_ref, result, wave_out, rows_ref, out_ref, sem, out_sem, wave_sem):
    core, z_lo, _, q = where()
    waves = [
        pltpu.make_async_copy(wave_ref.at[:, (q + o) & 31], wave_out.at[:, o], wave_sem.at[o])
        for o in range(3)
    ]
    for copy in waves:
        copy.start()
    copies = []
    for part in range(4):
        for second in range(2):
            copy = pltpu.make_async_copy(
                right_ref.at[pl.ds(part * 4, 4), core, :, :, z_lo ^ (2 * second)],
                rows_ref.at[second, pl.ds(part * 4, 4)],
                sem.at[part, second],
            )
            copy.start()
            copies.append(copy)
    leaving = []
    for part in range(4):
        for second in range(2):
            copies[part * 2 + second].wait()
        for target in range(part * 4, part * 4 + 4):
            for second in range(2):
                rows = jnp.concatenate(
                    [
                        rows_ref[second, target, 4 * w + 2 * h + t, c][None]
                        for h in range(2)
                        for c in range(2)
                        for w in range(2)
                        for t in range(2)
                    ],
                    axis=0,
                )
                rows = jnp.swapaxes(rows, 0, 1)
                if second:
                    out_ref[target, 16 : 16 + CROSS] = rows[SPLIT:16]
                else:
                    out_ref[target, 0:16] = rows
        copy = pltpu.make_async_copy(
            out_ref.at[pl.ds(part * 4, 4)], result.at[pl.ds(part * 4, 4)], out_sem.at[part]
        )
        copy.start()
        leaving.append(copy)
    for copy in waves + leaving:
        copy.wait()


def pick(right_operators, wave_blocks):
    whole = pl.BlockSpec(memory_space=pltpu.VMEM)
    return pl.pallas_call(
        pick_kernel,
        in_specs=[pl.BlockSpec(memory_space=pltpu.HBM)] * 2,
        out_specs=[pl.BlockSpec(memory_space=pl.ANY), whole],
        out_shape=[
            jax.ShapeDtypeStruct((16, 16 + CROSS, 16, 128), BF),
            jax.ShapeDtypeStruct((2, 3, 64, 128), BF),
        ],
        scratch_shapes=[
            pltpu.VMEM((2, 16, 8, 2, 16, 128), BF),
            pltpu.VMEM((16, 16 + CROSS, 16, 128), BF),
            pltpu.SemaphoreType.DMA((4, 2)),
            pltpu.SemaphoreType.DMA((4,)),
            pltpu.SemaphoreType.DMA((3,)),
        ],
        compiler_params=params(54),
        name="pick",
    )(right_operators.reshape(16, 2, 8, 2, 4, 16, 128), wave_blocks)


def tiles_kernel(
    sent, own_table, far_table, own_wave, far_wave, own_left, far_left, *refs
):
    count = 3 if sent else 1
    results, outs = refs[:count], refs[count : 2 * count] if sent else refs[:count]
    sides, bras, kets, operators, sem, out_sem = refs[-6:]
    core, _, z, q = where()
    ahead = 1 - 2 * core
    low = z < 4
    copies = [
        pltpu.make_async_copy(own_left.at[:, core], operators.at[0], sem.at[0]),
        pltpu.make_async_copy(far_left.at[:, core], operators.at[1], sem.at[1]),
    ]
    for copy in copies:
        copy.start()

    def wave(c, o):
        mine, other = own_wave[c, o], far_wave[c, o]
        return jnp.concatenate(
            [jnp.where(low, mine, other), jnp.where(low, other, mine)], axis=0
        )

    for o in range(3):
        re, im = wave(0, o), wave(1, o)
        top = jnp.concatenate([re, im, re, im], axis=1)
        bottom = jnp.concatenate([-im, re, im, -re], axis=1)
        sides[o] = jnp.concatenate([top, bottom], axis=0)
        if o == 0:
            re_t, im_t = re.T, im.T
            bras[0] = jnp.concatenate([re_t, im_t], axis=1)
            bras[1] = jnp.concatenate([-im_t, re_t], axis=1)

    columns = [
        jnp.sum(jnp.where(iota((12, 32), 1) == q, table[...], 0), axis=1, keepdims=True)
        for table in (own_table, far_table)
    ]
    labels = [column[s, 0] for column in columns for s in range(12)]
    shifts = [lax.rem(label - q + 32, 32) for label in labels]
    for i, out in enumerate(outs):
        start = 96 * (i + 1 if sent else 0)
        place = (iota((16, 128), 0) * 128 + iota((16, 128), 1) - start) >> 2
        label = jnp.zeros((16, 128), F32)
        for s in range(24):
            label = jnp.where(place == s, labels[s].astype(F32), label)
        out[out.shape[0] - 1] = label.astype(BF)

    leaving = []
    for half in range(2):
        if sent:
            spots = [(z + ahead) & 7, (z - ahead) & 7, (z + 2 * ahead) & 7]
        else:
            spots = [z, z ^ 2]
        width = 16 * len(spots)
        left = jnp.concatenate(
            [
                bras[c, pl.ds(pl.multiple_of(spot * 16, 16), 16), :]
                for c in range(2)
                for spot in spots
            ],
            axis=0,
        )
        copies[half].wait()
        for s in range(12):
            operator = jnp.concatenate(
                [operators[half, s, 0], operators[half, s, 1]], axis=1
            )
            turned = jnp.dot(
                operator, sides[shifts[half * 12 + s]], preferred_element_type=F32
            ).astype(BF)
            kets[half * 12 + s] = jnp.concatenate(
                [
                    jnp.concatenate([turned[:, 0:128], turned[:, 256:384]], axis=1),
                    jnp.concatenate([turned[:, 128:256], turned[:, 384:512]], axis=1),
                ],
                axis=0,
            )
        for group in range(3):
            whole = half * 3 + group
            brackets = [
                jnp.dot(left, kets[whole * 4 + s], preferred_element_type=F32).astype(BF)
                for s in range(4)
            ]
            for i in range(len(spots)):
                rows = jnp.concatenate(
                    [
                        brackets[s][
                            c * width + i * 16 : c * width + i * 16 + 16,
                            kind * 128 : kind * 128 + 128,
                        ][None]
                        for s in range(4)
                        for kind in range(2)
                        for c in range(2)
                    ],
                    axis=0,
                )
                rows = jnp.swapaxes(rows, 0, 1)
                if sent and i == 2:
                    outs[2][whole * SPLIT : whole * SPLIT + SPLIT] = rows[0:SPLIT]
                elif i == 1 and not sent:
                    outs[0][96 + whole * CROSS : 96 + whole * CROSS + CROSS] = rows[SPLIT:16]
                else:
                    outs[i][whole * 16 : whole * 16 + 16] = rows
        if sent:
            for i, out in enumerate(outs):
                middle = TILES[i + 1] // 2
                size = middle + 1 if half else middle
                copy = pltpu.make_async_copy(
                    out.at[pl.ds(middle * half, size)],
                    results[i].at[pl.ds(middle * half, size)],
                    out_sem.at[half, i],
                )
                copy.start()
                leaving.append(copy)
    for copy in leaving:
        copy.wait()


def make_tiles(sent, own_table, far_table, own_wave, far_wave, left_operators, far_left):
    anywhere, whole = pl.BlockSpec(memory_space=pl.ANY), pl.BlockSpec(memory_space=pltpu.VMEM)
    shapes = [(n + 1, 16, 128) for n in (TILES[1:] if sent else TILES[:1])]
    return pl.pallas_call(
        functools.partial(tiles_kernel, sent),
        in_specs=[whole] * 4 + [anywhere] * 2,
        out_specs=[anywhere if sent else whole] * len(shapes),
        out_shape=[jax.ShapeDtypeStruct(shape, BF) for shape in shapes],
        scratch_shapes=[pltpu.VMEM(shape, BF) for shape in shapes if sent]
        + [
            pltpu.VMEM((3, 256, 512), BF),
            pltpu.VMEM((2, 128, 256), BF),
            pltpu.VMEM((24, 256, 256), BF),
            pltpu.VMEM((2, 12, 2, 128, 128), BF),
            pltpu.SemaphoreType.DMA((2,)),
            pltpu.SemaphoreType.DMA((2, 3)),
        ],
        cost_estimate=pl.CostEstimate(
            flops=1000000000, bytes_accessed=4000000, transcendentals=0
        ),
        compiler_params=params(20),
        name="make_tiles" if sent else "make_home",
    )(own_table, far_table, own_wave, far_wave, left_operators, far_left)


def picks_kernel(slot_key, real_key, imag_key, sign, out):
    out[0:384] = (slot_key[...] == real_key[...]).astype(F32).astype(BF)
    out[384:768] = jnp.where(slot_key[...] == imag_key[...], sign[...], 0.0).astype(BF)


def make_picks(keys):
    return pl.pallas_call(
        picks_kernel,
        out_shape=jax.ShapeDtypeStruct((768, 384), BF),
        compiler_params=params(8),
        name="make_picks",
    )(*keys)


def contract_kernel(
    home, ahead1, back1, ahead2, right, right_table, picks, out, paired_ref
):
    arrays = (home, ahead1, back1, ahead2)
    zero = jnp.zeros((96, 128), BF)

    def lefts(a):
        if a >= 16:
            return [home[96 + g * CROSS + a - 16] for g in range(6)] + [zero[0:32]]
        tiles = [ref[g * 16 + a] for ref in arrays[0:3] for g in range(6)]
        if a >= SPLIT:
            return tiles + [zero]
        return tiles + [ahead2[g * SPLIT + a] for g in range(6)]

    def product(start, stop):
        total = 0.0
        for first in range(start, stop, 2):
            pair = range(first, min(first + 2, stop))
            total += lax.dot_general(
                jnp.concatenate([right[:, a].reshape(256, 128) for a in pair], axis=1),
                jnp.concatenate([jnp.concatenate(lefts(a), axis=0) for a in pair], axis=1),
                (((1,), (1,)), ((), ())),
                preferred_element_type=F32,
            )
        return total

    paired = product(0, 16)
    cross = product(16, 16 + CROSS)
    for third in range(3):
        lanes = slice(third * 128, third * 128 + 128)
        paired_ref[third] = paired[:, lanes] + cross if third == 0 else paired[:, lanes]

    slot_label = sum(ref[n].astype(F32) for ref, n in zip(arrays, TILES))
    slot_label = jnp.concatenate([slot_label[i : i + 1] for i in range(3)], axis=1)
    row = iota((128, 128), 0)
    j = row % 32 // 2 * 8 + row // 32 % 2 * 4 + row % 2 * 2 + row // 64
    labels = right_table[pl.ds(where()[3], 1), :].astype(F32)
    right_label = jnp.sum(jnp.where(iota((128, 128), 1) == j, labels, 0.0), axis=1, keepdims=True)
    match = right_label == slot_label

    def part(c):
        rows = [
            jnp.concatenate(
                [paired_ref[third, pl.ds(c * 4 + w * 2 + t, 32, 8), :] for third in range(3)],
                axis=1,
            )
            for t in range(2)
            for w in range(2)
        ]
        return jnp.where(match, jnp.concatenate(rows, axis=0), 0.0)

    rest = jnp.concatenate([part(0), part(1)], axis=1)
    pieces = []
    for _ in range(2):
        pieces.append(rest.astype(BF))
        rest = rest - pieces[-1].astype(F32)
    total = jnp.dot(jnp.concatenate(pieces, axis=0), picks[...], preferred_element_type=F32)
    total = total[0:128] + total[128:256]
    total = total.astype(out.dtype)
    out[...] = jnp.zeros(out.shape, out.dtype)
    for t in range(2):
        for row in range(8):
            out[row, :, t * 48 : t * 48 + 48] = total[
                t * 64 : t * 64 + 64, row * 48 : row * 48 + 48
            ]


def contract(tiles, right, right_table, picks):
    whole = pl.BlockSpec(memory_space=pltpu.VMEM)
    return pl.pallas_call(
        contract_kernel,
        in_specs=[whole] * 7,
        out_specs=whole,
        out_shape=jax.ShapeDtypeStruct((8, 64, 128), BF),
        scratch_shapes=[pltpu.VMEM((3, 256, 128), F32)],
        compiler_params=params(16),
        name="contract",
    )(*tiles, right, right_table, picks)


def ring(step):
    pairs = []
    for z in range(8):
        for core in range(2):
            place = lambda z: ((z % 4) * 2 + core) * 2 + z // 4
            pairs.append((place(z), place(step(z, core))))
    return pairs


def local(
    wave_blocks, left_operators, right_operators, left_table, right_table, assignment, kramers_map
):
    line = ("row", "wf")
    core, z_lo, _, _ = where()
    right, own_wave = pick(right_operators, wave_blocks)
    far_wave = lax.ppermute(
        own_wave, line, ring(lambda z, core: (z + 2) % 8 if z in (2, 3, 6, 7) else (z - 2) % 8)
    )
    swap = [(i, i ^ 1) for i in range(8)]
    far_left = lax.ppermute(left_operators, "row", swap)
    far_table = lax.ppermute(left_table, "row", swap)
    right = lax.all_to_all(right, "col", 0, 0, tiled=True)
    ahead1, back1, ahead2 = make_tiles(
        True, left_table, far_table, own_wave, far_wave, left_operators, far_left
    )
    far_wave, assignment, kramers_map, ahead1 = lax.optimization_barrier(
        (far_wave, assignment, kramers_map, ahead1)
    )
    ahead = lambda steps: ring(lambda z, core: (z + steps * (1 - 2 * core)) % 8)
    arrived = [
        lax.ppermute(ahead1, line, ahead(1)),
        lax.ppermute(back1, line, ahead(-1)),
        lax.ppermute(ahead2, line, ahead(2)),
    ]
    (home,) = make_tiles(
        False, left_table, far_table, own_wave, far_wave, left_operators, far_left
    )
    tiles = [home] + arrived

    held = assignment.reshape(4, 2, 12)
    held = jnp.where(core == 0, held, held[:, ::-1])
    held = lax.dynamic_slice_in_dim(jnp.concatenate([held, held], axis=0), z_lo, 4, 0)
    turned = jnp.concatenate([held[0:1], held[3:4], held[1:3]], axis=0)
    straight = jnp.concatenate([held[0:2], held[3:4], held[2:3]], axis=0)
    held = jnp.where(core == 0, turned, straight).reshape(96, 1)
    slot_key = (held * 4 + jnp.arange(4, dtype=jnp.int32)[None, :]).reshape(384, 1)
    target = jnp.stack([jnp.arange(96, dtype=jnp.int32), kramers_map]).reshape(1, 2, 8, 12)
    target = target.transpose(2, 0, 1, 3)
    kind = jnp.arange(2, dtype=jnp.int32)[None, None, :, None]
    part = jnp.arange(2, dtype=jnp.int32)[None, :, None, None]
    real_key = (target * 4 + kind * 2 + part).reshape(1, 384)
    imag_key = (target * 4 + kind * 2 + 1 - part).reshape(1, 384)
    sign = jnp.broadcast_to((2 * part - 1).astype(F32), (8, 2, 2, 12)).reshape(1, 384)

    picks = make_picks([slot_key, real_key, imag_key, sign])
    shares = contract(tiles, right, right_table.T, picks)
    shares = lax.all_to_all(
        shares.reshape(256, 2, 128), ("row", "wf", "col"), 0, 0, tiled=True
    )
    total = jnp.sum(shares.astype(F32), axis=0)[:, 0:96]
    return total.reshape(2, 2, 2, 2, 12).transpose(2, 3, 4, 0, 1).reshape(2, 2, 12, 4)


def solution(mesh):
    return jax.shard_map(
        local,
        mesh=mesh,
        in_specs=(
            P(None, None, "wf", None),
            P("row", "col", None, None, None),
            P(None, "col", None, "wf", None),
            P("row", None),
            P(),
            P(),
            P(),
        ),
        out_specs=P(None, None, "row", ("col", "wf")),
        check_vma=False,
    )
```

```python
import functools

import jax
import jax.numpy as jnp
from jax import lax
from jax.experimental import pallas as pl
from jax.experimental.pallas import tpu as pltpu
from jax.sharding import PartitionSpec as P

BF = jnp.bfloat16
F32 = jnp.float32


def iota(shape, axis):
    return lax.broadcasted_iota(jnp.int32, shape, axis)


def where():
    row, col, wf = lax.axis_index("row"), lax.axis_index("col"), lax.axis_index("wf")
    return row & 1, row >> 1, wf * 4 + (row >> 1), 2 * col + (row & 1)


def params(mebibytes):
    return pltpu.CompilerParams(vmem_limit_bytes=mebibytes * 1024 * 1024)


SPLIT = 7
CROSS = 16 - SPLIT
ROWS = (16 + CROSS, 16, 16, SPLIT)
TILES = tuple(6 * rows for rows in ROWS)


def pick_kernel(right_ref, wave_ref, out_ref, wave_out, rows_ref, sem, wave_sem):
    core, z_lo, _, q = where()
    waves = [
        pltpu.make_async_copy(wave_ref.at[:, (q + o) & 31], wave_out.at[:, o], wave_sem.at[o])
        for o in range(3)
    ]
    for copy in waves:
        copy.start()
    copies = []
    for part in range(4):
        for second in range(2):
            copy = pltpu.make_async_copy(
                right_ref.at[pl.ds(part * 4, 4), core, :, :, z_lo ^ (2 * second)],
                rows_ref.at[second, pl.ds(part * 4, 4)],
                sem.at[part, second],
            )
            copy.start()
            copies.append(copy)
    for part in range(4):
        for second in range(2):
            copies[part * 2 + second].wait()
        for target in range(part * 4, part * 4 + 4):
            for second in range(2):
                rows = jnp.concatenate(
                    [
                        rows_ref[second, target, 4 * w + 2 * h + t, c][None]
                        for h in range(2)
                        for c in range(2)
                        for w in range(2)
                        for t in range(2)
                    ],
                    axis=0,
                )
                rows = jnp.swapaxes(rows, 0, 1)
                if second:
                    out_ref[target, 16 : 16 + CROSS] = rows[SPLIT:16]
                else:
                    out_ref[target, 0:16] = rows
    for copy in waves:
        copy.wait()


def pick(right_operators, wave_blocks):
    whole = pl.BlockSpec(memory_space=pltpu.VMEM)
    return pl.pallas_call(
        pick_kernel,
        in_specs=[pl.BlockSpec(memory_space=pltpu.HBM)] * 2,
        out_specs=[whole] * 2,
        out_shape=[
            jax.ShapeDtypeStruct((16, 16 + CROSS, 16, 128), BF),
            jax.ShapeDtypeStruct((2, 3, 64, 128), BF),
        ],
        scratch_shapes=[
            pltpu.VMEM((2, 16, 8, 2, 16, 128), BF),
            pltpu.SemaphoreType.DMA((4, 2)),
            pltpu.SemaphoreType.DMA((3,)),
        ],
        compiler_params=params(54),
        name="pick",
    )(right_operators.reshape(16, 2, 8, 2, 4, 16, 128), wave_blocks)


def tiles_kernel(
    sent, own_table, far_table, own_wave, far_wave, own_left, far_left, *refs
):
    count = 3 if sent else 1
    results, outs = refs[:count], refs[count : 2 * count] if sent else refs[:count]
    sides, bras, kets, operators, sem, out_sem = refs[-6:]
    core, _, z, q = where()
    ahead = 1 - 2 * core
    low = z < 4
    copies = [
        pltpu.make_async_copy(own_left.at[:, core], operators.at[0], sem.at[0]),
        pltpu.make_async_copy(far_left.at[:, core], operators.at[1], sem.at[1]),
    ]
    for copy in copies:
        copy.start()

    def wave(c, o):
        mine, other = own_wave[c, o], far_wave[c, o]
        return jnp.concatenate(
            [jnp.where(low, mine, other), jnp.where(low, other, mine)], axis=0
        )

    for o in range(3):
        re, im = wave(0, o), wave(1, o)
        top = jnp.concatenate([re, im, re, im], axis=1)
        bottom = jnp.concatenate([-im, re, im, -re], axis=1)
        sides[o] = jnp.concatenate([top, bottom], axis=0)
        if o == 0:
            re_t, im_t = re.T, im.T
            bras[0] = jnp.concatenate([re_t, im_t], axis=1)
            bras[1] = jnp.concatenate([-im_t, re_t], axis=1)

    columns = [
        jnp.sum(jnp.where(iota((12, 32), 1) == q, table[...], 0), axis=1, keepdims=True)
        for table in (own_table, far_table)
    ]
    labels = [column[s, 0] for column in columns for s in range(12)]
    shifts = [lax.rem(label - q + 32, 32) for label in labels]
    for i, out in enumerate(outs):
        start = 96 * (i + 1 if sent else 0)
        place = (iota((16, 128), 0) * 128 + iota((16, 128), 1) - start) >> 2
        label = jnp.zeros((16, 128), F32)
        for s in range(24):
            label = jnp.where(place == s, labels[s].astype(F32), label)
        out[out.shape[0] - 1] = label.astype(BF)

    leaving = []
    for half in range(2):
        if sent:
            spots = [(z + ahead) & 7, (z - ahead) & 7, (z + 2 * ahead) & 7]
        else:
            spots = [z, z ^ 2]
        width = 16 * len(spots)
        left = jnp.concatenate(
            [
                bras[c, pl.ds(pl.multiple_of(spot * 16, 16), 16), :]
                for c in range(2)
                for spot in spots
            ],
            axis=0,
        )
        copies[half].wait()
        for s in range(12):
            operator = jnp.concatenate(
                [operators[half, s, 0], operators[half, s, 1]], axis=1
            )
            turned = jnp.dot(
                operator, sides[shifts[half * 12 + s]], preferred_element_type=F32
            ).astype(BF)
            kets[half * 12 + s] = jnp.concatenate(
                [
                    jnp.concatenate([turned[:, 0:128], turned[:, 256:384]], axis=1),
                    jnp.concatenate([turned[:, 128:256], turned[:, 384:512]], axis=1),
                ],
                axis=0,
            )
        for group in range(3):
            whole = half * 3 + group
            brackets = [
                jnp.dot(left, kets[whole * 4 + s], preferred_element_type=F32).astype(BF)
                for s in range(4)
            ]
            for i in range(len(spots)):
                rows = jnp.concatenate(
                    [
                        brackets[s][
                            c * width + i * 16 : c * width + i * 16 + 16,
                            kind * 128 : kind * 128 + 128,
                        ][None]
                        for s in range(4)
                        for kind in range(2)
                        for c in range(2)
                    ],
                    axis=0,
                )
                rows = jnp.swapaxes(rows, 0, 1)
                if sent and i == 2:
                    outs[2][whole * SPLIT : whole * SPLIT + SPLIT] = rows[0:SPLIT]
                elif i == 1 and not sent:
                    outs[0][96 + whole * CROSS : 96 + whole * CROSS + CROSS] = rows[SPLIT:16]
                else:
                    outs[i][whole * 16 : whole * 16 + 16] = rows
        if sent:
            for i, out in enumerate(outs):
                middle = TILES[i + 1] // 2
                size = middle + 1 if half else middle
                copy = pltpu.make_async_copy(
                    out.at[pl.ds(middle * half, size)],
                    results[i].at[pl.ds(middle * half, size)],
                    out_sem.at[half, i],
                )
                copy.start()
                leaving.append(copy)
    for copy in leaving:
        copy.wait()


def make_tiles(sent, own_table, far_table, own_wave, far_wave, left_operators, far_left):
    anywhere, whole = pl.BlockSpec(memory_space=pl.ANY), pl.BlockSpec(memory_space=pltpu.VMEM)
    shapes = [(n + 1, 16, 128) for n in (TILES[1:] if sent else TILES[:1])]
    return pl.pallas_call(
        functools.partial(tiles_kernel, sent),
        in_specs=[whole] * 4 + [anywhere] * 2,
        out_specs=[anywhere if sent else whole] * len(shapes),
        out_shape=[jax.ShapeDtypeStruct(shape, BF) for shape in shapes],
        scratch_shapes=[pltpu.VMEM(shape, BF) for shape in shapes if sent]
        + [
            pltpu.VMEM((3, 256, 512), BF),
            pltpu.VMEM((2, 128, 256), BF),
            pltpu.VMEM((24, 256, 256), BF),
            pltpu.VMEM((2, 12, 2, 128, 128), BF),
            pltpu.SemaphoreType.DMA((2,)),
            pltpu.SemaphoreType.DMA((2, 3)),
        ],
        cost_estimate=pl.CostEstimate(
            flops=1000000000, bytes_accessed=4000000, transcendentals=0
        ),
        compiler_params=params(20),
        name="make_tiles" if sent else "make_home",
    )(own_table, far_table, own_wave, far_wave, left_operators, far_left)


def picks_kernel(slot_key, real_key, imag_key, out):
    out[0:384] = (slot_key[...] == real_key[...]).astype(F32).astype(BF)
    sign = jnp.where(iota((384, 384), 1) % 48 < 24, -1.0, 1.0)
    out[384:768] = jnp.where(slot_key[...] == imag_key[...], sign, 0.0).astype(BF)


def make_picks(keys):
    return pl.pallas_call(
        picks_kernel,
        out_shape=jax.ShapeDtypeStruct((768, 384), BF),
        compiler_params=params(8),
        name="make_picks",
    )(*keys)


def contract_kernel(
    home, ahead1, back1, ahead2, right, right_table, picks, out, paired_ref
):
    arrays = (home, ahead1, back1, ahead2)
    zero = jnp.zeros((96, 128), BF)

    def lefts(a):
        if a >= 16:
            return [home[96 + g * CROSS + a - 16] for g in range(6)] + [zero[0:32]]
        tiles = [ref[g * 16 + a] for ref in arrays[0:3] for g in range(6)]
        if a >= SPLIT:
            return tiles + [zero]
        return tiles + [ahead2[g * SPLIT + a] for g in range(6)]

    def product(start, stop):
        total = 0.0
        for first in range(start, stop, 2):
            pair = range(first, min(first + 2, stop))
            total += lax.dot_general(
                jnp.concatenate([right[:, a].reshape(256, 128) for a in pair], axis=1),
                jnp.concatenate([jnp.concatenate(lefts(a), axis=0) for a in pair], axis=1),
                (((1,), (1,)), ((), ())),
                preferred_element_type=F32,
            )
        return total

    paired = product(0, 16)
    cross = product(16, 16 + CROSS)
    for third in range(3):
        lanes = slice(third * 128, third * 128 + 128)
        paired_ref[third] = paired[:, lanes] + cross if third == 0 else paired[:, lanes]

    slot_label = sum(ref[n].astype(F32) for ref, n in zip(arrays, TILES))
    slot_label = jnp.concatenate([slot_label[i : i + 1] for i in range(3)], axis=1)
    row = iota((128, 128), 0)
    j = row % 32 // 2 * 8 + row // 32 % 2 * 4 + row % 2 * 2 + row // 64
    labels = right_table[pl.ds(where()[3], 1), :].astype(F32)
    right_label = jnp.sum(jnp.where(iota((128, 128), 1) == j, labels, 0.0), axis=1, keepdims=True)
    match = right_label == slot_label

    def part(c):
        rows = [
            jnp.concatenate(
                [paired_ref[third, pl.ds(c * 4 + w * 2 + t, 32, 8), :] for third in range(3)],
                axis=1,
            )
            for t in range(2)
            for w in range(2)
        ]
        return jnp.where(match, jnp.concatenate(rows, axis=0), 0.0)

    rest = jnp.concatenate([part(0), part(1)], axis=1)
    pieces = []
    for _ in range(2):
        pieces.append(rest.astype(BF))
        rest = rest - pieces[-1].astype(F32)
    total = jnp.dot(jnp.concatenate(pieces, axis=0), picks[...], preferred_element_type=F32)
    total = total[0:128] + total[128:256]
    total = total.astype(out.dtype)
    out[...] = jnp.zeros(out.shape, out.dtype)
    for t in range(2):
        for row in range(8):
            out[row, :, t * 48 : t * 48 + 48] = total[
                t * 64 : t * 64 + 64, row * 48 : row * 48 + 48
            ]


def contract(tiles, right, right_table, picks):
    whole = pl.BlockSpec(memory_space=pltpu.VMEM)
    return pl.pallas_call(
        contract_kernel,
        in_specs=[whole] * 7,
        out_specs=whole,
        out_shape=jax.ShapeDtypeStruct((8, 64, 128), BF),
        scratch_shapes=[pltpu.VMEM((3, 256, 128), F32)],
        compiler_params=params(16),
        name="contract",
    )(*tiles, right, right_table, picks)


def ring(step):
    pairs = []
    for z in range(8):
        for core in range(2):
            place = lambda z: ((z % 4) * 2 + core) * 2 + z // 4
            pairs.append((place(z), place(step(z, core))))
    return pairs


def local(
    wave_blocks, left_operators, right_operators, left_table, right_table, assignment, kramers_map
):
    line = ("row", "wf")
    core, z_lo, _, _ = where()
    right, own_wave = pick(right_operators, wave_blocks)
    far_wave = lax.ppermute(
        own_wave, line, ring(lambda z, core: (z + 2) % 8 if z in (2, 3, 6, 7) else (z - 2) % 8)
    )
    swap = [(i, i ^ 1) for i in range(8)]
    given, given_table, _ = lax.optimization_barrier((left_operators, left_table, own_wave))
    far_left = lax.ppermute(given, "row", swap)
    far_table = lax.ppermute(given_table, "row", swap)
    right = lax.all_to_all(right, "col", 0, 0, tiled=True)
    ahead1, back1, ahead2 = make_tiles(
        True, left_table, far_table, own_wave, far_wave, left_operators, far_left
    )
    far_wave, assignment, kramers_map, ahead1 = lax.optimization_barrier(
        (far_wave, assignment, kramers_map, ahead1)
    )
    ahead = lambda steps: ring(lambda z, core: (z + steps * (1 - 2 * core)) % 8)
    arrived = [
        lax.ppermute(ahead1, line, ahead(1)),
        lax.ppermute(back1, line, ahead(-1)),
        lax.ppermute(ahead2, line, ahead(2)),
    ]
    (home,) = make_tiles(
        False, left_table, far_table, own_wave, far_wave, left_operators, far_left
    )
    tiles = [home] + arrived

    held = assignment.reshape(4, 2, 12)
    held = jnp.where(core == 0, held, held[:, ::-1])
    held = lax.dynamic_slice_in_dim(jnp.concatenate([held, held], axis=0), z_lo, 4, 0)
    turned = jnp.concatenate([held[0:1], held[3:4], held[1:3]], axis=0)
    straight = jnp.concatenate([held[0:2], held[3:4], held[2:3]], axis=0)
    held = jnp.where(core == 0, turned, straight).reshape(96, 1)
    slot_key = (held * 4 + jnp.arange(4, dtype=jnp.int32)[None, :]).reshape(384, 1)
    target = jnp.stack([jnp.arange(96, dtype=jnp.int32), kramers_map]).reshape(1, 2, 8, 12)
    target = target.transpose(2, 0, 1, 3)
    kind = jnp.arange(2, dtype=jnp.int32)[None, None, :, None]
    part = jnp.arange(2, dtype=jnp.int32)[None, :, None, None]
    real_key = (target * 4 + kind * 2 + part).reshape(1, 384)
    imag_key = (target * 4 + kind * 2 + 1 - part).reshape(1, 384)

    picks = make_picks([slot_key, real_key, imag_key])
    shares = contract(tiles, right, right_table.T, picks)
    shares = lax.all_to_all(
        shares.reshape(256, 2, 128), ("row", "wf", "col"), 0, 0, tiled=True
    )
    total = jnp.sum(shares.astype(F32), axis=0)[:, 0:96]
    return total.reshape(2, 2, 2, 2, 12).transpose(2, 3, 4, 0, 1).reshape(2, 2, 12, 4)


def solution(mesh):
    return jax.shard_map(
        local,
        mesh=mesh,
        in_specs=(
            P(None, None, "wf", None),
            P("row", "col", None, None, None),
            P(None, "col", None, "wf", None),
            P("row", None),
            P(),
            P(),
            P(),
        ),
        out_specs=P(None, None, "row", ("col", "wf")),
        check_vma=False,
    )
```

```python
import functools

import jax
import jax.numpy as jnp
from jax import lax
from jax.experimental import pallas as pl
from jax.experimental.pallas import tpu as pltpu
from jax.sharding import PartitionSpec as P

BF = jnp.bfloat16
F32 = jnp.float32


def iota(shape, axis):
    return lax.broadcasted_iota(jnp.int32, shape, axis)


def where():
    row, col, wf = lax.axis_index("row"), lax.axis_index("col"), lax.axis_index("wf")
    return row & 1, row >> 1, wf * 4 + (row >> 1), 2 * col + (row & 1)


def params(mebibytes):
    return pltpu.CompilerParams(vmem_limit_bytes=mebibytes * 1024 * 1024)


SPLIT = 8
CROSS = 16 - SPLIT
ROWS = (16 + CROSS, 16, 16, SPLIT)
TILES = tuple(6 * rows for rows in ROWS)


def pick_kernel(right_ref, wave_ref, out_ref, wave_out, rows_ref, sem, wave_sem):
    core, z_lo, _, q = where()
    waves = [
        pltpu.make_async_copy(wave_ref.at[:, (q + o) & 31], wave_out.at[:, o], wave_sem.at[o])
        for o in range(3)
    ]
    for copy in waves:
        copy.start()
    copies = []
    for part in range(4):
        for second in range(2):
            copy = pltpu.make_async_copy(
                right_ref.at[pl.ds(part * 4, 4), core, :, :, z_lo ^ (2 * second)],
                rows_ref.at[second, pl.ds(part * 4, 4)],
                sem.at[part, second],
            )
            copy.start()
            copies.append(copy)
    for part in range(4):
        for second in range(2):
            copies[part * 2 + second].wait()
        for target in range(part * 4, part * 4 + 4):
            for second in range(2):
                rows = jnp.concatenate(
                    [
                        rows_ref[second, target, 4 * w + 2 * h + t, c][None]
                        for h in range(2)
                        for c in range(2)
                        for w in range(2)
                        for t in range(2)
                    ],
                    axis=0,
                )
                rows = jnp.swapaxes(rows, 0, 1)
                if second:
                    out_ref[target, 16 : 16 + CROSS] = rows[SPLIT:16]
                else:
                    out_ref[target, 0:16] = rows
    for copy in waves:
        copy.wait()


def pick(right_operators, wave_blocks):
    whole = pl.BlockSpec(memory_space=pltpu.VMEM)
    return pl.pallas_call(
        pick_kernel,
        in_specs=[pl.BlockSpec(memory_space=pltpu.HBM)] * 2,
        out_specs=[whole] * 2,
        out_shape=[
            jax.ShapeDtypeStruct((16, 16 + CROSS, 16, 128), BF),
            jax.ShapeDtypeStruct((2, 3, 64, 128), BF),
        ],
        scratch_shapes=[
            pltpu.VMEM((2, 16, 8, 2, 16, 128), BF),
            pltpu.SemaphoreType.DMA((4, 2)),
            pltpu.SemaphoreType.DMA((3,)),
        ],
        compiler_params=params(54),
        name="pick",
    )(right_operators.reshape(16, 2, 8, 2, 4, 16, 128), wave_blocks)


def tiles_kernel(
    sent, own_table, far_table, own_wave, far_wave, own_left, far_left, *refs
):
    count = 3 if sent else 1
    results, outs = refs[:count], refs[count : 2 * count] if sent else refs[:count]
    sides, bras, kets, operators, sem, out_sem = refs[-6:]
    core, _, z, q = where()
    ahead = 1 - 2 * core
    low = z < 4
    copies = [
        pltpu.make_async_copy(own_left.at[:, core], operators.at[0], sem.at[0]),
        pltpu.make_async_copy(far_left.at[:, core], operators.at[1], sem.at[1]),
    ]
    for copy in copies:
        copy.start()

    def wave(c, o):
        mine, other = own_wave[c, o], far_wave[c, o]
        return jnp.concatenate(
            [jnp.where(low, mine, other), jnp.where(low, other, mine)], axis=0
        )

    for o in range(3):
        re, im = wave(0, o), wave(1, o)
        top = jnp.concatenate([re, im, re, im], axis=1)
        bottom = jnp.concatenate([-im, re, im, -re], axis=1)
        sides[o] = jnp.concatenate([top, bottom], axis=0)
        if o == 0:
            re_t, im_t = re.T, im.T
            bras[0] = jnp.concatenate([re_t, im_t], axis=1)
            bras[1] = jnp.concatenate([-im_t, re_t], axis=1)

    columns = [
        jnp.sum(jnp.where(iota((12, 32), 1) == q, table[...], 0), axis=1, keepdims=True)
        for table in (own_table, far_table)
    ]
    labels = [column[s, 0] for column in columns for s in range(12)]
    shifts = [lax.rem(label - q + 32, 32) for label in labels]
    for i, out in enumerate(outs):
        start = 96 * (i + 1 if sent else 0)
        place = (iota((16, 128), 0) * 128 + iota((16, 128), 1) - start) >> 2
        label = jnp.zeros((16, 128), F32)
        for s in range(24):
            label = jnp.where(place == s, labels[s].astype(F32), label)
        out[out.shape[0] - 1] = label.astype(BF)

    leaving = []
    for half in range(2):
        if sent:
            spots = [(z + ahead) & 7, (z - ahead) & 7, (z + 2 * ahead) & 7]
        else:
            spots = [z, z ^ 2]
        width = 16 * len(spots)
        left = jnp.concatenate(
            [
                bras[c, pl.ds(pl.multiple_of(spot * 16, 16), 16), :]
                for c in range(2)
                for spot in spots
            ],
            axis=0,
        )
        copies[half].wait()
        for s in range(12):
            operator = jnp.concatenate(
                [operators[half, s, 0], operators[half, s, 1]], axis=1
            )
            turned = jnp.dot(
                operator, sides[shifts[half * 12 + s]], preferred_element_type=F32
            ).astype(BF)
            kets[half * 12 + s] = jnp.concatenate(
                [
                    jnp.concatenate([turned[:, 0:128], turned[:, 256:384]], axis=1),
                    jnp.concatenate([turned[:, 128:256], turned[:, 384:512]], axis=1),
                ],
                axis=0,
            )
        for group in range(3):
            whole = half * 3 + group
            brackets = [
                jnp.dot(left, kets[whole * 4 + s], preferred_element_type=F32).astype(BF)
                for s in range(4)
            ]
            for i in range(len(spots)):
                rows = jnp.concatenate(
                    [
                        brackets[s][
                            c * width + i * 16 : c * width + i * 16 + 16,
                            kind * 128 : kind * 128 + 128,
                        ][None]
                        for s in range(4)
                        for kind in range(2)
                        for c in range(2)
                    ],
                    axis=0,
                )
                rows = jnp.swapaxes(rows, 0, 1)
                if sent and i == 2:
                    outs[2][whole * SPLIT : whole * SPLIT + SPLIT] = rows[0:SPLIT]
                elif i == 1 and not sent:
                    outs[0][96 + whole * CROSS : 96 + whole * CROSS + CROSS] = rows[SPLIT:16]
                else:
                    outs[i][whole * 16 : whole * 16 + 16] = rows
        if sent:
            for i, out in enumerate(outs):
                middle = TILES[i + 1] // 2
                size = middle + 1 if half else middle
                copy = pltpu.make_async_copy(
                    out.at[pl.ds(middle * half, size)],
                    results[i].at[pl.ds(middle * half, size)],
                    out_sem.at[half, i],
                )
                copy.start()
                leaving.append(copy)
    for copy in leaving:
        copy.wait()


def make_tiles(sent, own_table, far_table, own_wave, far_wave, left_operators, far_left):
    anywhere, whole = pl.BlockSpec(memory_space=pl.ANY), pl.BlockSpec(memory_space=pltpu.VMEM)
    shapes = [(n + 1, 16, 128) for n in (TILES[1:] if sent else TILES[:1])]
    return pl.pallas_call(
        functools.partial(tiles_kernel, sent),
        in_specs=[whole] * 4 + [anywhere] * 2,
        out_specs=[anywhere if sent else whole] * len(shapes),
        out_shape=[jax.ShapeDtypeStruct(shape, BF) for shape in shapes],
        scratch_shapes=[pltpu.VMEM(shape, BF) for shape in shapes if sent]
        + [
            pltpu.VMEM((3, 256, 512), BF),
            pltpu.VMEM((2, 128, 256), BF),
            pltpu.VMEM((24, 256, 256), BF),
            pltpu.VMEM((2, 12, 2, 128, 128), BF),
            pltpu.SemaphoreType.DMA((2,)),
            pltpu.SemaphoreType.DMA((2, 3)),
        ],
        cost_estimate=pl.CostEstimate(
            flops=1000000000, bytes_accessed=4000000, transcendentals=0
        ),
        compiler_params=params(20),
        name="make_tiles" if sent else "make_home",
    )(own_table, far_table, own_wave, far_wave, left_operators, far_left)


def picks_kernel(slot_key, real_key, imag_key, out):
    out[0:384] = (slot_key[...] == real_key[...]).astype(F32).astype(BF)
    sign = jnp.where(iota((384, 384), 1) % 48 < 24, -1.0, 1.0)
    out[384:768] = jnp.where(slot_key[...] == imag_key[...], sign, 0.0).astype(BF)


def make_picks(keys):
    return pl.pallas_call(
        picks_kernel,
        out_shape=jax.ShapeDtypeStruct((768, 384), BF),
        compiler_params=params(8),
        name="make_picks",
    )(*keys)


def contract_kernel(
    home, ahead1, back1, ahead2, right, right_table, picks, out, paired_ref
):
    arrays = (home, ahead1, back1, ahead2)
    zero = jnp.zeros((96, 128), BF)

    def lefts(a):
        if a >= 16:
            return [home[96 + g * CROSS + a - 16] for g in range(6)] + [zero[0:32]]
        tiles = [ref[g * 16 + a] for ref in arrays[0:3] for g in range(6)]
        if a >= SPLIT:
            return tiles + [zero]
        return tiles + [ahead2[g * SPLIT + a] for g in range(6)]

    def product(start, stop):
        total = 0.0
        for first in range(start, stop, 2):
            pair = range(first, min(first + 2, stop))
            total += lax.dot_general(
                jnp.concatenate([right[:, a].reshape(256, 128) for a in pair], axis=1),
                jnp.concatenate([jnp.concatenate(lefts(a), axis=0) for a in pair], axis=1),
                (((1,), (1,)), ((), ())),
                preferred_element_type=F32,
            )
        return total

    paired = product(0, 16)
    cross = product(16, 16 + CROSS)
    for third in range(3):
        lanes = slice(third * 128, third * 128 + 128)
        paired_ref[third] = paired[:, lanes] + cross if third == 0 else paired[:, lanes]

    slot_label = sum(ref[n].astype(F32) for ref, n in zip(arrays, TILES))
    slot_label = jnp.concatenate([slot_label[i : i + 1] for i in range(3)], axis=1)
    row = iota((128, 128), 0)
    j = row % 32 // 2 * 8 + row // 32 % 2 * 4 + row % 2 * 2 + row // 64
    labels = right_table[pl.ds(where()[3], 1), :].astype(F32)
    right_label = jnp.sum(jnp.where(iota((128, 128), 1) == j, labels, 0.0), axis=1, keepdims=True)
    match = right_label == slot_label

    def part(c):
        rows = [
            jnp.concatenate(
                [paired_ref[third, pl.ds(c * 4 + w * 2 + t, 32, 8), :] for third in range(3)],
                axis=1,
            )
            for t in range(2)
            for w in range(2)
        ]
        return jnp.where(match, jnp.concatenate(rows, axis=0), 0.0)

    rest = jnp.concatenate([part(0), part(1)], axis=1)
    pieces = []
    for _ in range(2):
        pieces.append(rest.astype(BF))
        rest = rest - pieces[-1].astype(F32)
    total = jnp.dot(jnp.concatenate(pieces, axis=0), picks[...], preferred_element_type=F32)
    total = total[0:128] + total[128:256]
    total = total.astype(out.dtype)
    out[...] = jnp.zeros(out.shape, out.dtype)
    for t in range(2):
        for row in range(8):
            out[row, :, t * 48 : t * 48 + 48] = total[
                t * 64 : t * 64 + 64, row * 48 : row * 48 + 48
            ]


def contract(tiles, right, right_table, picks):
    whole = pl.BlockSpec(memory_space=pltpu.VMEM)
    return pl.pallas_call(
        contract_kernel,
        in_specs=[whole] * 7,
        out_specs=whole,
        out_shape=jax.ShapeDtypeStruct((8, 64, 128), BF),
        scratch_shapes=[pltpu.VMEM((3, 256, 128), F32)],
        compiler_params=params(16),
        name="contract",
    )(*tiles, right, right_table, picks)


def ring(step):
    pairs = []
    for z in range(8):
        for core in range(2):
            place = lambda z: ((z % 4) * 2 + core) * 2 + z // 4
            pairs.append((place(z), place(step(z, core))))
    return pairs


def local(
    wave_blocks, left_operators, right_operators, left_table, right_table, assignment, kramers_map
):
    line = ("row", "wf")
    core, z_lo, _, _ = where()
    right, own_wave = pick(right_operators, wave_blocks)
    far_wave = lax.ppermute(
        own_wave, line, ring(lambda z, core: (z + 2) % 8 if z in (2, 3, 6, 7) else (z - 2) % 8)
    )
    swap = [(i, i ^ 1) for i in range(8)]
    far_left = lax.ppermute(left_operators, "row", swap)
    far_table = lax.ppermute(left_table, "row", swap)
    right = lax.all_to_all(right, "col", 0, 0, tiled=True)
    ahead1, back1, ahead2 = make_tiles(
        True, left_table, far_table, own_wave, far_wave, left_operators, far_left
    )
    far_wave, assignment, kramers_map, ahead1 = lax.optimization_barrier(
        (far_wave, assignment, kramers_map, ahead1)
    )
    ahead = lambda steps: ring(lambda z, core: (z + steps * (1 - 2 * core)) % 8)
    arrived = [
        lax.ppermute(ahead1, line, ahead(1)),
        lax.ppermute(back1, line, ahead(-1)),
        lax.ppermute(ahead2, line, ahead(2)),
    ]
    (home,) = make_tiles(
        False, left_table, far_table, own_wave, far_wave, left_operators, far_left
    )
    tiles = [home] + arrived

    held = assignment.reshape(4, 2, 12)
    held = jnp.where(core == 0, held, held[:, ::-1])
    held = lax.dynamic_slice_in_dim(jnp.concatenate([held, held], axis=0), z_lo, 4, 0)
    turned = jnp.concatenate([held[0:1], held[3:4], held[1:3]], axis=0)
    straight = jnp.concatenate([held[0:2], held[3:4], held[2:3]], axis=0)
    held = jnp.where(core == 0, turned, straight).reshape(96, 1)
    slot_key = (held * 4 + jnp.arange(4, dtype=jnp.int32)[None, :]).reshape(384, 1)
    target = jnp.stack([jnp.arange(96, dtype=jnp.int32), kramers_map]).reshape(1, 2, 8, 12)
    target = target.transpose(2, 0, 1, 3)
    kind = jnp.arange(2, dtype=jnp.int32)[None, None, :, None]
    part = jnp.arange(2, dtype=jnp.int32)[None, :, None, None]
    real_key = (target * 4 + kind * 2 + part).reshape(1, 384)
    imag_key = (target * 4 + kind * 2 + 1 - part).reshape(1, 384)

    picks = make_picks([slot_key, real_key, imag_key])
    shares = contract(tiles, right, right_table.T, picks)
    shares = lax.all_to_all(
        shares.reshape(256, 2, 128), ("row", "wf", "col"), 0, 0, tiled=True
    )
    total = jnp.sum(shares.astype(F32), axis=0)[:, 0:96]
    return total.reshape(2, 2, 2, 2, 12).transpose(2, 3, 4, 0, 1).reshape(2, 2, 12, 4)


def solution(mesh):
    return jax.shard_map(
        local,
        mesh=mesh,
        in_specs=(
            P(None, None, "wf", None),
            P("row", "col", None, None, None),
            P(None, "col", None, "wf", None),
            P("row", None),
            P(),
            P(),
            P(),
        ),
        out_specs=P(None, None, "row", ("col", "wf")),
        check_vma=False,
    )
```

```python
import functools

import jax
import jax.numpy as jnp
from jax import lax
from jax.experimental import pallas as pl
from jax.experimental.pallas import tpu as pltpu
from jax.sharding import PartitionSpec as P

BF = jnp.bfloat16
F32 = jnp.float32


def iota(shape, axis):
    return lax.broadcasted_iota(jnp.int32, shape, axis)


def where():
    row, col, wf = lax.axis_index("row"), lax.axis_index("col"), lax.axis_index("wf")
    return row & 1, row >> 1, wf * 4 + (row >> 1), 2 * col + (row & 1)


def params(mebibytes):
    return pltpu.CompilerParams(vmem_limit_bytes=mebibytes * 1024 * 1024)


SPLIT = 8
CROSS = 16 - SPLIT
ROWS = (16 + CROSS, 16, 16, SPLIT)
TILES = tuple(6 * rows for rows in ROWS)


def pick_kernel(right_ref, wave_ref, out_ref, wave_out, rows_ref, sem, wave_sem):
    core, z_lo, _, q = where()
    waves = [
        pltpu.make_async_copy(wave_ref.at[:, (q + o) & 31], wave_out.at[:, o], wave_sem.at[o])
        for o in range(3)
    ]
    for copy in waves:
        copy.start()
    copies = []
    for part in range(4):
        for second in range(2):
            copy = pltpu.make_async_copy(
                right_ref.at[pl.ds(part * 4, 4), core, :, :, z_lo ^ (2 * second)],
                rows_ref.at[second, pl.ds(part * 4, 4)],
                sem.at[part, second],
            )
            copy.start()
            copies.append(copy)
    for part in range(4):
        for second in range(2):
            copies[part * 2 + second].wait()
        for target in range(part * 4, part * 4 + 4):
            for second in range(2):
                rows = jnp.concatenate(
                    [
                        rows_ref[second, target, 4 * w + 2 * h + t, c][None]
                        for h in range(2)
                        for c in range(2)
                        for w in range(2)
                        for t in range(2)
                    ],
                    axis=0,
                )
                rows = jnp.swapaxes(rows, 0, 1)
                if second:
                    out_ref[target, 16 : 16 + CROSS] = rows[SPLIT:16]
                else:
                    out_ref[target, 0:16] = rows
    for copy in waves:
        copy.wait()


def pick(right_operators, wave_blocks):
    whole = pl.BlockSpec(memory_space=pltpu.VMEM)
    return pl.pallas_call(
        pick_kernel,
        in_specs=[pl.BlockSpec(memory_space=pltpu.HBM)] * 2,
        out_specs=[whole] * 2,
        out_shape=[
            jax.ShapeDtypeStruct((16, 16 + CROSS, 16, 128), BF),
            jax.ShapeDtypeStruct((2, 3, 64, 128), BF),
        ],
        scratch_shapes=[
            pltpu.VMEM((2, 16, 8, 2, 16, 128), BF),
            pltpu.SemaphoreType.DMA((4, 2)),
            pltpu.SemaphoreType.DMA((3,)),
        ],
        compiler_params=params(54),
        name="pick",
    )(right_operators.reshape(16, 2, 8, 2, 4, 16, 128), wave_blocks)


def tiles_kernel(
    sent, own_table, far_table, own_wave, far_wave, own_left, far_left, *refs
):
    count = 3 if sent else 1
    results, outs = refs[:count], refs[count : 2 * count] if sent else refs[:count]
    sides, bras, kets, operators, sem, out_sem = refs[-6:]
    core, _, z, q = where()
    ahead = 1 - 2 * core
    low = z < 4
    copies = [
        pltpu.make_async_copy(own_left.at[:, core], operators.at[0], sem.at[0]),
        pltpu.make_async_copy(far_left.at[:, core], operators.at[1], sem.at[1]),
    ]
    for copy in copies:
        copy.start()

    def wave(c, o):
        mine, other = own_wave[c, o], far_wave[c, o]
        return jnp.concatenate(
            [jnp.where(low, mine, other), jnp.where(low, other, mine)], axis=0
        )

    for o in range(3):
        re, im = wave(0, o), wave(1, o)
        top = jnp.concatenate([re, im, re, im], axis=1)
        bottom = jnp.concatenate([-im, re, im, -re], axis=1)
        sides[o] = jnp.concatenate([top, bottom], axis=0)
        if o == 0:
            re_t, im_t = re.T, im.T
            bras[0] = jnp.concatenate([re_t, im_t], axis=1)
            bras[1] = jnp.concatenate([-im_t, re_t], axis=1)

    columns = [
        jnp.sum(jnp.where(iota((12, 32), 1) == q, table[...], 0), axis=1, keepdims=True)
        for table in (own_table, far_table)
    ]
    labels = [column[s, 0] for column in columns for s in range(12)]
    shifts = [lax.rem(label - q + 32, 32) for label in labels]
    for i, out in enumerate(outs):
        start = 96 * (i + 1 if sent else 0)
        place = (iota((16, 128), 0) * 128 + iota((16, 128), 1) - start) >> 2
        label = jnp.zeros((16, 128), F32)
        for s in range(24):
            label = jnp.where(place == s, labels[s].astype(F32), label)
        out[out.shape[0] - 1] = label.astype(BF)

    leaving = []
    for half in range(2):
        if sent:
            spots = [(z + ahead) & 7, (z - ahead) & 7, (z + 2 * ahead) & 7]
        else:
            spots = [z, z ^ 2]
        width = 16 * len(spots)
        left = jnp.concatenate(
            [
                bras[c, pl.ds(pl.multiple_of(spot * 16, 16), 16), :]
                for c in range(2)
                for spot in spots
            ],
            axis=0,
        )
        copies[half].wait()
        for s in range(12):
            operator = jnp.concatenate(
                [operators[half, s, 0], operators[half, s, 1]], axis=1
            )
            turned = jnp.dot(
                operator, sides[shifts[half * 12 + s]], preferred_element_type=F32
            ).astype(BF)
            kets[half * 12 + s] = jnp.concatenate(
                [
                    jnp.concatenate([turned[:, 0:128], turned[:, 256:384]], axis=1),
                    jnp.concatenate([turned[:, 128:256], turned[:, 384:512]], axis=1),
                ],
                axis=0,
            )
        for group in range(3):
            whole = half * 3 + group
            brackets = [
                jnp.dot(left, kets[whole * 4 + s], preferred_element_type=F32).astype(BF)
                for s in range(4)
            ]
            for i in range(len(spots)):
                rows = jnp.concatenate(
                    [
                        brackets[s][
                            c * width + i * 16 : c * width + i * 16 + 16,
                            kind * 128 : kind * 128 + 128,
                        ][None]
                        for s in range(4)
                        for kind in range(2)
                        for c in range(2)
                    ],
                    axis=0,
                )
                rows = jnp.swapaxes(rows, 0, 1)
                if sent and i == 2:
                    outs[2][whole * SPLIT : whole * SPLIT + SPLIT] = rows[0:SPLIT]
                elif i == 1 and not sent:
                    outs[0][96 + whole * CROSS : 96 + whole * CROSS + CROSS] = rows[SPLIT:16]
                else:
                    outs[i][whole * 16 : whole * 16 + 16] = rows
        if sent:
            for i, out in enumerate(outs):
                middle = TILES[i + 1] // 2
                size = middle + 1 if half else middle
                copy = pltpu.make_async_copy(
                    out.at[pl.ds(middle * half, size)],
                    results[i].at[pl.ds(middle * half, size)],
                    out_sem.at[half, i],
                )
                copy.start()
                leaving.append(copy)
    for copy in leaving:
        copy.wait()


def make_tiles(sent, own_table, far_table, own_wave, far_wave, left_operators, far_left):
    anywhere, whole = pl.BlockSpec(memory_space=pl.ANY), pl.BlockSpec(memory_space=pltpu.VMEM)
    shapes = [(n + 1, 16, 128) for n in (TILES[1:] if sent else TILES[:1])]
    return pl.pallas_call(
        functools.partial(tiles_kernel, sent),
        in_specs=[whole] * 4 + [anywhere] * 2,
        out_specs=[anywhere if sent else whole] * len(shapes),
        out_shape=[jax.ShapeDtypeStruct(shape, BF) for shape in shapes],
        scratch_shapes=[pltpu.VMEM(shape, BF) for shape in shapes if sent]
        + [
            pltpu.VMEM((3, 256, 512), BF),
            pltpu.VMEM((2, 128, 256), BF),
            pltpu.VMEM((24, 256, 256), BF),
            pltpu.VMEM((2, 12, 2, 128, 128), BF),
            pltpu.SemaphoreType.DMA((2,)),
            pltpu.SemaphoreType.DMA((2, 3)),
        ],
        cost_estimate=pl.CostEstimate(
            flops=1000000000, bytes_accessed=4000000, transcendentals=0
        ),
        compiler_params=params(20),
        name="make_tiles" if sent else "make_home",
    )(own_table, far_table, own_wave, far_wave, left_operators, far_left)


def picks_kernel(slot_key, real_key, imag_key, sign, out):
    out[0:384] = (slot_key[...] == real_key[...]).astype(F32).astype(BF)
    out[384:768] = jnp.where(slot_key[...] == imag_key[...], sign[...], 0.0).astype(BF)


def make_picks(keys):
    return pl.pallas_call(
        picks_kernel,
        out_shape=jax.ShapeDtypeStruct((768, 384), BF),
        compiler_params=params(8),
        name="make_picks",
    )(*keys)


def contract_kernel(
    home, ahead1, back1, ahead2, right, right_table, picks, out, paired_ref
):
    arrays = (home, ahead1, back1, ahead2)
    zero = jnp.zeros((96, 128), BF)

    def lefts(a):
        if a >= 16:
            return [home[96 + g * CROSS + a - 16] for g in range(6)] + [zero[0:32]]
        tiles = [ref[g * 16 + a] for ref in arrays[0:3] for g in range(6)]
        if a >= SPLIT:
            return tiles + [zero]
        return tiles + [ahead2[g * SPLIT + a] for g in range(6)]

    def product(start, stop):
        total = 0.0
        for first in range(start, stop, 2):
            pair = range(first, min(first + 2, stop))
            total += lax.dot_general(
                jnp.concatenate([right[:, a].reshape(256, 128) for a in pair], axis=1),
                jnp.concatenate([jnp.concatenate(lefts(a), axis=0) for a in pair], axis=1),
                (((1,), (1,)), ((), ())),
                preferred_element_type=F32,
            )
        return total

    paired = product(0, 16)
    cross = product(16, 16 + CROSS)
    for third in range(3):
        lanes = slice(third * 128, third * 128 + 128)
        paired_ref[third] = paired[:, lanes] + cross if third == 0 else paired[:, lanes]

    slot_label = sum(ref[n].astype(F32) for ref, n in zip(arrays, TILES))
    slot_label = jnp.concatenate([slot_label[i : i + 1] for i in range(3)], axis=1)
    row = iota((128, 128), 0)
    j = row % 32 // 2 * 8 + row // 32 % 2 * 4 + row % 2 * 2 + row // 64
    labels = right_table[pl.ds(where()[3], 1), :].astype(F32)
    right_label = jnp.sum(jnp.where(iota((128, 128), 1) == j, labels, 0.0), axis=1, keepdims=True)
    match = right_label == slot_label

    def part(c):
        rows = [
            jnp.concatenate(
                [paired_ref[third, pl.ds(c * 4 + w * 2 + t, 32, 8), :] for third in range(3)],
                axis=1,
            )
            for t in range(2)
            for w in range(2)
        ]
        return jnp.where(match, jnp.concatenate(rows, axis=0), 0.0)

    rest = jnp.concatenate([part(0), part(1)], axis=1)
    pieces = []
    for _ in range(2):
        pieces.append(rest.astype(BF))
        rest = rest - pieces[-1].astype(F32)
    total = jnp.dot(jnp.concatenate(pieces, axis=0), picks[...], preferred_element_type=F32)
    total = total[0:128] + total[128:256]
    total = total.astype(out.dtype)
    out[...] = jnp.zeros(out.shape, out.dtype)
    for t in range(2):
        for row in range(8):
            out[row, :, t * 48 : t * 48 + 48] = total[
                t * 64 : t * 64 + 64, row * 48 : row * 48 + 48
            ]


def contract(tiles, right, right_table, picks):
    whole = pl.BlockSpec(memory_space=pltpu.VMEM)
    return pl.pallas_call(
        contract_kernel,
        in_specs=[whole] * 7,
        out_specs=whole,
        out_shape=jax.ShapeDtypeStruct((8, 64, 128), BF),
        scratch_shapes=[pltpu.VMEM((3, 256, 128), F32)],
        compiler_params=params(16),
        name="contract",
    )(*tiles, right, right_table, picks)


def ring(step):
    pairs = []
    for z in range(8):
        for core in range(2):
            place = lambda z: ((z % 4) * 2 + core) * 2 + z // 4
            pairs.append((place(z), place(step(z, core))))
    return pairs


def local(
    wave_blocks, left_operators, right_operators, left_table, right_table, assignment, kramers_map
):
    line = ("row", "wf")
    core, z_lo, _, _ = where()
    right, own_wave = pick(right_operators, wave_blocks)
    far_wave = lax.ppermute(
        own_wave, line, ring(lambda z, core: (z + 2) % 8 if z in (2, 3, 6, 7) else (z - 2) % 8)
    )
    swap = [(i, i ^ 1) for i in range(8)]
    far_left = lax.ppermute(left_operators, "row", swap)
    far_table = lax.ppermute(left_table, "row", swap)
    right = lax.all_to_all(right, "col", 0, 0, tiled=True)
    ahead1, back1, ahead2 = make_tiles(
        True, left_table, far_table, own_wave, far_wave, left_operators, far_left
    )
    far_wave, assignment, kramers_map, ahead1 = lax.optimization_barrier(
        (far_wave, assignment, kramers_map, ahead1)
    )
    ahead = lambda steps: ring(lambda z, core: (z + steps * (1 - 2 * core)) % 8)
    arrived = [
        lax.ppermute(ahead1, line, ahead(1)),
        lax.ppermute(back1, line, ahead(-1)),
        lax.ppermute(ahead2, line, ahead(2)),
    ]
    (home,) = make_tiles(
        False, left_table, far_table, own_wave, far_wave, left_operators, far_left
    )
    tiles = [home] + arrived

    held = assignment.reshape(4, 2, 12)
    held = jnp.where(core == 0, held, held[:, ::-1])
    held = lax.dynamic_slice_in_dim(jnp.concatenate([held, held], axis=0), z_lo, 4, 0)
    turned = jnp.concatenate([held[0:1], held[3:4], held[1:3]], axis=0)
    straight = jnp.concatenate([held[0:2], held[3:4], held[2:3]], axis=0)
    held = jnp.where(core == 0, turned, straight).reshape(96, 1)
    slot_key = (held * 4 + jnp.arange(4, dtype=jnp.int32)[None, :]).reshape(384, 1)
    target = jnp.stack([jnp.arange(96, dtype=jnp.int32), kramers_map]).reshape(1, 2, 8, 12)
    target = target.transpose(2, 0, 1, 3)
    kind = jnp.arange(2, dtype=jnp.int32)[None, None, :, None]
    part = jnp.arange(2, dtype=jnp.int32)[None, :, None, None]
    real_key = (target * 4 + kind * 2 + part).reshape(1, 384)
    imag_key = (target * 4 + kind * 2 + 1 - part).reshape(1, 384)
    sign = jnp.broadcast_to((2 * part - 1).astype(F32), (8, 2, 2, 12)).reshape(1, 384)

    picks = make_picks([slot_key, real_key, imag_key, sign])
    shares = contract(tiles, right, right_table.T, picks)
    shares = lax.all_to_all(
        shares.reshape(256, 2, 128), ("row", "wf", "col"), 0, 0, tiled=True
    )
    total = jnp.sum(shares.astype(F32), axis=0)[:, 0:96]
    return total.reshape(2, 2, 2, 2, 12).transpose(2, 3, 4, 0, 1).reshape(2, 2, 12, 4)


def solution(mesh):
    return jax.shard_map(
        local,
        mesh=mesh,
        in_specs=(
            P(None, None, "wf", None),
            P("row", "col", None, None, None),
            P(None, "col", None, "wf", None),
            P("row", None),
            P(),
            P(),
            P(),
        ),
        out_specs=P(None, None, "row", ("col", "wf")),
        check_vma=False,
    )
```
